128 devices in a mesh: expert: 32 (over z, x, core), wshard: 4 (over y).
Axes of the slice: x: 4, y: 4, z: 4, core: 2. Of those that a mesh axis runs over, the one named last changes fastest.
Arguments:
- tokens: bfloat16 [25216, 768], P(('expert', 'wshard')), may hold values from -6 to 6
- ln1_gain: bfloat16 [768], P('wshard'), may hold values from 0.5 to 1.5
- ln1_bias: bfloat16 [768], P('wshard'), may hold values from -2 to 2
- w_qkv: bfloat16 [768, 2304], P('wshard'), may hold values from -0.21875 to 0.21875
- w_proj: bfloat16 [768, 768], P('wshard'), may hold values from -0.875 to 0.875
- ln2_gain: bfloat16 [768], P('wshard'), may hold values from 0.5 to 1.5
- ln2_bias: bfloat16 [768], P('wshard'), may hold values from -2 to 2
- w_router: bfloat16 [768, 32], P('wshard'), may hold values from -0.15625 to 0.15625
- expert_in: bfloat16 [32, 768, 3072], P('expert'), may hold values from -0.21875 to 0.21875
- expert_out: bfloat16 [32, 3072, 768], P('expert'), may hold values from -1.75 to 1.75
- routes: int32 [25216, 2], P(('expert', 'wshard')), may hold values from 0 to 31, all different within a row; in each aligned block of 197 rows (0 to 196, 197 to 393, ...) at most 16 rows name the same one
- cotangent: bfloat16 [25216, 768], P(('expert', 'wshard')), may hold values from -6 to 6
Outputs:
- mixed: bfloat16 [25216, 768], P(('expert', 'wshard'))
- grad_tokens: float32 [25216, 768], P(('expert', 'wshard'))
- grad_ln1_gain: float32 [768], P('wshard')
- grad_ln1_bias: float32 [768], P('wshard')
- grad_w_qkv: float32 [768, 2304], P('wshard')
- grad_w_proj: float32 [768, 768], P('wshard')
- grad_ln2_gain: float32 [768], P('wshard')
- grad_ln2_bias: float32 [768], P('wshard')
- grad_w_router: float32 [768, 32], P('wshard')
- grad_expert_in: float32 [32, 768, 3072], P('expert', 'wshard')
- grad_expert_out: float32 [32, 3072, 768], P('expert', 'wshard')
The draws below stay inside these ranges and needn't reach their ends.
Inputs may be any that keep to these rules, and one draw needn't show every extreme that they name: `routes`: each token names two different experts; among the 197 tokens of one device no expert is named more than 16 times, a bound that some block reaches.
All inputs are finite; a program needn't handle non-finite values.
Results may differ from the reference program's by a relative error of at most 0.025.
Values may be sent and summed in bfloat16 or wider, within the bound.
A program may use at most 128 MiB of HBM per device.

```python
import math
import jax
import jax.numpy as jnp
import numpy as np
from jax import lax

D = 768
HEADS = 12
HEAD_DIM = 64
FF = 3072
LENGTH = 197
TOK_DEV = 197
EXPERTS = 32
IMAGES = 128
TOKENS = 25216
CAP = 16


def steps_of(own_key, shape, cuts, least, largest):
    def one(dim, blocks):
        heights = jax.random.uniform(jax.random.fold_in(jax.random.fold_in(own_key, 6), dim), (blocks,), jnp.float32, least / len(cuts), largest / len(cuts))
        return jnp.repeat(jnp.exp(heights), shape[dim] // blocks).reshape((-1,) + (1,) * (len(shape) - dim - 1))

    factor_of = one(*cuts[0])
    for cut in cuts[1:]:
        factor_of = factor_of * one(*cut)
    return factor_of


def routed_block(own_key, own, number, rows, amount, top, reach, skew):
    sequence = jax.random.permutation(own_key, amount)
    crowded, ordinary = portions_of(amount, rows * top, reach, skew, True), portions_of(amount, rows * top, reach, skew, False)
    places = jnp.arange(amount)

    def named(sizes, rotation):
        used = int((sizes > 0).sum())
        fixed = max(1, used // 4)
        shifted = fixed + (places - fixed + rotation * (used - fixed)) % max(1, amount - fixed)
        return jnp.zeros((amount,), jnp.int32).at[sequence[jnp.where(places < fixed, places, shifted)]].set(jnp.asarray(sizes, jnp.int32))

    sizes = jnp.where(number % 4 == 0, named(crowded, number // 4), named(ordinary, number - number // 4 - 1))
    mixed = jax.random.permutation(jax.random.fold_in(own, 3), amount)
    source_of, receiver = mixed[0:amount // 2 * 2:2], mixed[1:amount // 2 * 2:2]
    room = jnp.minimum(sizes[source_of] - 1, reach - sizes[receiver]) // 2
    room = jnp.where((source_of == sequence[0]) | (receiver == sequence[0]) | (sizes[receiver] == 0), 0, jnp.maximum(room, 0))
    shifted = jax.random.randint(jax.random.fold_in(own, 4), (amount // 2,), 0, 1 << 20) % (room + 1)
    sizes = sizes.at[source_of].add(-shifted).at[receiver].add(shifted)
    members = jnp.searchsorted(jnp.cumsum(sizes), jnp.arange(rows * top), side="right").astype(jnp.int32)
    table = members.reshape(top, rows).T
    table = table[jax.random.permutation(jax.random.fold_in(own, 1), rows)]
    rotation = jax.random.randint(jax.random.fold_in(own, 2), (rows, 1), 0, top)
    return jnp.take_along_axis(table, (jnp.arange(top)[None, :] + rotation) % top, axis=1)


def portions_of(number_of, total, most, lean, full):
    portions = [(1 << 20) // math.isqrt(rank ** lean) + 1 for rank in range(1, number_of + 1)]
    largest = most if full else min(most, max(-(-total // number_of), total * portions[0] // sum(portions)))
    least = 1 if total - largest >= number_of - 1 else 0
    holding, surplus = [largest] + [least] * (number_of - 1), total - largest - least * (number_of - 1)
    while surplus > 0:
        candidates = [i for i in range(1, number_of) if holding[i] < largest] or [i for i in range(1, number_of) if holding[i] < most]
        pool, remaining = sum([portions[i] for i in candidates]), surplus
        for i in candidates:
            more = min(most - holding[i], max(1, remaining * portions[i] // pool), surplus)
            holding[i] = holding[i] + more
            surplus = surplus - more
    return np.array(holding)


def normal_values(key, extent, scale, reach, shards=(), kind=jnp.bfloat16):
    drawn = scale * jax.random.normal(key, extent, jnp.float32)
    if shards:
        drawn = drawn * steps_of(key, extent, shards, -0.22, 0.18)
    return jnp.clip(drawn, -reach, reach).astype(kind)


def setup_inputs(seed: int = 0) -> dict:
    arg_keys = jax.random.split(jax.random.key(seed), 13)
    tokens = normal_values(arg_keys[0], (TOKENS, D), 1.0, 6.0, ((0, 128),))
    ln1_gain = jnp.clip(1.0 + 0.1 * jax.random.normal(arg_keys[1], (D,), jnp.float32), 0.5, 1.5).astype(jnp.bfloat16)
    ln1_bias = normal_values(arg_keys[2], (D,), 0.3, 2.0, ((0, 4),))
    w_qkv = normal_values(arg_keys[3], (D, 3 * D), D ** -0.5, 0.21875, ((0, 4),))
    w_proj = normal_values(arg_keys[4], (D, D), (D // 16) ** -0.5, 0.875, ((0, 4),))
    ln2_gain = jnp.clip(1.0 + 0.1 * jax.random.normal(arg_keys[5], (D,), jnp.float32), 0.5, 1.5).astype(jnp.bfloat16)
    ln2_bias = normal_values(arg_keys[6], (D,), 0.3, 2.0, ((0, 4),))
    w_router = normal_values(arg_keys[7], (D, EXPERTS), (2 * D) ** -0.5, 0.15625, ((0, 4),))
    expert_in = normal_values(arg_keys[8], (EXPERTS, D, FF), D ** -0.5, 0.21875, ((0, 32),))
    expert_out = normal_values(arg_keys[9], (EXPERTS, FF, D), (max(FF // 256, 1)) ** -0.5, 1.75, ((0, 32),))
    routes_keys = jax.random.split(jax.random.fold_in(arg_keys[10], 1), TOKENS // TOK_DEV)
    routes_turns = jax.random.permutation(jax.random.fold_in(arg_keys[10], 3), TOKENS // TOK_DEV)
    routes = jax.vmap(lambda own, number: routed_block(jax.random.fold_in(arg_keys[10], 2), own, number, TOK_DEV, EXPERTS, 2, CAP, 2))(routes_keys, routes_turns).reshape((TOKENS, 2))
    cotangent = normal_values(arg_keys[11], (TOKENS, D), 1.0, 6.0, ((0, 128),))
    return {"tokens": tokens, "ln1_gain": ln1_gain, "ln1_bias": ln1_bias, "w_qkv": w_qkv, "w_proj": w_proj, "ln2_gain": ln2_gain, "ln2_bias": ln2_bias, "w_router": w_router, "expert_in": expert_in, "expert_out": expert_out, "routes": routes, "cotangent": cotangent}


@jax.custom_vjp
def low(v):
    return lax.optimization_barrier(v.astype(jnp.bfloat16)).astype(jnp.float32)

@jax.custom_vjp
def low_back(v):
    return v

def low_keep(v):
    return (low(v), None)

def low_pass(kept, grad):
    return (grad,)

def back_keep(v):
    return (v, None)

def back_low(kept, grad):
    return (low(grad),)
low.defvjp(low_keep, low_pass)
low_back.defvjp(back_keep, back_low)
epsilon = 1e-06

def normalize(values, gain_vec, shift_vec):
    centered = values - lax.optimization_barrier(jnp.mean(values, -1, keepdims=True))
    inverse = lax.rsqrt(lax.optimization_barrier(jnp.mean(centered * centered, -1, keepdims=True)) + epsilon)
    return centered * inverse * gain_vec + shift_vec

def matmul(left, right):
    return jnp.dot(left, right, precision=lax.Precision.HIGHEST)

def attend(packed):
    group = packed.shape[0]
    query_heads = packed[..., :D].reshape(group, LENGTH, HEADS, HEAD_DIM)
    key_heads = packed[..., D:2 * D].reshape(group, LENGTH, HEADS, HEAD_DIM)
    value_heads = packed[..., 2 * D:].reshape(group, LENGTH, HEADS, HEAD_DIM)
    scores = low_back(jnp.einsum('gqhc,gkhc->ghqk', query_heads, key_heads, precision=lax.Precision.HIGHEST) * HEAD_DIM ** (-0.5))
    probs = jax.nn.softmax(scores, axis=-1)
    attended = jnp.einsum('ghqk,gkhc->gqhc', low(probs), value_heads, precision=lax.Precision.HIGHEST)
    return low(low_back(attended)).reshape(group, LENGTH, D)

def expert_apply(operands):
    rows_in, first_layer, second_layer = operands
    hidden = low_back(matmul(rows_in, first_layer))
    active = low(jax.nn.gelu(hidden, approximate=False))
    return low(low_back(matmul(active, second_layer)))

def reference(tokens, ln1_gain, ln1_bias, w_qkv, w_proj, ln2_gain, ln2_bias, w_router, expert_in, expert_out, routes, cotangent):
    devices = TOKENS // TOK_DEV
    route_flat = routes.reshape(-1).astype(jnp.int32)
    owner_dev = jnp.arange(2 * TOKENS, dtype=jnp.int32) // (2 * TOK_DEV)
    hit_table = (routes.reshape(devices, 2 * TOK_DEV)[:, :, None] == jnp.arange(EXPERTS, dtype=jnp.int32)).astype(jnp.int32)
    slot_index = lax.optimization_barrier(jnp.sum((jnp.cumsum(hit_table, axis=1) - hit_table) * hit_table, axis=-1)).reshape(-1).astype(jnp.int32)

    def forward(inputs, gain_one, shift_one, weight_qkv, weight_proj, gain_two, shift_two, weight_router, first_layer, second_layer):
        first_in = low(normalize(inputs, gain_one, shift_one))
        packed = low(low_back(matmul(first_in, weight_qkv)))
        groups = packed.reshape(IMAGES // 16, 16, LENGTH, 3 * D)
        attended = lax.map(jax.checkpoint(attend), groups).reshape(TOKENS, D)
        residual = inputs + low_back(matmul(attended, weight_proj))
        second_in = low(normalize(residual, gain_two, shift_two))
        gate_probs = jax.nn.softmax(low_back(matmul(second_in, weight_router)), axis=-1)
        chosen = jnp.take_along_axis(gate_probs, routes, axis=1)
        buffer_rows = jnp.zeros((devices, CAP, EXPERTS, D), jnp.float32)
        buffer_rows = buffer_rows.at[owner_dev, slot_index, route_flat].add(jnp.repeat(second_in, 2, axis=0))
        buffer_rows = low_back(buffer_rows)
        per_expert = jnp.transpose(buffer_rows, (2, 0, 1, 3)).reshape(EXPERTS, devices * CAP, D)
        results = lax.map(jax.checkpoint(expert_apply), (per_expert, first_layer, second_layer))
        results = results.reshape(EXPERTS, devices, CAP, D)
        picked = results[route_flat, owner_dev, slot_index].reshape(TOKENS, 2, D)
        return residual + lax.optimization_barrier(jnp.sum(chosen[..., None] * picked, axis=1))
    primals = tuple((member.astype(jnp.float32) for member in (tokens, ln1_gain, ln1_bias, w_qkv, w_proj, ln2_gain, ln2_bias, w_router, expert_in, expert_out)))
    output, pullback = jax.vjp(forward, *primals)
    grads = pullback(cotangent.astype(jnp.float32))
    return (output.astype(jnp.bfloat16), grads[0], grads[1], grads[2], grads[3], grads[4], grads[5], grads[6], grads[7], grads[8], grads[9])
```

```python
import functools

import jax
import jax.numpy as jnp
from jax import lax
from jax.experimental import pallas as pl
from jax.experimental.pallas import tpu as pltpu
from jax.sharding import PartitionSpec as P

HEAD_DIM = 64
EPSILON = 1e-06
F32 = jnp.float32
BF16 = jnp.bfloat16
LANES = 128
MIB = 1 << 20


def mm(left, right, left_dim=1, right_dim=0):
    return lax.dot_general(
        left, right, (((left_dim,), (right_dim,)), ((), ())), preferred_element_type=F32
    )


def normalize(values):
    centered = values - jnp.mean(values, -1, keepdims=True)
    inverse = lax.rsqrt(jnp.mean(centered * centered, -1, keepdims=True) + EPSILON)
    return centered * inverse, inverse


def norm_back(upstream, normed, inverse, gain):
    scaled = upstream * gain
    return inverse * (
        scaled
        - jnp.mean(scaled, -1, keepdims=True)
        - normed * jnp.mean(scaled * normed, -1, keepdims=True)
    )


def lane_iota(rows, columns=LANES):
    return lax.broadcasted_iota(jnp.int32, (rows, columns), 1)


MESH = pl.DeviceIdType.MESH
SIDE = 4


def remote(source, target, send, receive, expert, shard):
    return pltpu.make_async_remote_copy(
        src_ref=source, dst_ref=target, send_sem=send, recv_sem=receive,
        device_id=(expert, shard), device_id_type=MESH,
    )


def greet(devices):
    barrier = pltpu.get_barrier_semaphore()
    for expert, shard in devices:
        pl.semaphore_signal(barrier, inc=1, device_id=(expert, shard), device_id_type=MESH)
    pl.semaphore_wait(barrier, len(devices))


class RowGather:
    def __init__(self, shard_ref, full_ref, split, send, receive, expert, shard):
        self.rows, columns = shard_ref.shape
        self.shard_ref, self.full_ref = shard_ref, full_ref
        self.send, self.receive = send, receive
        self.expert, self.shard = expert, shard
        core = lax.rem(expert, 2)
        self.split = split
        self.sibling = expert + 1 - 2 * core
        self.after, self.before = lax.rem(shard + 1, SIDE), lax.rem(shard + 3, SIDE)
        self.across = lax.rem(shard + 2, SIDE)
        if split:
            half = columns // 2
            self.columns = pl.ds(pl.multiple_of(core * half, LANES), half)
            self.others = pl.ds(pl.multiple_of((1 - core) * half, LANES), half)
        else:
            self.columns = self.others = pl.ds(0, columns)

    def at(self, shard, start, count, columns):
        place = pl.multiple_of(shard * self.rows + start, 16)
        return self.full_ref.at[pl.ds(place, count), columns]

    def ring(self, number, source, target, shard):
        return remote(
            source, target, self.send.at[number], self.receive.at[number], self.expert, shard
        )

    def first(self):
        target = self.at(self.shard, 0, self.rows, self.columns)
        source = self.shard_ref.at[:, self.columns]
        self.to_after = self.ring(0, source, target, self.after)
        self.to_before = self.ring(1, source, target, self.before)
        self.own = pltpu.make_async_copy(
            self.shard_ref, self.at(self.shard, 0, self.rows, pl.ds(0, self.shard_ref.shape[1])),
            self.send.at[8],
        )
        self.to_after.start()
        self.to_before.start()
        self.own.start()

    def hand(self, number, shard, start, count):
        if not self.split:
            return None
        block = self.at(shard, start, count, self.columns)
        copy = remote(
            block, block, self.send.at[number], self.receive.at[number], self.sibling, self.shard
        )
        copy.start()
        return copy

    def second(self):
        half = self.rows // 2
        self.to_after.wait_recv()
        top = self.at(self.before, 0, half, self.columns)
        self.pass_after = self.ring(2, top, top, self.after)
        self.pass_after.start()
        self.to_before.wait_recv()
        bottom = self.at(self.after, half, half, self.columns)
        self.pass_before = self.ring(3, bottom, bottom, self.before)
        self.pass_before.start()
        self.handed = [
            self.hand(4, self.before, 0, self.rows),
            self.hand(5, self.after, 0, self.rows),
        ]

    def third(self):
        half = self.rows // 2
        self.pass_after.wait_recv()
        self.handed.append(self.hand(6, self.across, 0, half))
        self.pass_before.wait_recv()
        self.handed.append(self.hand(7, self.across, half, half))

    def finish(self):
        self.own.wait()
        for copy in self.handed:
            if copy is not None:
                copy.wait_recv()

    def drain(self):
        for copy in (self.to_after, self.to_before, self.pass_after, self.pass_before, *self.handed):
            if copy is not None:
                copy.wait_send()


def exchange_peers(expert):
    return [
        lax.rem(expert // 8 + dz, SIDE) * 8 + lax.rem(lax.rem(expert // 2, SIDE) + dx, SIDE) * 2
        + lax.rem(expert + dc, 2)
        for dz, dx, dc in exchange_order()
    ]


def exchange_order():
    reach = [0, 1, 2, 1]
    steps = [(dz, dx, dc) for dz in range(SIDE) for dx in range(SIDE) for dc in range(2)]
    return sorted(steps[1:], key=lambda step: -reach[step[0]] - reach[step[1]])


def exchange_start(source_ref, target_ref, send, receive, local, expert, shard, capacity):
    own = pl.ds(pl.multiple_of(expert * capacity, 16), capacity)
    copies = []
    for number, peer in enumerate(exchange_peers(expert)):
        block = pl.ds(pl.multiple_of(peer * capacity, 16), capacity)
        copy = remote(
            source_ref.at[block, :], target_ref.at[own, :], send.at[number], receive.at[number], peer, shard
        )
        copy.start()
        copies.append(copy)
    keep = pltpu.make_async_copy(source_ref.at[own, :], target_ref.at[own, :], local)
    keep.start()
    return copies, keep


def exchange_wait(copies, keep):
    keep.wait()
    for copy in copies:
        copy.wait()


def exchange_kernel(capacity, source_ref, target_ref, send, receive, local):
    expert, shard = lax.axis_index("expert"), lax.axis_index("wshard")
    greet([(peer, shard) for peer in exchange_peers(expert)])
    exchange_wait(*exchange_start(source_ref, target_ref, send, receive, local, expert, shard, capacity))


def exchange(rows, capacity, collective_id):
    return pl.pallas_call(
        functools.partial(exchange_kernel, capacity),
        out_shape=jax.ShapeDtypeStruct(rows.shape, rows.dtype),
        in_specs=[pl.BlockSpec(memory_space=pl.ANY)],
        out_specs=pl.BlockSpec(memory_space=pl.ANY),
        scratch_shapes=[
            pltpu.SemaphoreType.DMA((31,)), pltpu.SemaphoreType.DMA((31,)), pltpu.SemaphoreType.DMA,
        ],
        compiler_params=pltpu.CompilerParams(collective_id=collective_id, has_side_effects=True),
        cost_estimate=pl.CostEstimate(flops=0, bytes_accessed=4 * MIB, transcendentals=0),
        name="exchange_rows",
    )(rows)


def reduce_kernel(
    g_ref, s_ref, wide_ref, small_ref,
    paired, summed, side, first_in, second, second_in, third_in, piece, line, plane, gathered,
    s_pair, s_sum, s_in, s_out, s_other, send, receive, s_send, s_receive,
):
    expert, shard = lax.axis_index("expert"), lax.axis_index("wshard")
    core = lax.rem(expert, 2)
    x, z = lax.rem(expert // 2, SIDE), expert // 8
    sibling = expert + 1 - 2 * core
    first, second_at = x * (1 - core) + z * core, z * (1 - core) + x * core
    first_step, second_step = 2 + 6 * core, 8 - 6 * core

    def turn(place, by):
        return lax.rem(place + by, SIDE)

    def on_first(by):
        return expert + (turn(first, by) - first) * first_step

    def on_second(by):
        return expert + (turn(second_at, by) - second_at) * second_step

    greet(
        [(sibling, shard)]
        + [(on_first(by), shard) for by in (1, 2, 3)]
        + [(on_second(by), shard) for by in (1, 2, 3)]
        + [(expert, turn(shard, by)) for by in (1, 2, 3)]
    )
    rows = s_ref.shape[1]
    part = rows // 2
    quarter = rows // 4
    count = [0]
    small_count = [0]
    started = []

    def go(source, target, to_expert, to_shard, small=False):
        number = small_count if small else count
        sends, receives = (s_send, s_receive) if small else (send, receive)
        copy = remote(
            source, target, sends.at[number[0]], receives.at[number[0]], to_expert, to_shard
        )
        number[0] += 1
        copy.start()
        started.append(copy)
        return copy

    order = (2, 1, 3, 0)
    theirs = second_at
    pair = [
        go(g_ref.at[(1 - core) * SIDE + turn(theirs, by)], paired.at[number], sibling, shard)
        for number, by in enumerate(order)
    ]
    small_pair = go(s_ref, s_pair, sibling, shard, True)

    def add_pair(number):
        pair[number].wait_recv()
        own = g_ref[core * SIDE + turn(first, order[number])]
        summed[number] = (own.astype(F32) + paired[number].astype(F32)).astype(BF16)

    half = 2 * rows
    add_pair(0)
    relay_up = go(summed.at[0, pl.ds(0, half)], side.at[0], on_first(1), shard)
    relay_down = go(summed.at[0, pl.ds(half, half)], side.at[1], on_first(3), shard)
    add_pair(1)
    add_pair(2)
    small_pair.wait_recv()
    s_sum[...] = (s_ref[...].astype(F32) + s_pair[...].astype(F32)).astype(BF16)
    mine = pl.ds(pl.multiple_of(core * part, 16), part)
    others = pl.ds(pl.multiple_of((1 - core) * part, 16), part)
    small_along = [
        go(s_sum.at[turn(shard, by), mine, :], s_in.at[by - 1], expert, turn(shard, by), True)
        for by in (1, 2, 3)
    ]
    relay_up.wait_recv()
    summed[1, :half] = (summed[1, :half].astype(F32) + side[0].astype(F32)).astype(BF16)
    up = go(summed.at[1], first_in.at[0], on_first(1), shard)
    relay_down.wait_recv()
    summed[2, half:] = (summed[2, half:].astype(F32) + side[1].astype(F32)).astype(BF16)
    down = go(summed.at[2], first_in.at[1], on_first(3), shard)
    add_pair(3)

    for copy in small_along:
        copy.wait_recv()
    s_out[0] = (
        s_sum[shard, mine, :].astype(F32) + s_in[0].astype(F32) + s_in[1].astype(F32) + s_in[2].astype(F32)
    ).astype(BF16)
    small_first = [
        go(s_out.at[0], s_in.at[2 + by], on_first(by), shard, True) for by in (1, 2, 3)
    ]

    up.wait_recv()
    down.wait_recv()
    for own_shard in range(SIDE):
        for place in range(SIDE):
            at = pl.ds(own_shard * rows + place * quarter, quarter)
            second[place, own_shard] = (
                summed[3, at, :].astype(F32) + first_in[0, at, :].astype(F32) + first_in[1, at, :].astype(F32)
            ).astype(BF16)
    along_second = [
        go(second.at[turn(second_at, by)], second_in.at[by - 1], on_second(by), shard) for by in (2, 1, 3)
    ]
    for copy in small_first:
        copy.wait_recv()
    s_out[1] = (
        s_out[0].astype(F32) + s_in[3].astype(F32) + s_in[4].astype(F32) + s_in[5].astype(F32)
    ).astype(BF16)
    small_second = [
        go(s_out.at[1], s_in.at[5 + by], on_second(by), shard, True) for by in (1, 2, 3)
    ]
    for copy in along_second:
        copy.wait_recv()
    piece[...] = (
        second[second_at].astype(F32) + second_in[0].astype(F32) + second_in[1].astype(F32)
        + second_in[2].astype(F32)
    ).astype(BF16)
    along_shard = [
        go(piece.at[turn(shard, by)], third_in.at[by - 1], expert, turn(shard, by)) for by in (2, 1, 3)
    ]
    for copy in small_second:
        copy.wait_recv()
    s_out[2] = (
        s_out[1].astype(F32) + s_in[6].astype(F32) + s_in[7].astype(F32) + s_in[8].astype(F32)
    ).astype(BF16)
    small_back = go(s_out.at[2], s_other, sibling, shard, True)
    for copy in along_shard:
        copy.wait_recv()
    line[second_at] = (
        piece[shard].astype(F32) + third_in[0].astype(F32) + third_in[1].astype(F32) + third_in[2].astype(F32)
    ).astype(BF16)
    back_second = [
        go(line.at[second_at], line.at[second_at], on_second(by), shard) for by in (2, 1, 3)
    ]
    small_back.wait_recv()
    small_ref[mine, :] = s_out[2].astype(F32)
    small_ref[others, :] = s_other[...].astype(F32)
    for copy in back_second:
        copy.wait_recv()
    plane[first] = line[...].reshape(rows, line.shape[-1])
    back_first = [
        go(plane.at[first], plane.at[first], on_first(by), shard) for by in (2, 1, 3)
    ]
    own_back = go(plane.at[first], gathered.at[first], sibling, shard)
    hands = []
    for copy, by in zip(back_first, (2, 1, 3)):
        copy.wait_recv()
        came = turn(first, SIDE - by)
        hands.append(go(plane.at[came], gathered.at[came], sibling, shard))
    wide_ref[pl.ds(core * SIDE, SIDE)] = plane[...].astype(F32)
    own_back.wait_recv()
    for copy in hands:
        copy.wait_recv()
    wide_ref[pl.ds((1 - core) * SIDE, SIDE)] = gathered[...].astype(F32)
    for copy in started:
        copy.wait_send()


def reduce_all(blocks, small, collective_id):
    _, total_rows, columns = blocks.shape
    rows = total_rows // SIDE
    quarter, part = rows // 4, rows // 2
    vmem = pltpu.VMEM
    return pl.pallas_call(
        reduce_kernel,
        out_shape=(
            jax.ShapeDtypeStruct((2 * SIDE, rows, columns), F32),
            jax.ShapeDtypeStruct((rows, LANES), F32),
        ),
        in_specs=[pl.BlockSpec(memory_space=vmem)] * 2,
        out_specs=[pl.BlockSpec(memory_space=vmem)] * 2,
        scratch_shapes=[
            vmem((SIDE, total_rows, columns), BF16),
            vmem((SIDE, total_rows, columns), BF16),
            vmem((2, 2 * rows, columns), BF16),
            vmem((2, total_rows, columns), BF16),
            vmem((SIDE, SIDE, quarter, columns), BF16),
            vmem((3, SIDE, quarter, columns), BF16),
            vmem((3, quarter, columns), BF16),
            vmem((SIDE, quarter, columns), BF16),
            vmem((SIDE, quarter, columns), BF16),
            vmem((SIDE, rows, columns), BF16),
            vmem((SIDE, rows, columns), BF16),
            vmem((SIDE, rows, LANES), BF16),
            vmem((SIDE, rows, LANES), BF16),
            vmem((9, part, LANES), BF16),
            vmem((3, part, LANES), BF16),
            vmem((part, LANES), BF16),
            pltpu.SemaphoreType.DMA((28,)),
            pltpu.SemaphoreType.DMA((28,)),
            pltpu.SemaphoreType.DMA((11,)),
            pltpu.SemaphoreType.DMA((11,)),
        ],
        compiler_params=pltpu.CompilerParams(
            vmem_limit_bytes=48 * MIB, collective_id=collective_id, has_side_effects=True
        ),
        cost_estimate=pl.CostEstimate(flops=0, bytes_accessed=32 * MIB, transcendentals=0),
        name="reduce_all",
    )(blocks, small.reshape(SIDE, rows, LANES))


def forward_kernel(
    experts, capacity, x_ref, g_ref, routes_ref, wq_shard, wp_shard, ws_shard,
    wq_out, wp_out, ws_ref, ln_ref, qkv_ref, lse_ref, o_ref, x2_ref, gates_ref, pick0_ref, pick1_ref, arrived_ref,
    wq_ref, wp_ref, small_ref, send_ref, sends, receives, ex_send, ex_receive, local,
):
    rows, width = x_ref.shape
    expert, shard = lax.axis_index("expert"), lax.axis_index("wshard")
    core = lax.rem(expert, 2)
    greet(
        [(expert, lax.rem(shard + 1, SIDE)), (expert, lax.rem(shard + 3, SIDE))]
        + [(peer, shard) for peer in exchange_peers(expert)]
    )
    small, first_w, second_w = [
        RowGather(shard_ref, full_ref, split, sends.at[number], receives.at[number], expert, shard)
        for number, (shard_ref, full_ref, split) in enumerate(
            ((ws_shard, small_ref, False), (wq_shard, wq_ref, True), (wp_shard, wp_ref, True))
        )
    ]
    small.first()
    first_w.first()
    x = x_ref[...].astype(F32)
    normed, _ = normalize(x)
    small.second()
    first_w.second()
    second_w.first()
    small.third()
    small.finish()
    lane = lane_iota(rows)
    both = small_ref[...].astype(F32)
    vectors = both.T[experts : experts + 8, :]
    ln_ref[...] = vectors
    ws_ref[...] = jnp.where(lane_iota(width) < experts, both, 0.0).astype(BF16)
    h1 = (normed * vectors[0:1, :] + vectors[1:2, :]).astype(BF16)
    first_w.third()
    second_w.second()
    first_w.finish()
    keep_first = pltpu.make_async_copy(wq_ref, wq_out, local.at[1])
    keep_first.start()
    qkv_ref[...] = mm(h1, wq_ref[...]).astype(BF16)
    scale = HEAD_DIM ** (-0.5)
    lse_all = jnp.zeros((rows, LANES), F32)
    for pair in range(width // LANES):
        if pair == 2:
            second_w.third()
        at = pair * LANES
        q = qkv_ref[:, at : at + LANES]
        k = qkv_ref[:, width + at : width + at + LANES]
        v = qkv_ref[:, 2 * width + at : 2 * width + at + LANES]
        halves = []
        for half in range(2):
            own = (lane // HEAD_DIM) == half
            s = mm(jnp.where(own, q, jnp.zeros_like(q)), k, 1, 1) * scale
            top = jnp.max(s, -1, keepdims=True)
            e = jnp.exp(s - top)
            total = jnp.sum(e, -1, keepdims=True)
            lse_all = jnp.where(lane == 2 * pair + half, top + jnp.log(total), lse_all)
            halves.append(mm((e / total).astype(BF16), v))
        o_ref[:, at : at + LANES] = jnp.where(lane < HEAD_DIM, halves[0], halves[1]).astype(BF16)
    lse_ref[...] = lse_all
    second_w.finish()
    keep_second = pltpu.make_async_copy(wp_ref, wp_out, local.at[2])
    keep_second.start()
    x2 = x + mm(o_ref[...], wp_ref[...])
    x2_ref[...] = x2
    normed2, _ = normalize(x2)
    h2 = (normed2 * vectors[2:3, :] + vectors[3:4, :]).astype(BF16)
    logits = jnp.where(lane < experts, mm(h2, ws_ref[...]), -jnp.inf)
    e = jnp.exp(logits - jnp.max(logits, -1, keepdims=True))
    gates = e / jnp.sum(e, -1, keepdims=True)
    gates_ref[...] = gates
    routes = routes_ref[...]
    match = [lane == routes[:, k : k + 1] for k in range(2)]
    hits = (match[0] | match[1]).astype(F32).astype(BF16)
    earlier = lax.broadcasted_iota(jnp.int32, (rows, rows), 0) > lane_iota(rows, rows)
    before = mm(earlier.astype(F32).astype(BF16), hits)
    slots = lane_iota(rows, experts * capacity).astype(F32)
    g = g_ref[...].astype(F32)
    picks, grads = [], []
    for k in range(2):
        slot = jnp.sum(jnp.where(match[k], before, 0.0), -1, keepdims=True)
        place = (routes[:, k : k + 1] * capacity).astype(F32) + slot
        picks.append((slots == place).astype(F32).astype(BF16))
        chosen = jnp.sum(jnp.where(match[k], gates, 0.0), -1, keepdims=True)
        grads.append((chosen * g).astype(BF16))
    pick0_ref[...] = picks[0]
    pick1_ref[...] = picks[1]
    send_ref[:, :width] = mm(picks[0] + picks[1], h2, 0, 0).astype(BF16)
    send_ref[:, width:] = (mm(picks[0], grads[0], 0, 0) + mm(picks[1], grads[1], 0, 0)).astype(BF16)
    copies, keep = exchange_start(
        send_ref, arrived_ref, ex_send, ex_receive, local.at[0], expert, shard, capacity
    )
    for gather in (small, first_w, second_w):
        gather.drain()
    keep_first.wait()
    keep_second.wait()
    exchange_wait(copies, keep)


def forward(tokens, cotangent, routes, wq, wp, ws, experts, capacity):
    rows, width = tokens.shape
    slots = experts * capacity
    vmem, anywhere = pl.BlockSpec(memory_space=pltpu.VMEM), pl.BlockSpec(memory_space=pl.ANY)
    return pl.pallas_call(
        functools.partial(forward_kernel, experts, capacity),
        out_shape=(
            jax.ShapeDtypeStruct((width, 3 * width), BF16),
            jax.ShapeDtypeStruct((width, width), BF16),
            jax.ShapeDtypeStruct((width, LANES), BF16),
            jax.ShapeDtypeStruct((8, width), F32),
            jax.ShapeDtypeStruct((rows, 3 * width), BF16),
            jax.ShapeDtypeStruct((rows, LANES), F32),
            jax.ShapeDtypeStruct((rows, width), BF16),
            jax.ShapeDtypeStruct((rows, width), F32),
            jax.ShapeDtypeStruct((rows, LANES), F32),
            jax.ShapeDtypeStruct((rows, slots), BF16),
            jax.ShapeDtypeStruct((rows, slots), BF16),
            jax.ShapeDtypeStruct((slots, 2 * width), BF16),
        ),
        in_specs=[vmem] * 6,
        out_specs=[anywhere] * 2 + [vmem] * 9 + [anywhere],
        scratch_shapes=[
            pltpu.VMEM((width, 3 * width), BF16),
            pltpu.VMEM((width, width), BF16),
            pltpu.VMEM((width, LANES), BF16),
            pltpu.VMEM((slots, 2 * width), BF16),
            pltpu.SemaphoreType.DMA((3, 9)),
            pltpu.SemaphoreType.DMA((3, 8)),
            pltpu.SemaphoreType.DMA((31,)),
            pltpu.SemaphoreType.DMA((31,)),
            pltpu.SemaphoreType.DMA((3,)),
        ],
        compiler_params=pltpu.CompilerParams(
            vmem_limit_bytes=48 * MIB, collective_id=1, has_side_effects=True
        ),
        cost_estimate=pl.CostEstimate(
            flops=2 * rows * width * 6 * width, bytes_accessed=16 * MIB, transcendentals=rows * rows * 12
        ),
        name="attention_forward",
    )(tokens, cotangent, routes, wq, wp, ws)


def expert_kernel(arrived_ref, w1_ref, w2_ref, a_ref, du_ref, gw1_ref, gw2_ref):
    width = w1_ref.shape[0]
    z = arrived_ref[:, :width]
    dy = arrived_ref[:, width:]
    u = mm(z, w1_ref[...])
    da = mm(dy, w2_ref[...], 1, 1)
    phi = 0.5 * (1.0 + lax.erf(u * (2.0**-0.5)))
    density = jnp.exp(-0.5 * u * u) * 0.3989422804014327
    a = (u * phi).astype(BF16)
    du = (da * (phi + u * density)).astype(BF16)
    a_ref[...] = a
    du_ref[...] = du
    gw2_ref[...] = mm(a, dy, 0, 0).astype(BF16)
    gw1_ref[...] = mm(z, du, 0, 0).astype(BF16)


def expert_grads(arrived, w1, w2):
    rows = arrived.shape[0]
    width, hidden = w1.shape
    block = 512
    return pl.pallas_call(
        expert_kernel,
        grid=(hidden // block,),
        in_specs=[
            pl.BlockSpec((rows, 2 * width), lambda f: (0, 0)),
            pl.BlockSpec((width, block), lambda f: (0, f)),
            pl.BlockSpec((block, width), lambda f: (f, 0)),
        ],
        out_specs=[
            pl.BlockSpec((rows, block), lambda f: (0, f)),
            pl.BlockSpec((rows, block), lambda f: (0, f)),
            pl.BlockSpec((width, block), lambda f: (0, f)),
            pl.BlockSpec((block, width), lambda f: (f, 0)),
        ],
        out_shape=(
            jax.ShapeDtypeStruct((rows, hidden), BF16),
            jax.ShapeDtypeStruct((rows, hidden), BF16),
            jax.ShapeDtypeStruct((width, hidden), BF16),
            jax.ShapeDtypeStruct((hidden, width), BF16),
        ),
        compiler_params=pltpu.CompilerParams(vmem_limit_bytes=48 * MIB),
        cost_estimate=pl.CostEstimate(
            flops=8 * rows * width * hidden, bytes_accessed=24 * MIB, transcendentals=2 * rows * hidden
        ),
        name="expert_grads",
    )(arrived, w1, w2)


def expert_out_kernel(a_ref, du_ref, w1_ref, w2_ref, back_ref, total_ref):
    width = w1_ref.shape[0]
    step = pl.program_id(0)

    @pl.when(step == 0)
    def _():
        total_ref[...] = jnp.zeros_like(total_ref)

    total_ref[:, :width] += mm(a_ref[...], w2_ref[...])
    total_ref[:, width:] += mm(du_ref[...], w1_ref[...], 1, 1)

    @pl.when(step == pl.num_programs(0) - 1)
    def _():
        back_ref[...] = total_ref[...].astype(BF16)


def expert_rows(a, du, w1, w2):
    rows, hidden = a.shape
    width = w1.shape[0]
    block = 768
    return pl.pallas_call(
        expert_out_kernel,
        grid=(hidden // block,),
        in_specs=[
            pl.BlockSpec((rows, block), lambda f: (0, f)),
            pl.BlockSpec((rows, block), lambda f: (0, f)),
            pl.BlockSpec((width, block), lambda f: (0, f)),
            pl.BlockSpec((block, width), lambda f: (f, 0)),
        ],
        out_specs=pl.BlockSpec((rows, 2 * width), lambda f: (0, 0)),
        out_shape=jax.ShapeDtypeStruct((rows, 2 * width), BF16),
        scratch_shapes=[pltpu.VMEM((rows, 2 * width), F32)],
        compiler_params=pltpu.CompilerParams(vmem_limit_bytes=48 * MIB),
        cost_estimate=pl.CostEstimate(
            flops=4 * rows * width * hidden, bytes_accessed=18 * MIB, transcendentals=0
        ),
        name="expert_rows",
    )(a, du, w1, w2)


def backward_kernel(
    x_ref, g_ref, routes_ref, wq_ref, wp_ref, ws_ref, ln_ref,
    qkv_ref, lse_ref, o_ref, x2_ref, gates_ref, pick0_ref, pick1_ref, ret_ref,
    mixed_ref, dx_ref, gw_ref, gws_ref, dqkv_ref,
):
    rows, width = x_ref.shape
    lane = lane_iota(rows)
    g = g_ref[...].astype(F32)
    x2 = x2_ref[...]
    gates = gates_ref[...]
    routes = routes_ref[...]
    out = x2
    dgates = jnp.zeros((rows, LANES), F32)
    for k, pick_ref in enumerate((pick0_ref, pick1_ref)):
        match = lane == routes[:, k : k + 1]
        picked = mm(pick_ref[...], ret_ref[:, :width])
        chosen = jnp.sum(jnp.where(match, gates, 0.0), -1, keepdims=True)
        out = out + chosen * picked
        dgates = jnp.where(match, jnp.sum(g * picked, -1, keepdims=True), dgates)
    mixed_ref[...] = out.astype(BF16)
    dl = (gates * (dgates - jnp.sum(gates * dgates, -1, keepdims=True))).astype(BF16)
    dh2 = mm(pick0_ref[...] + pick1_ref[...], ret_ref[:, width:]) + mm(dl, ws_ref[...], 1, 1)
    gain1, bias1 = ln_ref[0:1, :], ln_ref[1:2, :]
    gain2, bias2 = ln_ref[2:3, :], ln_ref[3:4, :]
    n2, r2 = normalize(x2)
    h2 = (n2 * gain2 + bias2).astype(BF16)
    g_router = mm(h2, dl, 0, 0)
    g_gain2 = jnp.sum(dh2 * n2, 0, keepdims=True)
    g_bias2 = jnp.sum(dh2, 0, keepdims=True)
    dx2 = g + norm_back(dh2, n2, r2, gain2)
    dx2b = dx2.astype(BF16)
    block = gw_ref.shape[2]
    for core in range(2):
        columns = dx2b[:, core * block : (core + 1) * block]
        gw_ref[core * SIDE + 3] = mm(o_ref[...], columns, 0, 0).astype(BF16)
    do_all = mm(dx2b, wp_ref[...], 1, 1).astype(BF16)
    scale = HEAD_DIM ** (-0.5)
    for pair in range(width // LANES):
        at = pair * LANES
        q = qkv_ref[:, at : at + LANES]
        k = qkv_ref[:, width + at : width + at + LANES]
        v = qkv_ref[:, 2 * width + at : 2 * width + at + LANES]
        do = do_all[:, at : at + LANES]
        parts = []
        for half in range(2):
            own = (lane // HEAD_DIM) == half
            head = 2 * pair + half
            s = mm(jnp.where(own, q, jnp.zeros_like(q)), k, 1, 1) * scale
            p = jnp.exp(s - lse_ref[:, head : head + 1])
            dp = mm(jnp.where(own, do, jnp.zeros_like(do)), v, 1, 1)
            ds = (p * (dp - jnp.sum(dp * p, -1, keepdims=True))).astype(BF16)
            parts.append((mm(ds, k) * scale, mm(ds, q, 0, 0) * scale, mm(p.astype(BF16), do, 0, 0)))
        low = lane < HEAD_DIM
        for third, (first, second) in enumerate(zip(*parts)):
            start = third * width + at
            dqkv_ref[:, start : start + LANES] = jnp.where(low, first, second).astype(BF16)
    n1, r1 = normalize(x_ref[...].astype(F32))
    h1 = (n1 * gain1 + bias1).astype(BF16)
    for number in range(6):
        columns = dqkv_ref[:, number * block : (number + 1) * block]
        gw_ref[number // 3 * SIDE + number % 3] = mm(h1, columns, 0, 0).astype(BF16)
    dh1 = mm(dqkv_ref[...], wq_ref[...], 1, 1)
    g_gain1 = jnp.sum(dh1 * n1, 0, keepdims=True)
    g_bias1 = jnp.sum(dh1, 0, keepdims=True)
    dx_ref[...] = dx2 + norm_back(dh1, n1, r1, gain1)
    row = lax.broadcasted_iota(jnp.int32, (LANES, width), 0)
    vectors = jnp.zeros((LANES, width), F32)
    for place, vector in enumerate((g_gain1, g_bias1, g_gain2, g_bias2)):
        vectors = jnp.where(row == 32 + place, vector, vectors)
    gws_ref[...] = (g_router + vectors.T).astype(BF16)


def backward(tokens, cotangent, routes, wq, wp, ws, ln, kept, returned):
    rows, width = tokens.shape
    return pl.pallas_call(
        backward_kernel,
        out_shape=(
            jax.ShapeDtypeStruct((rows, width), BF16),
            jax.ShapeDtypeStruct((rows, width), F32),
            jax.ShapeDtypeStruct((2 * SIDE, width, width // 2), BF16),
            jax.ShapeDtypeStruct((width, LANES), BF16),
        ),
        scratch_shapes=[pltpu.VMEM((rows, 3 * width), BF16)],
        compiler_params=pltpu.CompilerParams(vmem_limit_bytes=48 * MIB),
        cost_estimate=pl.CostEstimate(
            flops=2 * rows * width * 14 * width, bytes_accessed=24 * MIB, transcendentals=rows * rows * 12
        ),
        name="attention_backward",
    )(tokens, cotangent, routes, wq, wp, ws, ln, *kept, returned)


def on_device(
    tokens, ln1_gain, ln1_bias, w_qkv, w_proj, ln2_gain, ln2_bias, w_router,
    expert_in, expert_out, routes, cotangent,
):
    rows, width = tokens.shape
    experts = w_router.shape[1]
    capacity = (5 * rows // 2 + 8 * experts - 1) // (8 * experts) * 8
    shard = w_qkv.shape[0]
    vectors = jnp.stack([ln1_gain, ln1_bias, ln2_gain, ln2_bias], 1)
    small = jnp.concatenate(
        [w_router, vectors, jnp.zeros((shard, LANES - experts - 4), BF16)], 1
    )
    wq, wp, ws, ln, *kept, arrived = forward(
        tokens, cotangent, routes, w_qkv, w_proj, small, experts, capacity
    )
    w1, w2 = expert_in[0], expert_out[0]
    active, d_hidden, g_first, g_second = expert_grads(arrived, w1, w2)
    g_first = lax.psum_scatter(g_first, "wshard", scatter_dimension=0, tiled=True)
    g_second = lax.psum_scatter(g_second, "wshard", scatter_dimension=0, tiled=True)
    back = expert_rows(active, d_hidden, w1, w2)
    returned = exchange(back, capacity, 2)
    mixed, grad_tokens, gw, gws = backward(
        tokens, cotangent, routes, wq, wp, ws, ln, kept, returned
    )
    gw, gws = reduce_all(gw, gws, 3)
    return (
        mixed,
        grad_tokens,
        gws[:, experts],
        gws[:, experts + 1],
        jnp.concatenate([gw[0], gw[1], gw[2], gw[4], gw[5], gw[6]], 1),
        jnp.concatenate([gw[3], gw[7]], 1),
        gws[:, experts + 2],
        gws[:, experts + 3],
        gws[:, :experts],
        g_first.astype(F32)[None],
        g_second.astype(F32)[None],
    )


def solution(mesh):
    in_specs = (
        P(("expert", "wshard"), None),
        P("wshard"),
        P("wshard"),
        P("wshard", None),
        P("wshard", None),
        P("wshard"),
        P("wshard"),
        P("wshard", None),
        P("expert", None, None),
        P("expert", None, None),
        P(("expert", "wshard"), None),
        P(("expert", "wshard"), None),
    )
    out_specs = (
        P(("expert", "wshard"), None),
        P(("expert", "wshard"), None),
        P("wshard"),
        P("wshard"),
        P("wshard", None),
        P("wshard", None),
        P("wshard"),
        P("wshard"),
        P("wshard", None),
        P("expert", "wshard", None),
        P("expert", "wshard", None),
    )
    return jax.shard_map(
        on_device, mesh=mesh, in_specs=in_specs, out_specs=out_specs, check_vma=False
    )
```

```python
import functools

import jax
import jax.numpy as jnp
from jax import lax
from jax.experimental import pallas as pl
from jax.experimental.pallas import tpu as pltpu
from jax.sharding import PartitionSpec as P

HEAD_DIM = 64
EPSILON = 1e-06
F32 = jnp.float32
BF16 = jnp.bfloat16
LANES = 128
MIB = 1 << 20


def mm(left, right, left_dim=1, right_dim=0):
    return lax.dot_general(
        left, right, (((left_dim,), (right_dim,)), ((), ())), preferred_element_type=F32
    )


def normalize(values):
    centered = values - jnp.mean(values, -1, keepdims=True)
    inverse = lax.rsqrt(jnp.mean(centered * centered, -1, keepdims=True) + EPSILON)
    return centered * inverse, inverse


def norm_back(upstream, normed, inverse, gain):
    scaled = upstream * gain
    return inverse * (
        scaled
        - jnp.mean(scaled, -1, keepdims=True)
        - normed * jnp.mean(scaled * normed, -1, keepdims=True)
    )


def lane_iota(rows, columns=LANES):
    return lax.broadcasted_iota(jnp.int32, (rows, columns), 1)


MESH = pl.DeviceIdType.MESH
SIDE = 4


def remote(source, target, send, receive, expert, shard):
    return pltpu.make_async_remote_copy(
        src_ref=source, dst_ref=target, send_sem=send, recv_sem=receive,
        device_id=(expert, shard), device_id_type=MESH,
    )


def greet(devices):
    barrier = pltpu.get_barrier_semaphore()
    for expert, shard in devices:
        pl.semaphore_signal(barrier, inc=1, device_id=(expert, shard), device_id_type=MESH)
    pl.semaphore_wait(barrier, len(devices))


class RowGather:
    def __init__(self, shard_ref, full_ref, send, receive, expert, shard):
        self.rows, columns = shard_ref.shape
        self.shard_ref, self.full_ref = shard_ref, full_ref
        self.send, self.receive = send, receive
        self.expert, self.shard = expert, shard
        core = lax.rem(expert, 2)
        self.sibling = expert + 1 - 2 * core
        self.after, self.before = lax.rem(shard + 1, SIDE), lax.rem(shard + 3, SIDE)
        self.across = lax.rem(shard + 2, SIDE)
        half = columns // 2
        self.columns = pl.ds(pl.multiple_of(core * half, LANES), half)

    def at(self, shard, start, count, columns):
        place = pl.multiple_of(shard * self.rows + start, 16)
        return self.full_ref.at[pl.ds(place, count), columns]

    def ring(self, number, source, target, shard):
        return remote(
            source, target, self.send.at[number], self.receive.at[number], self.expert, shard
        )

    def first(self):
        target = self.at(self.shard, 0, self.rows, self.columns)
        source = self.shard_ref.at[:, self.columns]
        self.to_after = self.ring(0, source, target, self.after)
        self.to_before = self.ring(1, source, target, self.before)
        self.own = pltpu.make_async_copy(
            self.shard_ref, self.at(self.shard, 0, self.rows, pl.ds(0, self.shard_ref.shape[1])),
            self.send.at[8],
        )
        self.to_after.start()
        self.to_before.start()
        self.own.start()

    def hand(self, number, shard, start, count):
        block = self.at(shard, start, count, self.columns)
        copy = remote(
            block, block, self.send.at[number], self.receive.at[number], self.sibling, self.shard
        )
        copy.start()
        return copy

    def second(self):
        half = self.rows // 2
        self.to_after.wait_recv()
        top = self.at(self.before, 0, half, self.columns)
        self.pass_after = self.ring(2, top, top, self.after)
        self.pass_after.start()
        self.to_before.wait_recv()
        bottom = self.at(self.after, half, half, self.columns)
        self.pass_before = self.ring(3, bottom, bottom, self.before)
        self.pass_before.start()
        self.handed = [
            self.hand(4, self.before, 0, self.rows),
            self.hand(5, self.after, 0, self.rows),
        ]

    def third(self):
        half = self.rows // 2
        self.pass_after.wait_recv()
        self.handed.append(self.hand(6, self.across, 0, half))
        self.pass_before.wait_recv()
        self.handed.append(self.hand(7, self.across, half, half))

    def finish(self):
        self.own.wait()
        for copy in self.handed:
            copy.wait_recv()

    def drain(self):
        for copy in (self.to_after, self.to_before, self.pass_after, self.pass_before, *self.handed):
            copy.wait_send()


def exchange_peers(expert):
    return [
        lax.rem(expert // 8 + dz, SIDE) * 8 + lax.rem(lax.rem(expert // 2, SIDE) + dx, SIDE) * 2
        + lax.rem(expert + dc, 2)
        for dz, dx, dc in exchange_order()
    ]


def exchange_order():
    reach = [0, 1, 2, 1]
    steps = [(dz, dx, dc) for dz in range(SIDE) for dx in range(SIDE) for dc in range(2)]
    return sorted(steps[1:], key=lambda step: -reach[step[0]] - reach[step[1]])


def exchange_start(source_ref, target_ref, send, receive, local, expert, shard, capacity):
    own = pl.ds(pl.multiple_of(expert * capacity, 16), capacity)
    copies = []
    for number, peer in enumerate(exchange_peers(expert)):
        block = pl.ds(pl.multiple_of(peer * capacity, 16), capacity)
        copy = remote(
            source_ref.at[block, :], target_ref.at[own, :], send.at[number], receive.at[number], peer, shard
        )
        copy.start()
        copies.append(copy)
    keep = pltpu.make_async_copy(source_ref.at[own, :], target_ref.at[own, :], local)
    keep.start()
    return copies, keep


def exchange_wait(copies, keep):
    keep.wait()
    for copy in copies:
        copy.wait()


def forward_kernel(
    experts, capacity, x_in, g_in, routes_ref, wq_shard, wp_shard, router_ref, gain1_ref, bias1_ref, gain2_ref, bias2_ref,
    routes_out, wq_out, wp_out, ws_ref, ln_ref, qkv_ref, lse_ref, o_ref, x2_ref, gates_ref, pick0_ref, pick1_ref, arrived_ref,
    x_ref, g_ref, own_ref, small_ref, wq_ref, wp_ref, send_ref, sends, receives, s_send, s_receive, ex_send, ex_receive, local,
):
    rows, width = x_ref.shape
    load_x = pltpu.make_async_copy(x_in, x_ref, local.at[3])
    load_x.start()
    load_g = pltpu.make_async_copy(g_in, g_ref, local.at[4])
    load_g.start()
    expert, shard = lax.axis_index("expert"), lax.axis_index("wshard")
    core = lax.rem(expert, 2)
    pad = jnp.zeros((own_ref.shape[0] - experts - 4, width // SIDE), F32)
    mini = [router_ref[...].astype(F32)] + [
        ref[...].astype(F32).reshape(1, width // SIDE) for ref in (gain1_ref, bias1_ref, gain2_ref, bias2_ref)
    ]
    own_ref[:, : width // SIDE] = jnp.concatenate(mini + [pad], 0).astype(BF16)
    own_ref[:, width // SIDE :] = jnp.zeros((own_ref.shape[0], own_ref.shape[1] - width // SIDE), BF16)
    greet(
        [(expert, lax.rem(shard + by, SIDE)) for by in (1, 2, 3)]
        + [(peer, shard) for peer in exchange_peers(expert)]
    )
    small = []
    for by in (1, 2, 3):
        copy = remote(
            own_ref, small_ref.at[by - 1], s_send.at[by - 1], s_receive.at[by - 1], expert, lax.rem(shard + by, SIDE)
        )
        copy.start()
        small.append(copy)
    first_w, second_w = [
        RowGather(shard_ref, full_ref, sends.at[number], receives.at[number], expert, shard)
        for number, (shard_ref, full_ref) in enumerate(((wq_shard, wq_ref), (wp_shard, wp_ref)))
    ]
    first_w.first()
    load_x.wait()
    x = x_ref[...].astype(F32)
    normed, _ = normalize(x)
    first_w.second()
    second_w.first()
    for copy in small:
        copy.wait_recv()
    pieces = []
    for place in range(SIDE):
        piece = own_ref[...].astype(F32)
        for by in (1, 2, 3):
            piece = jnp.where(lax.rem(shard + SIDE - by, SIDE) == place, small_ref[by - 1].astype(F32), piece)
        pieces.append(piece[:, : width // SIDE])
    lane = lane_iota(rows)
    both = jnp.concatenate(pieces, 1)
    vectors = both[experts : experts + 8, :]
    ln_ref[...] = vectors
    ws_ref[...] = jnp.concatenate([both[:experts], jnp.zeros((LANES - experts, width), F32)], 0).astype(BF16)
    h1 = (normed * vectors[0:1, :] + vectors[1:2, :]).astype(BF16)
    first_w.third()
    second_w.second()
    first_w.finish()
    keep_first = pltpu.make_async_copy(wq_ref, wq_out, local.at[1])
    keep_first.start()
    qkv_ref[...] = mm(h1, wq_ref[...]).astype(BF16)
    scale = HEAD_DIM ** (-0.5)
    lse_all = jnp.zeros((rows, LANES), F32)
    for pair in range(width // LANES):
        if pair == 2:
            second_w.third()
        at = pair * LANES
        q = qkv_ref[:, at : at + LANES]
        k = qkv_ref[:, width + at : width + at + LANES]
        v = qkv_ref[:, 2 * width + at : 2 * width + at + LANES]
        halves = []
        for half in range(2):
            own = (lane // HEAD_DIM) == half
            s = mm(jnp.where(own, q, jnp.zeros_like(q)), k, 1, 1) * scale
            top = jnp.max(s, -1, keepdims=True)
            e = jnp.exp(s - top)
            total = jnp.sum(e, -1, keepdims=True)
            lse_all = jnp.where(lane == 2 * pair + half, top + jnp.log(total), lse_all)
            halves.append(mm((e / total).astype(BF16), v))
        o_ref[:, at : at + LANES] = jnp.where(lane < HEAD_DIM, halves[0], halves[1]).astype(BF16)
    lse_ref[...] = lse_all
    second_w.finish()
    keep_second = pltpu.make_async_copy(wp_ref, wp_out, local.at[2])
    keep_second.start()
    x2 = x + mm(o_ref[...], wp_ref[...])
    x2_ref[...] = x2
    normed2, _ = normalize(x2)
    h2 = (normed2 * vectors[2:3, :] + vectors[3:4, :]).astype(BF16)
    logits = jnp.where(lane < experts, mm(h2, ws_ref[...], 1, 1), -jnp.inf)
    e = jnp.exp(logits - jnp.max(logits, -1, keepdims=True))
    gates = e / jnp.sum(e, -1, keepdims=True)
    gates_ref[...] = gates
    diagonal = lax.broadcasted_iota(jnp.int32, (rows, rows), 0) == lane_iota(rows, rows)
    routes = mm(diagonal.astype(F32).astype(BF16), routes_ref[...].astype(F32).astype(BF16), 1, 1)
    lane_number = lane.astype(F32)
    match = [lane_number == routes[:, k : k + 1] for k in range(2)]
    routes_out[...] = jnp.where(lane == 0, routes[:, 0:1], routes[:, 1:2])
    hits = (match[0] | match[1]).astype(F32).astype(BF16)
    earlier = lax.broadcasted_iota(jnp.int32, (rows, rows), 0) > lane_iota(rows, rows)
    before = mm(earlier.astype(F32).astype(BF16), hits)
    slots = lane_iota(rows, experts * capacity).astype(F32)
    load_g.wait()
    g = g_ref[...].astype(F32)
    picks, grads = [], []
    for k in range(2):
        slot = jnp.sum(jnp.where(match[k], before, 0.0), -1, keepdims=True)
        place = routes[:, k : k + 1] * capacity + slot
        picks.append((slots == place).astype(F32).astype(BF16))
        chosen = jnp.sum(jnp.where(match[k], gates, 0.0), -1, keepdims=True)
        grads.append((chosen * g).astype(BF16))
    pick0_ref[...] = picks[0]
    pick1_ref[...] = picks[1]
    send_ref[:, :width] = mm(picks[0] + picks[1], h2, 0, 0).astype(BF16)
    send_ref[:, width:] = (mm(picks[0], grads[0], 0, 0) + mm(picks[1], grads[1], 0, 0)).astype(BF16)
    copies, keep = exchange_start(
        send_ref, arrived_ref, ex_send, ex_receive, local.at[0], expert, shard, capacity
    )
    for copy in small:
        copy.wait_send()
    for gather in (first_w, second_w):
        gather.drain()
    keep_first.wait()
    keep_second.wait()
    exchange_wait(copies, keep)


def forward(tokens, cotangent, routes, wq, wp, router, vectors, experts, capacity):
    rows, width = tokens.shape
    slots = experts * capacity
    vmem, anywhere = pl.BlockSpec(memory_space=pltpu.VMEM), pl.BlockSpec(memory_space=pl.ANY)
    return pl.pallas_call(
        functools.partial(forward_kernel, experts, capacity),
        out_shape=(
            jax.ShapeDtypeStruct((rows, LANES), F32),
            jax.ShapeDtypeStruct((width, 3 * width), BF16),
            jax.ShapeDtypeStruct((width, width), BF16),
            jax.ShapeDtypeStruct((LANES, width), BF16),
            jax.ShapeDtypeStruct((8, width), F32),
            jax.ShapeDtypeStruct((rows, 3 * width), BF16),
            jax.ShapeDtypeStruct((rows, LANES), F32),
            jax.ShapeDtypeStruct((rows, width), BF16),
            jax.ShapeDtypeStruct((rows, width), F32),
            jax.ShapeDtypeStruct((rows, LANES), F32),
            jax.ShapeDtypeStruct((rows, slots), BF16),
            jax.ShapeDtypeStruct((rows, slots), BF16),
            jax.ShapeDtypeStruct((slots, 2 * width), BF16),
        ),
        in_specs=[anywhere] * 2 + [vmem] + [anywhere] * 2 + [vmem] * 5,
        out_specs=[vmem] + [anywhere] * 2 + [vmem] * 9 + [anywhere],
        scratch_shapes=[
            pltpu.VMEM((rows, width), BF16),
            pltpu.VMEM((rows, width), BF16),
            pltpu.VMEM((48, 256), BF16),
            pltpu.VMEM((3, 48, 256), BF16),
            pltpu.VMEM((width, 3 * width), BF16),
            pltpu.VMEM((width, width), BF16),
            pltpu.VMEM((slots, 2 * width), BF16),
            pltpu.SemaphoreType.DMA((2, 9)),
            pltpu.SemaphoreType.DMA((2, 8)),
            pltpu.SemaphoreType.DMA((3,)),
            pltpu.SemaphoreType.DMA((3,)),
            pltpu.SemaphoreType.DMA((31,)),
            pltpu.SemaphoreType.DMA((31,)),
            pltpu.SemaphoreType.DMA((5,)),
        ],
        compiler_params=pltpu.CompilerParams(
            vmem_limit_bytes=58 * MIB, collective_id=1, has_side_effects=True
        ),
        cost_estimate=pl.CostEstimate(
            flops=2 * rows * width * 6 * width, bytes_accessed=16 * MIB, transcendentals=rows * rows * 12
        ),
        name="attention_forward",
    )(tokens, cotangent, routes, wq, wp, router, *vectors)


def expert_kernel(arrived_ref, w1_ref, w2_ref, a_ref, du_ref, gw1_ref, gw2_ref):
    width = w1_ref.shape[0]
    z = arrived_ref[:, :width]
    dy = arrived_ref[:, width:]
    u = mm(z, w1_ref[...])
    da = mm(dy, w2_ref[...], 1, 1)
    phi = 0.5 * (1.0 + lax.erf(u * (2.0**-0.5)))
    density = jnp.exp(-0.5 * u * u) * 0.3989422804014327
    a = (u * phi).astype(BF16)
    du = (da * (phi + u * density)).astype(BF16)
    a_ref[...] = a
    du_ref[...] = du
    gw2_ref[...] = mm(a, dy, 0, 0).astype(BF16)
    gw1_ref[...] = mm(z, du, 0, 0).astype(BF16)


def expert_grads(arrived, w1, w2):
    rows = arrived.shape[0]
    width, hidden = w1.shape
    block = 512
    return pl.pallas_call(
        expert_kernel,
        grid=(hidden // block,),
        in_specs=[
            pl.BlockSpec((rows, 2 * width), lambda f: (0, 0)),
            pl.BlockSpec((width, block), lambda f: (0, f)),
            pl.BlockSpec((block, width), lambda f: (f, 0)),
        ],
        out_specs=[
            pl.BlockSpec((rows, block), lambda f: (0, f)),
            pl.BlockSpec((rows, block), lambda f: (0, f)),
            pl.BlockSpec((width, block), lambda f: (0, f)),
            pl.BlockSpec((block, width), lambda f: (f, 0)),
        ],
        out_shape=(
            jax.ShapeDtypeStruct((rows, hidden), BF16),
            jax.ShapeDtypeStruct((rows, hidden), BF16),
            jax.ShapeDtypeStruct((width, hidden), BF16),
            jax.ShapeDtypeStruct((hidden, width), BF16),
        ),
        compiler_params=pltpu.CompilerParams(vmem_limit_bytes=58 * MIB),
        cost_estimate=pl.CostEstimate(
            flops=8 * rows * width * hidden, bytes_accessed=24 * MIB, transcendentals=2 * rows * hidden
        ),
        name="expert_grads",
    )(arrived, w1, w2)


def rows_kernel(
    capacity, a_ref, du_ref, w1_ref, w2_ref, gw1_ref, gw2_ref, y_ref, dz_ref, side1_ref, side2_ref,
    a_buf, du_buf, w1_buf, w2_buf, y_buf, dz_buf, total, loads, sends, receives, half_send, half_receive,
):
    expert, shard = lax.axis_index("expert"), lax.axis_index("wshard")
    width, hidden = w1_ref.shape
    block = hidden // SIDE
    after, before, across = [lax.rem(shard + by, SIDE) for by in (1, 3, 2)]
    queue = []
    for number in range(SIDE):
        at = pl.ds(number * block, block)
        for place, (source, target) in enumerate(
            ((a_ref.at[:, at], a_buf.at[:, at]), (w2_ref.at[at, :], w2_buf.at[at, :]))
        ):
            queue.append(pltpu.make_async_copy(source, target, loads.at[place, number]))
    for number in range(SIDE):
        at = pl.ds(number * block, block)
        for place, (source, target) in enumerate(
            ((du_ref.at[:, at], du_buf.at[:, at]), (w1_ref.at[:, at], w1_buf.at[:, at]))
        ):
            queue.append(pltpu.make_async_copy(source, target, loads.at[2 + place, number]))
    for copy in queue:
        copy.start()
    greet([(peer, shard) for peer in exchange_peers(expert)] + [(expert, after), (expert, before)])
    halves = []
    for place, (source, target, rows) in enumerate(
        ((gw1_ref, side1_ref, width // SIDE), (gw2_ref, side2_ref, hidden // SIDE))
    ):
        for number, peer in enumerate((after, before)):
            start = pl.multiple_of(across * rows + number * (rows // 2), 16)
            copy = remote(
                source.at[pl.ds(start, rows // 2), :], target.at[number],
                half_send.at[place, number], half_receive.at[place, number], expert, peer,
            )
            copy.start()
            halves.append(copy)
    moves = []
    for number in range(SIDE):
        queue[2 * number].wait()
        queue[2 * number + 1].wait()
        at = slice(number * block, (number + 1) * block)
        term = mm(a_buf[:, at], w2_buf[at, :])
        total[...] = term if number == 0 else total[...] + term
    y_buf[...] = total[...].astype(BF16)
    moves.append(
        exchange_start(y_buf, y_ref, sends.at[0], receives.at[0], loads.at[4, 0], expert, shard, capacity)
    )
    for number in range(SIDE):
        queue[2 * SIDE + 2 * number].wait()
        queue[2 * SIDE + 2 * number + 1].wait()
        at = slice(number * block, (number + 1) * block)
        term = mm(du_buf[:, at], w1_buf[:, at], 1, 1)
        total[...] = term if number == 0 else total[...] + term
    dz_buf[...] = total[...].astype(BF16)
    moves.append(
        exchange_start(dz_buf, dz_ref, sends.at[1], receives.at[1], loads.at[4, 1], expert, shard, capacity)
    )
    for copies, keep in moves:
        exchange_wait(copies, keep)
    for copy in halves:
        copy.wait()


def expert_rows(a, du, w1, w2, gw1, gw2, capacity, collective_id):
    rows, hidden = a.shape
    width = w1.shape[0]
    vmem, semaphores = pltpu.VMEM, pltpu.SemaphoreType.DMA
    anywhere = pl.BlockSpec(memory_space=pl.ANY)
    return pl.pallas_call(
        functools.partial(rows_kernel, capacity),
        out_shape=(
            jax.ShapeDtypeStruct((rows, width), BF16),
            jax.ShapeDtypeStruct((rows, width), BF16),
            jax.ShapeDtypeStruct((2, width // 8, hidden), BF16),
            jax.ShapeDtypeStruct((2, hidden // 8, width), BF16),
        ),
        in_specs=[anywhere] * 6,
        out_specs=[anywhere] * 4,
        scratch_shapes=[
            vmem((rows, hidden), BF16), vmem((rows, hidden), BF16),
            vmem((width, hidden), BF16), vmem((hidden, width), BF16),
            vmem((rows, width), BF16), vmem((rows, width), BF16), vmem((rows, width), F32),
            semaphores((5, SIDE)), semaphores((2, 31)), semaphores((2, 31)),
            semaphores((2, 2)), semaphores((2, 2)),
        ],
        compiler_params=pltpu.CompilerParams(
            vmem_limit_bytes=58 * MIB, collective_id=collective_id, has_side_effects=True
        ),
        cost_estimate=pl.CostEstimate(
            flops=4 * rows * width * hidden, bytes_accessed=24 * MIB, transcendentals=0
        ),
        name="expert_rows",
    )(a, du, w1, w2, gw1, gw2)


def tail_kernel(
    x_in, g_in, routes_in, wq_in, wp_in, ws_in, ln_in, qkv_in, lse_in, o_in, x2_in, gates_in, pick0_in, pick1_in,
    y_in, dz_in, gw1_in, gw2_in, side1_in, side2_in,
    mixed_ref, dx_ref, gwq_ref, gwp_ref, small_ref, gw1_ref, gw2_ref,
    x_ref, g_ref, routes_ref, wq_ref, wp_ref, ws_ref, ln_ref, qkv_ref, lse_ref, o_ref, x2_ref, gates_ref,
    pick0_ref, pick1_ref, y_ref, dz_ref, side1, side2, part1, part2, came1, came2, do_ref, dqkv_ref, h1_ref,
    theirs, ours, paired, summed, side, first_in, second, second_in, third_in, piece, line, plane, gathered,
    s_ref, s_pair, s_sum, s_in, s_out, s_other,
    loads, send, receive, s_send, s_receive, g_send, g_receive,
):
    expert, shard = lax.axis_index("expert"), lax.axis_index("wshard")
    core = lax.rem(expert, 2)
    x_at, z_at = lax.rem(expert // 2, SIDE), expert // 8
    sibling = expert + 1 - 2 * core
    first, second_at = x_at * (1 - core) + z_at * core, z_at * (1 - core) + x_at * core
    first_step, second_step = 2 + 6 * core, 8 - 6 * core

    def turn(place, by):
        return lax.rem(place + by, SIDE)

    def on_first(by):
        return expert + (turn(first, by) - first) * first_step

    def on_second(by):
        return expert + (turn(second_at, by) - second_at) * second_step

    load_count = [0]

    def load(source, target):
        copy = pltpu.make_async_copy(source, target, loads.at[load_count[0]])
        load_count[0] += 1
        copy.start()
        return copy

    rows1, rows2 = part1.shape[1], part2.shape[1]

    def shard_rows(ref, by, rows):
        return ref.at[pl.ds(pl.multiple_of(turn(shard, by) * rows, 16), rows), :]

    load_first = [load(side1_in, side1)] + [
        load(shard_rows(gw1_in, by, rows1), part1.at[number]) for number, by in enumerate((1, 3))
    ]
    load_out = [
        load(*pair) for pair in (
            (y_in, y_ref), (pick0_in, pick0_ref), (pick1_in, pick1_ref), (x2_in, x2_ref), (g_in, g_ref),
            (gates_in, gates_ref), (routes_in, routes_ref),
        )
    ]
    load_gates = [
        load(*pair) for pair in (
            (dz_in, dz_ref), (ws_in, ws_ref), (ln_in, ln_ref), (wp_in, wp_ref), (o_in, o_ref), (x_in, x_ref),
        )
    ]
    load_heads = [load(qkv_in, qkv_ref), load(lse_in, lse_ref)]
    load_second = [load(side2_in, side2)] + [
        load(shard_rows(gw2_in, by, rows2), part2.at[number]) for number, by in enumerate((1, 3))
    ]
    load_last = [load(wq_in, wq_ref)]
    load_own = [
        load(shard_rows(gw1_in, 0, rows1), part1.at[2]), load(shard_rows(gw2_in, 0, rows2), part2.at[2])
    ]

    greet(
        [(sibling, shard)]
        + [(on_first(by), shard) for by in (1, 2, 3)]
        + [(on_second(by), shard) for by in (1, 2, 3)]
        + [(expert, turn(shard, by)) for by in (1, 2, 3)]
    )
    started = []
    counts = {}

    def go(source, target, to_expert, to_shard, sends=send, receives=receive, kind="wide"):
        number = counts.get(kind, 0)
        counts[kind] = number + 1
        copy = remote(source, target, sends.at[number], receives.at[number], to_expert, to_shard)
        copy.start()
        started.append(copy)
        return copy

    def go_small(*args):
        return go(*args, sends=s_send, receives=s_receive, kind="small")

    def add(left, right):
        return (left.astype(F32) + right.astype(F32)).astype(BF16)

    def join(part, came_half):
        half = part.shape[1] // 2
        part[0, :half] = add(part[0, :half], came_half[0])
        part[1, half:] = add(part[1, half:], came_half[1])

    def pass_on(part, came, start, count):
        at = pl.ds(start, count)
        return [
            go(
                part.at[number, at], came.at[number, at], expert, turn(shard, by), g_send, g_receive, "expert"
            )
            for number, by in enumerate((1, 3))
        ]

    for copy in load_first:
        copy.wait()
    join(part1, side1)
    grads_first = pass_on(part1, came1, 0, rows1)

    for copy in load_out:
        copy.wait()
    rows, width = x_ref.shape
    lane = lane_iota(rows)
    g = g_ref[...].astype(F32)
    x2 = x2_ref[...]
    gates = gates_ref[...]
    routes = routes_ref[...]
    out = x2
    dgates = jnp.zeros((rows, LANES), F32)
    for k, pick_ref in enumerate((pick0_ref, pick1_ref)):
        match = lane.astype(F32) == routes[:, k : k + 1]
        picked = mm(pick_ref[...], y_ref[...])
        chosen = jnp.sum(jnp.where(match, gates, 0.0), -1, keepdims=True)
        out = out + chosen * picked
        dgates = jnp.where(match, jnp.sum(g * picked, -1, keepdims=True), dgates)
    mixed_ref[...] = out.astype(BF16)
    dl = (gates * (dgates - jnp.sum(gates * dgates, -1, keepdims=True))).astype(BF16)
    for copy in load_gates:
        copy.wait()
    dh2 = mm(pick0_ref[...] + pick1_ref[...], dz_ref[...]) + mm(dl, ws_ref[...])
    gain1, bias1 = ln_ref[0:1, :], ln_ref[1:2, :]
    gain2, bias2 = ln_ref[2:3, :], ln_ref[3:4, :]
    n2, r2 = normalize(x2)
    h2 = (n2 * gain2 + bias2).astype(BF16)
    g_router = mm(dl, h2, 0, 0)
    g_gain2 = jnp.sum(dh2 * n2, 0, keepdims=True)
    g_bias2 = jnp.sum(dh2, 0, keepdims=True)
    dx2 = g + norm_back(dh2, n2, r2, gain2)
    dx_ref[...] = dx2
    dx2b = dx2.astype(BF16)
    do_ref[...] = dx2b
    block = width // 2
    mine = pl.ds(pl.multiple_of(core * block, LANES), block)
    others = pl.ds(pl.multiple_of((1 - core) * block, LANES), block)
    theirs[3] = mm(o_ref[...], do_ref[:, others], 0, 0).astype(BF16)
    pair = [None] * SIDE
    pair[3] = go(theirs.at[3], paired.at[3], sibling, shard)
    ours[3] = mm(o_ref[...], do_ref[:, mine], 0, 0).astype(BF16)
    do_ref[...] = mm(dx2b, wp_ref[...], 1, 1).astype(BF16)
    n1, r1 = normalize(x_ref[...].astype(F32))
    h1_ref[...] = (n1 * gain1 + bias1).astype(BF16)
    for copy in load_second:
        copy.wait()
    join(part2, side2)
    grads_second = pass_on(part2, came2, 0, rows2 // 2)
    for copy in load_heads:
        copy.wait()
    scale = HEAD_DIM ** (-0.5)
    low = lane < HEAD_DIM

    def heads(start):
        for step in range(block // LANES):
            at = [
                pl.ds(pl.multiple_of(third * width + start + step * LANES, LANES), LANES) for third in range(3)
            ]
            q, k, v = qkv_ref[:, at[0]], qkv_ref[:, at[1]], qkv_ref[:, at[2]]
            do = do_ref[:, at[0]]
            parts = []
            for half in range(2):
                own = (lane // HEAD_DIM) == half
                head = start // HEAD_DIM + 2 * step + half
                lse = jnp.sum(jnp.where(lane == head, lse_ref[...], 0.0), -1, keepdims=True)
                s = mm(jnp.where(own, q, jnp.zeros_like(q)), k, 1, 1) * scale
                p = jnp.exp(s - lse)
                dp = mm(jnp.where(own, do, jnp.zeros_like(do)), v, 1, 1)
                ds = (p * (dp - jnp.sum(dp * p, -1, keepdims=True))).astype(BF16)
                parts.append((mm(ds, k) * scale, mm(ds, q, 0, 0) * scale, mm(p.astype(BF16), do, 0, 0)))
            for third, (left, right) in enumerate(zip(*parts)):
                dqkv_ref[:, at[third]] = jnp.where(low, left, right).astype(BF16)

    def weight_grads(target, start):
        for third in range(3):
            columns = pl.ds(pl.multiple_of(third * width + start, LANES), block)
            target[third] = mm(h1_ref[...], dqkv_ref[:, columns], 0, 0).astype(BF16)

    heads((1 - core) * block)
    weight_grads(theirs, (1 - core) * block)
    for third in range(3):
        pair[third] = go(theirs.at[third], paired.at[third], sibling, shard)
    heads(core * block)
    weight_grads(ours, core * block)
    for copy in pair:
        copy.wait_recv()

    order = (2, 1, 3, 0)

    def add_pair(number):
        chunk = turn(first, order[number])
        summed[number] = add(ours[chunk], paired[chunk])

    wide = s_ref.shape[1]
    part, quarter, half = wide // 2, wide // 4, 2 * wide
    add_pair(0)
    relay_up = go(summed.at[0, pl.ds(0, half)], side.at[0], on_first(1), shard)
    relay_down = go(summed.at[0, pl.ds(half, half)], side.at[1], on_first(3), shard)
    add_pair(1)
    add_pair(2)

    for copy in load_last:
        copy.wait()
    dh1 = mm(dqkv_ref[...], wq_ref[...], 1, 1)
    g_gain1 = jnp.sum(dh1 * n1, 0, keepdims=True)
    g_bias1 = jnp.sum(dh1, 0, keepdims=True)
    row = lax.broadcasted_iota(jnp.int32, (LANES, width), 0)
    vectors = g_router
    for place, vector in enumerate((g_gain1, g_bias1, g_gain2, g_bias2)):
        vectors = jnp.where(row == 32 + place, vector, vectors)
    s_ref[...] = vectors.T.astype(BF16).reshape(s_ref.shape)
    small_pair = go_small(s_ref, s_pair, sibling, shard)

    relay_up.wait_recv()
    summed[1, :half] = add(summed[1, :half], side[0])
    up = go(summed.at[1], first_in.at[0], on_first(1), shard)
    relay_down.wait_recv()
    summed[2, half:] = add(summed[2, half:], side[1])
    down = go(summed.at[2], first_in.at[1], on_first(3), shard)
    add_pair(3)
    dx_ref[...] += norm_back(dh1, n1, r1, gain1)

    small_pair.wait_recv()
    s_sum[...] = add(s_ref[...], s_pair[...])
    s_mine = pl.ds(pl.multiple_of(core * part, 16), part)
    s_others = pl.ds(pl.multiple_of((1 - core) * part, 16), part)
    small_along = [
        go_small(s_sum.at[turn(shard, by), s_mine, :], s_in.at[by - 1], expert, turn(shard, by)) for by in (1, 2, 3)
    ]
    for copy in small_along:
        copy.wait_recv()

    def four(own, a, b, c):
        return own.astype(F32) + a.astype(F32) + b.astype(F32) + c.astype(F32)

    s_out[0] = four(s_sum[shard, s_mine, :], s_in[0], s_in[1], s_in[2]).astype(BF16)
    small_first = [go_small(s_out.at[0], s_in.at[2 + by], on_first(by), shard) for by in (1, 2, 3)]

    up.wait_recv()
    down.wait_recv()
    for own_shard in range(SIDE):
        for place in range(SIDE):
            at = pl.ds(own_shard * wide + place * quarter, quarter)
            second[place, own_shard] = (
                summed[3, at, :].astype(F32) + first_in[0, at, :].astype(F32) + first_in[1, at, :].astype(F32)
            ).astype(BF16)
    along_second = [
        go(second.at[turn(second_at, by)], second_in.at[by - 1], on_second(by), shard) for by in (2, 1, 3)
    ]
    for copy in small_first:
        copy.wait_recv()
    s_out[1] = four(s_out[0], s_in[3], s_in[4], s_in[5]).astype(BF16)
    small_second = [go_small(s_out.at[1], s_in.at[5 + by], on_second(by), shard) for by in (1, 2, 3)]
    for copy in along_second:
        copy.wait_recv()
    piece[...] = four(second[second_at], second_in[0], second_in[1], second_in[2]).astype(BF16)
    along_shard = [
        go(piece.at[turn(shard, by)], third_in.at[by - 1], expert, turn(shard, by)) for by in (2, 1, 3)
    ]
    grads_second += pass_on(part2, came2, rows2 // 2, rows2 // 2)
    for copy in small_second:
        copy.wait_recv()
    s_out[2] = four(s_out[1], s_in[6], s_in[7], s_in[8]).astype(BF16)
    small_back = go_small(s_out.at[2], s_other, sibling, shard)
    for copy in load_own:
        copy.wait()
    for copy in along_shard:
        copy.wait_recv()
    line[second_at] = four(piece[shard], third_in[0], third_in[1], third_in[2]).astype(BF16)
    back_second = [
        go(line.at[second_at], line.at[second_at], on_second(by), shard) for by in (2, 1, 3)
    ]
    small_back.wait_recv()
    small_ref[s_mine, :] = s_out[2].astype(F32)
    small_ref[s_others, :] = s_other[...].astype(F32)
    for copy in back_second:
        copy.wait_recv()
    plane[first] = line[...].reshape(wide, line.shape[-1])
    back_first = [
        go(plane.at[first], plane.at[first], on_first(by), shard) for by in (2, 1, 3)
    ]
    own_back = go(plane.at[first], gathered.at[first], sibling, shard)
    for copy in grads_first:
        copy.wait_recv()
    gw1_ref[...] = part1[2].astype(F32) + came1[0].astype(F32) + came1[1].astype(F32)
    hands = []
    for copy, by in zip(back_first, (2, 1, 3)):
        copy.wait_recv()
        came = turn(first, SIDE - by)
        hands.append(go(plane.at[came], gathered.at[came], sibling, shard))

    def put(source, start):
        for third in range(3):
            columns = pl.ds(pl.multiple_of(third * width + start, LANES), block)
            gwq_ref[:, columns] = source[third].astype(F32)
        gwp_ref[:, pl.ds(pl.multiple_of(start, LANES), block)] = source[3].astype(F32)

    put(plane, core * block)
    own_back.wait_recv()
    for copy in hands:
        copy.wait_recv()
    put(gathered, (1 - core) * block)
    for copy in grads_second:
        copy.wait_recv()
    gw2_ref[...] = part2[2].astype(F32) + came2[0].astype(F32) + came2[1].astype(F32)
    for copy in started:
        copy.wait_send()


def tail(operands, expert_operands, collective_id):
    tokens, width = operands[0].shape
    columns = width // 2
    rows = width // SIDE
    hidden = expert_operands[0].shape[1]
    quarter, part = rows // 4, rows // 2
    vmem, semaphores = pltpu.VMEM, pltpu.SemaphoreType.DMA
    anywhere = pl.BlockSpec(memory_space=pl.ANY)
    everything = (*operands, *expert_operands)
    return pl.pallas_call(
        tail_kernel,
        out_shape=(
            jax.ShapeDtypeStruct((tokens, width), BF16),
            jax.ShapeDtypeStruct((tokens, width), F32),
            jax.ShapeDtypeStruct((rows, 3 * width), F32),
            jax.ShapeDtypeStruct((rows, width), F32),
            jax.ShapeDtypeStruct((rows, LANES), F32),
            jax.ShapeDtypeStruct((rows, hidden), F32),
            jax.ShapeDtypeStruct((hidden // SIDE, width), F32),
        ),
        in_specs=[anywhere] * len(everything),
        out_specs=[pl.BlockSpec(memory_space=vmem)] * 7,
        scratch_shapes=[vmem(array.shape, array.dtype) for array in operands] + [
            vmem((2, rows // 2, hidden), BF16),
            vmem((2, hidden // 8, width), BF16),
            vmem((3, rows, hidden), BF16),
            vmem((3, hidden // SIDE, width), BF16),
            vmem((2, rows, hidden), BF16),
            vmem((2, hidden // SIDE, width), BF16),
            vmem((tokens, width), BF16),
            vmem((tokens, 3 * width), BF16),
            vmem((tokens, width), BF16),
            vmem((SIDE, width, columns), BF16),
            vmem((SIDE, width, columns), BF16),
            vmem((SIDE, width, columns), BF16),
            vmem((SIDE, width, columns), BF16),
            vmem((2, 2 * rows, columns), BF16),
            vmem((2, width, columns), BF16),
            vmem((SIDE, SIDE, quarter, columns), BF16),
            vmem((3, SIDE, quarter, columns), BF16),
            vmem((3, quarter, columns), BF16),
            vmem((SIDE, quarter, columns), BF16),
            vmem((SIDE, quarter, columns), BF16),
            vmem((SIDE, rows, columns), BF16),
            vmem((SIDE, rows, columns), BF16),
            vmem((SIDE, rows, LANES), BF16),
            vmem((SIDE, rows, LANES), BF16),
            vmem((SIDE, rows, LANES), BF16),
            vmem((9, part, LANES), BF16),
            vmem((3, part, LANES), BF16),
            vmem((part, LANES), BF16),
            semaphores((24,)),
            semaphores((24,)),
            semaphores((24,)),
            semaphores((11,)),
            semaphores((11,)),
            semaphores((6,)),
            semaphores((6,)),
        ],
        compiler_params=pltpu.CompilerParams(
            vmem_limit_bytes=58 * MIB, collective_id=collective_id, has_side_effects=True
        ),
        cost_estimate=pl.CostEstimate(
            flops=2 * tokens * width * 14 * width, bytes_accessed=48 * MIB, transcendentals=tokens * tokens * 12
        ),
        name="backward_and_sums",
    )(*everything)


def on_device(
    tokens, ln1_gain, ln1_bias, w_qkv, w_proj, ln2_gain, ln2_bias, w_router,
    expert_in, expert_out, routes, cotangent,
):
    rows, width = tokens.shape
    experts = w_router.shape[1]
    capacity = (5 * rows // 2 + 8 * experts - 1) // (8 * experts) * 8
    routes, wq, wp, ws, ln, *kept, arrived = forward(
        tokens, cotangent, routes.T, w_qkv, w_proj, w_router.T, (ln1_gain, ln1_bias, ln2_gain, ln2_bias),
        experts, capacity,
    )
    w1, w2 = expert_in[0], expert_out[0]
    active, d_hidden, g_first, g_second = expert_grads(arrived, w1, w2)
    y, dz, side_first, side_second = expert_rows(active, d_hidden, w1, w2, g_first, g_second, capacity, 2)
    mixed, grad_tokens, gwq, gwp, gws, g_first, g_second = tail(
        (tokens, cotangent, routes, wq, wp, ws, ln, *kept, y, dz), (g_first, g_second, side_first, side_second), 3
    )
    return (
        mixed,
        grad_tokens,
        gws[:, experts],
        gws[:, experts + 1],
        gwq,
        gwp,
        gws[:, experts + 2],
        gws[:, experts + 3],
        gws[:, :experts],
        g_first[None],
        g_second[None],
    )


def solution(mesh):
    in_specs = (
        P(("expert", "wshard"), None),
        P("wshard"),
        P("wshard"),
        P("wshard", None),
        P("wshard", None),
        P("wshard"),
        P("wshard"),
        P("wshard", None),
        P("expert", None, None),
        P("expert", None, None),
        P(("expert", "wshard"), None),
        P(("expert", "wshard"), None),
    )
    out_specs = (
        P(("expert", "wshard"), None),
        P(("expert", "wshard"), None),
        P("wshard"),
        P("wshard"),
        P("wshard", None),
        P("wshard", None),
        P("wshard"),
        P("wshard"),
        P("wshard", None),
        P("expert", "wshard", None),
        P("expert", "wshard", None),
    )
    return jax.shard_map(
        on_device, mesh=mesh, in_specs=in_specs, out_specs=out_specs, check_vma=False
    )
```

```python
import functools

import jax
import jax.numpy as jnp
from jax import lax
from jax.experimental import pallas as pl
from jax.experimental.pallas import tpu as pltpu
from jax.sharding import PartitionSpec as P

HEAD_DIM = 64
EPSILON = 1e-06
F32 = jnp.float32
BF16 = jnp.bfloat16
LANES = 128
MIB = 1 << 20


def mm(left, right, left_dim=1, right_dim=0):
    return lax.dot_general(
        left, right, (((left_dim,), (right_dim,)), ((), ())), preferred_element_type=F32
    )


def normalize(values):
    centered = values - jnp.mean(values, -1, keepdims=True)
    inverse = lax.rsqrt(jnp.mean(centered * centered, -1, keepdims=True) + EPSILON)
    return centered * inverse, inverse


def norm_back(upstream, normed, inverse, gain):
    scaled = upstream * gain
    return inverse * (
        scaled
        - jnp.mean(scaled, -1, keepdims=True)
        - normed * jnp.mean(scaled * normed, -1, keepdims=True)
    )


def lane_iota(rows, columns=LANES):
    return lax.broadcasted_iota(jnp.int32, (rows, columns), 1)


MESH = pl.DeviceIdType.MESH
SIDE = 4


def remote(source, target, send, receive, expert, shard):
    return pltpu.make_async_remote_copy(
        src_ref=source, dst_ref=target, send_sem=send, recv_sem=receive,
        device_id=(expert, shard), device_id_type=MESH,
    )


def greet(devices):
    barrier = pltpu.get_barrier_semaphore()
    for expert, shard in devices:
        pl.semaphore_signal(barrier, inc=1, device_id=(expert, shard), device_id_type=MESH)
    pl.semaphore_wait(barrier, len(devices))


class RowGather:
    def __init__(self, shard_ref, full_ref, send, receive, expert, shard):
        self.rows, columns = shard_ref.shape
        self.shard_ref, self.full_ref = shard_ref, full_ref
        self.send, self.receive = send, receive
        self.expert, self.shard = expert, shard
        core = lax.rem(expert, 2)
        self.sibling = expert + 1 - 2 * core
        self.after, self.before = lax.rem(shard + 1, SIDE), lax.rem(shard + 3, SIDE)
        self.across = lax.rem(shard + 2, SIDE)
        half = columns // 2
        self.columns = pl.ds(pl.multiple_of(core * half, LANES), half)

    def at(self, shard, start, count, columns):
        place = pl.multiple_of(shard * self.rows + start, 16)
        return self.full_ref.at[pl.ds(place, count), columns]

    def ring(self, number, source, target, shard):
        return remote(
            source, target, self.send.at[number], self.receive.at[number], self.expert, shard
        )

    def first(self):
        target = self.at(self.shard, 0, self.rows, self.columns)
        source = self.shard_ref.at[:, self.columns]
        self.to_after = self.ring(0, source, target, self.after)
        self.to_before = self.ring(1, source, target, self.before)
        self.own = pltpu.make_async_copy(
            self.shard_ref, self.at(self.shard, 0, self.rows, pl.ds(0, self.shard_ref.shape[1])),
            self.send.at[8],
        )
        self.to_after.start()
        self.to_before.start()
        self.own.start()

    def hand(self, number, shard, start, count):
        block = self.at(shard, start, count, self.columns)
        copy = remote(
            block, block, self.send.at[number], self.receive.at[number], self.sibling, self.shard
        )
        copy.start()
        return copy

    def second(self):
        half = self.rows // 2
        self.to_after.wait_recv()
        top = self.at(self.before, 0, half, self.columns)
        self.pass_after = self.ring(2, top, top, self.after)
        self.pass_after.start()
        self.to_before.wait_recv()
        bottom = self.at(self.after, half, half, self.columns)
        self.pass_before = self.ring(3, bottom, bottom, self.before)
        self.pass_before.start()
        self.handed = [
            self.hand(4, self.before, 0, self.rows),
            self.hand(5, self.after, 0, self.rows),
        ]

    def third(self):
        half = self.rows // 2
        self.pass_after.wait_recv()
        self.handed.append(self.hand(6, self.across, 0, half))
        self.pass_before.wait_recv()
        self.handed.append(self.hand(7, self.across, half, half))

    def finish(self):
        self.own.wait()
        for copy in self.handed:
            copy.wait_recv()

    def drain(self):
        for copy in (self.to_after, self.to_before, self.pass_after, self.pass_before, *self.handed):
            copy.wait_send()


def exchange_peers(expert):
    return [
        lax.rem(expert // 8 + dz, SIDE) * 8 + lax.rem(lax.rem(expert // 2, SIDE) + dx, SIDE) * 2
        + lax.rem(expert + dc, 2)
        for dz, dx, dc in exchange_order()
    ]


def exchange_order():
    reach = [0, 1, 2, 1]
    steps = [(dz, dx, dc) for dz in range(SIDE) for dx in range(SIDE) for dc in range(2)]
    return sorted(steps[1:], key=lambda step: -reach[step[0]] - reach[step[1]])


def exchange_start(source_ref, target_ref, send, receive, local, expert, shard, capacity):
    own = pl.ds(pl.multiple_of(expert * capacity, 16), capacity)
    copies = []
    for number, peer in enumerate(exchange_peers(expert)):
        block = pl.ds(pl.multiple_of(peer * capacity, 16), capacity)
        copy = remote(
            source_ref.at[block, :], target_ref.at[own, :], send.at[number], receive.at[number], peer, shard
        )
        copy.start()
        copies.append(copy)
    keep = pltpu.make_async_copy(source_ref.at[own, :], target_ref.at[own, :], local)
    keep.start()
    return copies, keep


def exchange_wait(copies, keep):
    keep.wait()
    for copy in copies:
        copy.wait()


def main_kernel(
    experts, capacity, x_in, g_in, routes_ref, wq_shard, wp_shard, router_ref, gain1_ref, bias1_ref, gain2_ref, bias2_ref,
    w1_in, w2_in,
    routes_out, wq_out, wp_out, ws_ref, ln_ref, qkv_ref, lse_ref, o_ref, x2_ref, gates_ref, pick0_ref, pick1_ref,
    y_out, dz_out, gw1_out, gw2_out, side1_out, side2_out,
    x_ref, g_ref, own_ref, small_ref, wq_ref, wp_ref, send_z, send_dy, z_ref, dy_ref,
    w1_ref, w2_ref, a_ref, slope_ref, gw1_ref, gw2_ref, rows_ref, y_ref, dz_ref,
    sends, receives, s_send, s_receive, ex_send, ex_receive, half_send, half_receive, local,
):
    rows, width = x_ref.shape
    load_x = pltpu.make_async_copy(x_in, x_ref, local.at[3])
    load_x.start()
    load_g = pltpu.make_async_copy(g_in, g_ref, local.at[4])
    load_g.start()
    expert, shard = lax.axis_index("expert"), lax.axis_index("wshard")
    core = lax.rem(expert, 2)
    pad = jnp.zeros((own_ref.shape[0] - experts - 4, width // SIDE), F32)
    mini = [router_ref[...].astype(F32)] + [
        ref[...].astype(F32).reshape(1, width // SIDE) for ref in (gain1_ref, bias1_ref, gain2_ref, bias2_ref)
    ]
    own_ref[:, : width // SIDE] = jnp.concatenate(mini + [pad], 0).astype(BF16)
    own_ref[:, width // SIDE :] = jnp.zeros((own_ref.shape[0], own_ref.shape[1] - width // SIDE), BF16)
    greet(
        [(expert, lax.rem(shard + by, SIDE)) for by in (1, 2, 3)]
        + [(peer, shard) for peer in exchange_peers(expert)]
    )
    small = []
    for by in (1, 2, 3):
        copy = remote(
            own_ref, small_ref.at[by - 1], s_send.at[by - 1], s_receive.at[by - 1], expert, lax.rem(shard + by, SIDE)
        )
        copy.start()
        small.append(copy)
    first_w, second_w = [
        RowGather(shard_ref, full_ref, sends.at[number], receives.at[number], expert, shard)
        for number, (shard_ref, full_ref) in enumerate(((wq_shard, wq_ref), (wp_shard, wp_ref)))
    ]
    first_w.first()
    load_w1 = pltpu.make_async_copy(w1_in, w1_ref, local.at[5])
    load_w1.start()
    load_w2 = pltpu.make_async_copy(w2_in, w2_ref, local.at[6])
    load_w2.start()
    load_x.wait()
    x = x_ref[...].astype(F32)
    normed, _ = normalize(x)
    first_w.second()
    second_w.first()
    for copy in small:
        copy.wait_recv()
    pieces = []
    for place in range(SIDE):
        piece = own_ref[...].astype(F32)
        for by in (1, 2, 3):
            piece = jnp.where(lax.rem(shard + SIDE - by, SIDE) == place, small_ref[by - 1].astype(F32), piece)
        pieces.append(piece[:, : width // SIDE])
    lane = lane_iota(rows)
    both = jnp.concatenate(pieces, 1)
    vectors = both[experts : experts + 8, :]
    ln_ref[...] = vectors
    ws_ref[...] = jnp.concatenate([both[:experts], jnp.zeros((LANES - experts, width), F32)], 0).astype(BF16)
    h1 = (normed * vectors[0:1, :] + vectors[1:2, :]).astype(BF16)
    first_w.third()
    second_w.second()
    first_w.finish()
    keep_first = pltpu.make_async_copy(wq_ref, wq_out, local.at[1])
    keep_first.start()
    qkv_ref[...] = mm(h1, wq_ref[...]).astype(BF16)
    scale = HEAD_DIM ** (-0.5)
    lse_all = jnp.zeros((rows, LANES), F32)
    for pair in range(width // LANES):
        if pair == 2:
            second_w.third()
        at = pair * LANES
        q = qkv_ref[:, at : at + LANES]
        k = qkv_ref[:, width + at : width + at + LANES]
        v = qkv_ref[:, 2 * width + at : 2 * width + at + LANES]
        halves = []
        for half in range(2):
            own = (lane // HEAD_DIM) == half
            s = mm(jnp.where(own, q, jnp.zeros_like(q)), k, 1, 1) * scale
            top = jnp.max(s, -1, keepdims=True)
            e = jnp.exp(s - top)
            total = jnp.sum(e, -1, keepdims=True)
            lse_all = jnp.where(lane == 2 * pair + half, top + jnp.log(total), lse_all)
            halves.append(mm((e / total).astype(BF16), v))
        o_ref[:, at : at + LANES] = jnp.where(lane < HEAD_DIM, halves[0], halves[1]).astype(BF16)
    lse_ref[...] = lse_all
    second_w.finish()
    keep_second = pltpu.make_async_copy(wp_ref, wp_out, local.at[2])
    keep_second.start()
    x2 = x + mm(o_ref[...], wp_ref[...])
    x2_ref[...] = x2
    normed2, _ = normalize(x2)
    h2 = (normed2 * vectors[2:3, :] + vectors[3:4, :]).astype(BF16)
    logits = jnp.where(lane < experts, mm(h2, ws_ref[...], 1, 1), -jnp.inf)
    e = jnp.exp(logits - jnp.max(logits, -1, keepdims=True))
    gates = e / jnp.sum(e, -1, keepdims=True)
    gates_ref[...] = gates
    diagonal = lax.broadcasted_iota(jnp.int32, (rows, rows), 0) == lane_iota(rows, rows)
    routes = mm(diagonal.astype(F32).astype(BF16), routes_ref[...].astype(F32).astype(BF16), 1, 1)
    lane_number = lane.astype(F32)
    match = [lane_number == routes[:, k : k + 1] for k in range(2)]
    routes_out[...] = jnp.where(lane == 0, routes[:, 0:1], routes[:, 1:2])
    hits = (match[0] | match[1]).astype(F32).astype(BF16)
    earlier = lax.broadcasted_iota(jnp.int32, (rows, rows), 0) > lane_iota(rows, rows)
    before = mm(earlier.astype(F32).astype(BF16), hits)
    slots = lane_iota(rows, experts * capacity).astype(F32)
    load_g.wait()
    g = g_ref[...].astype(F32)
    picks, grads = [], []
    for k in range(2):
        slot = jnp.sum(jnp.where(match[k], before, 0.0), -1, keepdims=True)
        place = routes[:, k : k + 1] * capacity + slot
        picks.append((slots == place).astype(F32).astype(BF16))
        chosen = jnp.sum(jnp.where(match[k], gates, 0.0), -1, keepdims=True)
        grads.append((chosen * g).astype(BF16))
    pick0_ref[...] = picks[0]
    pick1_ref[...] = picks[1]
    moves = []

    def move(source, target):
        number = len(moves)
        moves.append(
            exchange_start(
                source, target, ex_send.at[number], ex_receive.at[number], local.at[7 + number], expert, shard, capacity
            )
        )
        return moves[-1]

    send_z[...] = mm(picks[0] + picks[1], h2, 0, 0).astype(BF16)
    z_move = move(send_z, z_ref)
    send_dy[...] = (mm(picks[0], grads[0], 0, 0) + mm(picks[1], grads[1], 0, 0)).astype(BF16)
    dy_move = move(send_dy, dy_ref)
    for copy in small:
        copy.wait_send()
    for gather in (first_w, second_w):
        gather.drain()
    keep_first.wait()
    keep_second.wait()
    load_w1.wait()
    load_w2.wait()
    block = width
    blocks = w1_ref.shape[1] // block
    exchange_wait(*z_move)

    def columns(number):
        return pl.ds(pl.multiple_of(number * block, block), block)

    rows_ref[...] = jnp.zeros_like(rows_ref)

    def activate(number, _):
        at = columns(number)
        u = mm(z_ref[...], w1_ref[:, at])
        phi = 0.5 * (1.0 + lax.erf(u * (2.0**-0.5)))
        density = jnp.exp(-0.5 * u * u) * 0.3989422804014327
        slope_ref[:, at] = phi + u * density
        a = (u * phi).astype(BF16)
        a_ref[:, at] = a
        rows_ref[...] += mm(a, w2_ref[at, :])
        return 0

    lax.fori_loop(0, blocks, activate, 0)
    y_ref[...] = rows_ref[...].astype(BF16)
    move(y_ref, y_out)
    exchange_wait(*dy_move)

    after, before, across = [lax.rem(shard + by, SIDE) for by in (1, 3, 2)]
    halves = []

    def pass_halves(place, source, target):
        rows_each = source.shape[0] // SIDE
        for number, peer in enumerate((after, before)):
            start = pl.multiple_of(across * rows_each + number * (rows_each // 2), 16)
            copy = remote(
                source.at[pl.ds(start, rows_each // 2), :], target.at[number],
                half_send.at[place, number], half_receive.at[place, number], expert, peer,
            )
            copy.start()
            halves.append(copy)

    def out_grads(number):
        at = columns(number)
        gw2_ref[at, :] = mm(a_ref[:, at], dy_ref[...], 0, 0).astype(BF16)

    out_grads(across)
    pass_halves(0, gw2_ref, side2_out)

    def other_grads(step, _):
        out_grads(lax.rem(across + step, SIDE))
        return 0

    lax.fori_loop(1, blocks, other_grads, 0)
    keep_gw2 = pltpu.make_async_copy(gw2_ref, gw2_out, local.at[11])
    keep_gw2.start()
    rows_ref[...] = jnp.zeros_like(rows_ref)

    def in_grads(number, _):
        at = columns(number)
        da = mm(dy_ref[...], w2_ref[at, :], 1, 1)
        du = (da * slope_ref[:, at]).astype(BF16)
        rows_ref[...] += mm(du, w1_ref[:, at], 1, 1)
        gw1_ref[:, at] = mm(z_ref[...], du, 0, 0).astype(BF16)
        return 0

    lax.fori_loop(0, blocks, in_grads, 0)
    dz_ref[...] = rows_ref[...].astype(BF16)
    move(dz_ref, dz_out)
    pass_halves(1, gw1_ref, side1_out)
    keep_gw1 = pltpu.make_async_copy(gw1_ref, gw1_out, local.at[12])
    keep_gw1.start()
    keep_gw2.wait()
    keep_gw1.wait()
    for copies, keep in moves[2:]:
        exchange_wait(copies, keep)
    for copy in halves:
        copy.wait()


def forward(tokens, cotangent, routes, wq, wp, router, vectors, w1, w2, experts, capacity):
    rows, width = tokens.shape
    hidden = w1.shape[1]
    slots = experts * capacity
    vmem, anywhere = pl.BlockSpec(memory_space=pltpu.VMEM), pl.BlockSpec(memory_space=pl.ANY)
    return pl.pallas_call(
        functools.partial(main_kernel, experts, capacity),
        out_shape=(
            jax.ShapeDtypeStruct((rows, LANES), F32),
            jax.ShapeDtypeStruct((width, 3 * width), BF16),
            jax.ShapeDtypeStruct((width, width), BF16),
            jax.ShapeDtypeStruct((LANES, width), BF16),
            jax.ShapeDtypeStruct((8, width), F32),
            jax.ShapeDtypeStruct((rows, 3 * width), BF16),
            jax.ShapeDtypeStruct((rows, LANES), F32),
            jax.ShapeDtypeStruct((rows, width), BF16),
            jax.ShapeDtypeStruct((rows, width), F32),
            jax.ShapeDtypeStruct((rows, LANES), F32),
            jax.ShapeDtypeStruct((rows, slots), BF16),
            jax.ShapeDtypeStruct((rows, slots), BF16),
            jax.ShapeDtypeStruct((slots, width), BF16),
            jax.ShapeDtypeStruct((slots, width), BF16),
            jax.ShapeDtypeStruct((width, hidden), BF16),
            jax.ShapeDtypeStruct((hidden, width), BF16),
            jax.ShapeDtypeStruct((2, width // 8, hidden), BF16),
            jax.ShapeDtypeStruct((2, hidden // 8, width), BF16),
        ),
        in_specs=[anywhere] * 2 + [vmem] + [anywhere] * 2 + [vmem] * 5 + [anywhere] * 2,
        out_specs=[vmem] + [anywhere] * 2 + [vmem] * 9 + [anywhere] * 6,
        scratch_shapes=[
            pltpu.VMEM((rows, width), BF16),
            pltpu.VMEM((rows, width), BF16),
            pltpu.VMEM((48, 256), BF16),
            pltpu.VMEM((3, 48, 256), BF16),
            pltpu.VMEM((width, 3 * width), BF16),
            pltpu.VMEM((width, width), BF16),
            *[pltpu.VMEM((slots, width), BF16)] * 4,
            pltpu.VMEM((width, hidden), BF16),
            pltpu.VMEM((hidden, width), BF16),
            pltpu.VMEM((slots, hidden), BF16),
            pltpu.VMEM((slots, hidden), F32),
            pltpu.VMEM((width, hidden), BF16),
            pltpu.VMEM((hidden, width), BF16),
            pltpu.VMEM((slots, width), F32),
            pltpu.VMEM((slots, width), BF16),
            pltpu.VMEM((slots, width), BF16),
            pltpu.SemaphoreType.DMA((2, 9)),
            pltpu.SemaphoreType.DMA((2, 8)),
            pltpu.SemaphoreType.DMA((3,)),
            pltpu.SemaphoreType.DMA((3,)),
            pltpu.SemaphoreType.DMA((4, 31)),
            pltpu.SemaphoreType.DMA((4, 31)),
            pltpu.SemaphoreType.DMA((2, 2)),
            pltpu.SemaphoreType.DMA((2, 2)),
            pltpu.SemaphoreType.DMA((13,)),
        ],
        compiler_params=pltpu.CompilerParams(
            vmem_limit_bytes=58 * MIB, collective_id=1, has_side_effects=True
        ),
        cost_estimate=pl.CostEstimate(
            flops=12 * slots * width * hidden, bytes_accessed=48 * MIB, transcendentals=2 * slots * hidden
        ),
        name="forward_and_experts",
    )(tokens, cotangent, routes, wq, wp, router, *vectors, w1, w2)


def tail_kernel(
    x_in, g_in, routes_in, wq_in, wp_in, ws_in, ln_in, qkv_in, lse_in, o_in, x2_in, gates_in, pick0_in, pick1_in,
    y_in, dz_in, gw1_in, gw2_in, side1_in, side2_in,
    mixed_ref, dx_ref, gwq_ref, gwp_ref, small_ref, gw1_ref, gw2_ref,
    x_ref, g_ref, routes_ref, wq_ref, wp_ref, ws_ref, ln_ref, qkv_ref, lse_ref, o_ref, x2_ref, gates_ref,
    pick0_ref, pick1_ref, y_ref, dz_ref, side1, side2, part1, part2, came1, came2, do_ref, dqkv_ref, h1_ref,
    theirs, ours, paired, summed, side, first_in, second, second_in, third_in, piece, line, plane, gathered,
    s_ref, s_pair, s_sum, s_in, s_out, s_other,
    loads, send, receive, s_send, s_receive, g_send, g_receive,
):
    expert, shard = lax.axis_index("expert"), lax.axis_index("wshard")
    core = lax.rem(expert, 2)
    x_at, z_at = lax.rem(expert // 2, SIDE), expert // 8
    sibling = expert + 1 - 2 * core
    first, second_at = x_at * (1 - core) + z_at * core, z_at * (1 - core) + x_at * core
    first_step, second_step = 2 + 6 * core, 8 - 6 * core

    def turn(place, by):
        return lax.rem(place + by, SIDE)

    def on_first(by):
        return expert + (turn(first, by) - first) * first_step

    def on_second(by):
        return expert + (turn(second_at, by) - second_at) * second_step

    load_count = [0]

    def load(source, target):
        copy = pltpu.make_async_copy(source, target, loads.at[load_count[0]])
        load_count[0] += 1
        copy.start()
        return copy

    rows1, rows2 = part1.shape[1], part2.shape[1]

    def shard_rows(ref, by, rows):
        return ref.at[pl.ds(pl.multiple_of(turn(shard, by) * rows, 16), rows), :]

    load_first = [load(side1_in, side1)] + [
        load(shard_rows(gw1_in, by, rows1), part1.at[number]) for number, by in enumerate((1, 3))
    ]
    load_out = [
        load(*pair) for pair in (
            (y_in, y_ref), (pick0_in, pick0_ref), (pick1_in, pick1_ref), (x2_in, x2_ref), (g_in, g_ref),
            (gates_in, gates_ref), (routes_in, routes_ref),
        )
    ]
    load_gates = [
        load(*pair) for pair in (
            (dz_in, dz_ref), (ws_in, ws_ref), (ln_in, ln_ref), (wp_in, wp_ref), (o_in, o_ref), (x_in, x_ref),
        )
    ]
    load_heads = [load(qkv_in, qkv_ref), load(lse_in, lse_ref)]
    load_second = [load(side2_in, side2)] + [
        load(shard_rows(gw2_in, by, rows2), part2.at[number]) for number, by in enumerate((1, 3))
    ]
    load_last = [load(wq_in, wq_ref)]
    load_own = [
        load(shard_rows(gw1_in, 0, rows1), part1.at[2]), load(shard_rows(gw2_in, 0, rows2), part2.at[2])
    ]

    greet(
        [(sibling, shard)]
        + [(on_first(by), shard) for by in (1, 2, 3)]
        + [(on_second(by), shard) for by in (1, 2, 3)]
        + [(expert, turn(shard, by)) for by in (1, 2, 3)]
    )
    started = []
    counts = {}

    def go(source, target, to_expert, to_shard, sends=send, receives=receive, kind="wide"):
        number = counts.get(kind, 0)
        counts[kind] = number + 1
        copy = remote(source, target, sends.at[number], receives.at[number], to_expert, to_shard)
        copy.start()
        started.append(copy)
        return copy

    def go_small(*args):
        return go(*args, sends=s_send, receives=s_receive, kind="small")

    def add(left, right):
        return (left.astype(F32) + right.astype(F32)).astype(BF16)

    def join(part, came_half):
        half = part.shape[1] // 2
        part[0, :half] = add(part[0, :half], came_half[0])
        part[1, half:] = add(part[1, half:], came_half[1])

    def pass_on(part, came, start, count):
        at = pl.ds(start, count)
        return [
            go(
                part.at[number, at], came.at[number, at], expert, turn(shard, by), g_send, g_receive, "expert"
            )
            for number, by in enumerate((1, 3))
        ]

    for copy in load_first:
        copy.wait()
    join(part1, side1)
    grads_first = pass_on(part1, came1, 0, rows1)

    for copy in load_out:
        copy.wait()
    rows, width = x_ref.shape
    lane = lane_iota(rows)
    g = g_ref[...].astype(F32)
    x2 = x2_ref[...]
    gates = gates_ref[...]
    routes = routes_ref[...]
    out = x2
    dgates = jnp.zeros((rows, LANES), F32)
    for k, pick_ref in enumerate((pick0_ref, pick1_ref)):
        match = lane.astype(F32) == routes[:, k : k + 1]
        picked = mm(pick_ref[...], y_ref[...])
        chosen = jnp.sum(jnp.where(match, gates, 0.0), -1, keepdims=True)
        out = out + chosen * picked
        dgates = jnp.where(match, jnp.sum(g * picked, -1, keepdims=True), dgates)
    mixed_ref[...] = out.astype(BF16)
    dl = (gates * (dgates - jnp.sum(gates * dgates, -1, keepdims=True))).astype(BF16)
    for copy in load_gates:
        copy.wait()
    dh2 = mm(pick0_ref[...] + pick1_ref[...], dz_ref[...]) + mm(dl, ws_ref[...])
    gain1, bias1 = ln_ref[0:1, :], ln_ref[1:2, :]
    gain2, bias2 = ln_ref[2:3, :], ln_ref[3:4, :]
    n2, r2 = normalize(x2)
    h2 = (n2 * gain2 + bias2).astype(BF16)
    g_router = mm(dl, h2, 0, 0)
    g_gain2 = jnp.sum(dh2 * n2, 0, keepdims=True)
    g_bias2 = jnp.sum(dh2, 0, keepdims=True)
    dx2 = g + norm_back(dh2, n2, r2, gain2)
    dx_ref[...] = dx2
    dx2b = dx2.astype(BF16)
    do_ref[...] = dx2b
    block = width // 2
    mine = pl.ds(pl.multiple_of(core * block, LANES), block)
    others = pl.ds(pl.multiple_of((1 - core) * block, LANES), block)
    theirs[3] = mm(o_ref[...], do_ref[:, others], 0, 0).astype(BF16)
    pair = [None] * SIDE
    pair[3] = go(theirs.at[3], paired.at[3], sibling, shard)
    ours[3] = mm(o_ref[...], do_ref[:, mine], 0, 0).astype(BF16)
    do_ref[...] = mm(dx2b, wp_ref[...], 1, 1).astype(BF16)
    n1, r1 = normalize(x_ref[...].astype(F32))
    h1_ref[...] = (n1 * gain1 + bias1).astype(BF16)
    for copy in load_second:
        copy.wait()
    join(part2, side2)
    grads_second = pass_on(part2, came2, 0, rows2 // 2)
    for copy in load_heads:
        copy.wait()
    scale = HEAD_DIM ** (-0.5)
    low = lane < HEAD_DIM

    def heads(start):
        for step in range(block // LANES):
            at = [
                pl.ds(pl.multiple_of(third * width + start + step * LANES, LANES), LANES) for third in range(3)
            ]
            q, k, v = qkv_ref[:, at[0]], qkv_ref[:, at[1]], qkv_ref[:, at[2]]
            do = do_ref[:, at[0]]
            parts = []
            for half in range(2):
                own = (lane // HEAD_DIM) == half
                head = start // HEAD_DIM + 2 * step + half
                lse = jnp.sum(jnp.where(lane == head, lse_ref[...], 0.0), -1, keepdims=True)
                s = mm(jnp.where(own, q, jnp.zeros_like(q)), k, 1, 1) * scale
                p = jnp.exp(s - lse)
                dp = mm(jnp.where(own, do, jnp.zeros_like(do)), v, 1, 1)
                ds = (p * (dp - jnp.sum(dp * p, -1, keepdims=True))).astype(BF16)
                parts.append((mm(ds, k) * scale, mm(ds, q, 0, 0) * scale, mm(p.astype(BF16), do, 0, 0)))
            for third, (left, right) in enumerate(zip(*parts)):
                dqkv_ref[:, at[third]] = jnp.where(low, left, right).astype(BF16)

    def weight_grads(target, start):
        for third in range(3):
            columns = pl.ds(pl.multiple_of(third * width + start, LANES), block)
            target[third] = mm(h1_ref[...], dqkv_ref[:, columns], 0, 0).astype(BF16)

    heads((1 - core) * block)
    weight_grads(theirs, (1 - core) * block)
    for third in range(3):
        pair[third] = go(theirs.at[third], paired.at[third], sibling, shard)
    heads(core * block)
    weight_grads(ours, core * block)
    for copy in pair:
        copy.wait_recv()

    order = (2, 1, 3, 0)

    def add_pair(number):
        chunk = turn(first, order[number])
        summed[number] = add(ours[chunk], paired[chunk])

    wide = s_ref.shape[1]
    part, quarter, half = wide // 2, wide // 4, 2 * wide
    add_pair(0)
    relay_up = go(summed.at[0, pl.ds(0, half)], side.at[0], on_first(1), shard)
    relay_down = go(summed.at[0, pl.ds(half, half)], side.at[1], on_first(3), shard)
    add_pair(1)
    add_pair(2)

    for copy in load_last:
        copy.wait()
    dh1 = mm(dqkv_ref[...], wq_ref[...], 1, 1)
    g_gain1 = jnp.sum(dh1 * n1, 0, keepdims=True)
    g_bias1 = jnp.sum(dh1, 0, keepdims=True)
    row = lax.broadcasted_iota(jnp.int32, (LANES, width), 0)
    vectors = g_router
    for place, vector in enumerate((g_gain1, g_bias1, g_gain2, g_bias2)):
        vectors = jnp.where(row == 32 + place, vector, vectors)
    s_ref[...] = vectors.T.astype(BF16).reshape(s_ref.shape)
    small_pair = go_small(s_ref, s_pair, sibling, shard)

    relay_up.wait_recv()
    summed[1, :half] = add(summed[1, :half], side[0])
    up = go(summed.at[1], first_in.at[0], on_first(1), shard)
    relay_down.wait_recv()
    summed[2, half:] = add(summed[2, half:], side[1])
    down = go(summed.at[2], first_in.at[1], on_first(3), shard)
    add_pair(3)
    dx_ref[...] += norm_back(dh1, n1, r1, gain1)

    small_pair.wait_recv()
    s_sum[...] = add(s_ref[...], s_pair[...])
    s_mine = pl.ds(pl.multiple_of(core * part, 16), part)
    s_others = pl.ds(pl.multiple_of((1 - core) * part, 16), part)
    small_along = [
        go_small(s_sum.at[turn(shard, by), s_mine, :], s_in.at[by - 1], expert, turn(shard, by)) for by in (1, 2, 3)
    ]
    for copy in small_along:
        copy.wait_recv()

    def four(own, a, b, c):
        return own.astype(F32) + a.astype(F32) + b.astype(F32) + c.astype(F32)

    s_out[0] = four(s_sum[shard, s_mine, :], s_in[0], s_in[1], s_in[2]).astype(BF16)
    small_first = [go_small(s_out.at[0], s_in.at[2 + by], on_first(by), shard) for by in (1, 2, 3)]

    up.wait_recv()
    down.wait_recv()
    for own_shard in range(SIDE):
        for place in range(SIDE):
            at = pl.ds(own_shard * wide + place * quarter, quarter)
            second[place, own_shard] = (
                summed[3, at, :].astype(F32) + first_in[0, at, :].astype(F32) + first_in[1, at, :].astype(F32)
            ).astype(BF16)
    along_second = [
        go(second.at[turn(second_at, by)], second_in.at[by - 1], on_second(by), shard) for by in (2, 1, 3)
    ]
    for copy in small_first:
        copy.wait_recv()
    s_out[1] = four(s_out[0], s_in[3], s_in[4], s_in[5]).astype(BF16)
    small_second = [go_small(s_out.at[1], s_in.at[5 + by], on_second(by), shard) for by in (1, 2, 3)]
    for copy in along_second:
        copy.wait_recv()
    piece[...] = four(second[second_at], second_in[0], second_in[1], second_in[2]).astype(BF16)
    along_shard = [
        go(piece.at[turn(shard, by)], third_in.at[by - 1], expert, turn(shard, by)) for by in (2, 1, 3)
    ]
    grads_second += pass_on(part2, came2, rows2 // 2, rows2 // 2)
    for copy in small_second:
        copy.wait_recv()
    s_out[2] = four(s_out[1], s_in[6], s_in[7], s_in[8]).astype(BF16)
    small_back = go_small(s_out.at[2], s_other, sibling, shard)
    for copy in load_own:
        copy.wait()
    for copy in along_shard:
        copy.wait_recv()
    line[second_at] = four(piece[shard], third_in[0], third_in[1], third_in[2]).astype(BF16)
    back_second = [
        go(line.at[second_at], line.at[second_at], on_second(by), shard) for by in (2, 1, 3)
    ]
    small_back.wait_recv()
    small_ref[s_mine, :] = s_out[2].astype(F32)
    small_ref[s_others, :] = s_other[...].astype(F32)
    for copy in back_second:
        copy.wait_recv()
    plane[first] = line[...].reshape(wide, line.shape[-1])
    back_first = [
        go(plane.at[first], plane.at[first], on_first(by), shard) for by in (2, 1, 3)
    ]
    own_back = go(plane.at[first], gathered.at[first], sibling, shard)
    for copy in grads_first:
        copy.wait_recv()
    gw1_ref[...] = (part1[2].astype(F32) + came1[0].astype(F32) + came1[1].astype(F32)).astype(BF16)
    hands = []
    for copy, by in zip(back_first, (2, 1, 3)):
        copy.wait_recv()
        came = turn(first, SIDE - by)
        hands.append(go(plane.at[came], gathered.at[came], sibling, shard))

    def put(source, start):
        for third in range(3):
            columns = pl.ds(pl.multiple_of(third * width + start, LANES), block)
            gwq_ref[:, columns] = source[third]
        gwp_ref[:, pl.ds(pl.multiple_of(start, LANES), block)] = source[3]

    put(plane, core * block)
    own_back.wait_recv()
    for copy in hands:
        copy.wait_recv()
    put(gathered, (1 - core) * block)
    for copy in grads_second:
        copy.wait_recv()
    gw2_ref[...] = (part2[2].astype(F32) + came2[0].astype(F32) + came2[1].astype(F32)).astype(BF16)
    for copy in started:
        copy.wait_send()


def tail(operands, expert_operands, collective_id):
    tokens, width = operands[0].shape
    columns = width // 2
    rows = width // SIDE
    hidden = expert_operands[0].shape[1]
    quarter, part = rows // 4, rows // 2
    vmem, semaphores = pltpu.VMEM, pltpu.SemaphoreType.DMA
    anywhere = pl.BlockSpec(memory_space=pl.ANY)
    everything = (*operands, *expert_operands)
    return pl.pallas_call(
        tail_kernel,
        out_shape=(
            jax.ShapeDtypeStruct((tokens, width), BF16),
            jax.ShapeDtypeStruct((tokens, width), F32),
            jax.ShapeDtypeStruct((rows, 3 * width), BF16),
            jax.ShapeDtypeStruct((rows, width), BF16),
            jax.ShapeDtypeStruct((rows, LANES), F32),
            jax.ShapeDtypeStruct((rows, hidden), BF16),
            jax.ShapeDtypeStruct((hidden // SIDE, width), BF16),
        ),
        in_specs=[anywhere] * len(everything),
        out_specs=[pl.BlockSpec(memory_space=vmem)] * 7,
        scratch_shapes=[vmem(array.shape, array.dtype) for array in operands] + [
            vmem((2, rows // 2, hidden), BF16),
            vmem((2, hidden // 8, width), BF16),
            vmem((3, rows, hidden), BF16),
            vmem((3, hidden // SIDE, width), BF16),
            vmem((2, rows, hidden), BF16),
            vmem((2, hidden // SIDE, width), BF16),
            vmem((tokens, width), BF16),
            vmem((tokens, 3 * width), BF16),
            vmem((tokens, width), BF16),
            vmem((SIDE, width, columns), BF16),
            vmem((SIDE, width, columns), BF16),
            vmem((SIDE, width, columns), BF16),
            vmem((SIDE, width, columns), BF16),
            vmem((2, 2 * rows, columns), BF16),
            vmem((2, width, columns), BF16),
            vmem((SIDE, SIDE, quarter, columns), BF16),
            vmem((3, SIDE, quarter, columns), BF16),
            vmem((3, quarter, columns), BF16),
            vmem((SIDE, quarter, columns), BF16),
            vmem((SIDE, quarter, columns), BF16),
            vmem((SIDE, rows, columns), BF16),
            vmem((SIDE, rows, columns), BF16),
            vmem((SIDE, rows, LANES), BF16),
            vmem((SIDE, rows, LANES), BF16),
            vmem((SIDE, rows, LANES), BF16),
            vmem((9, part, LANES), BF16),
            vmem((3, part, LANES), BF16),
            vmem((part, LANES), BF16),
            semaphores((24,)),
            semaphores((24,)),
            semaphores((24,)),
            semaphores((11,)),
            semaphores((11,)),
            semaphores((6,)),
            semaphores((6,)),
        ],
        compiler_params=pltpu.CompilerParams(
            vmem_limit_bytes=58 * MIB, collective_id=collective_id, has_side_effects=True
        ),
        cost_estimate=pl.CostEstimate(
            flops=2 * tokens * width * 14 * width, bytes_accessed=48 * MIB, transcendentals=tokens * tokens * 12
        ),
        name="backward_and_sums",
    )(*everything)


def widen_kernel(experts, *refs):
    ins, outs, buffers, wide, loads, stores = refs[:7], refs[7:18], refs[18:25], refs[25:32], refs[32], refs[33]
    small_in, small_buffer = ins[4], buffers[4]
    incoming = []
    for number, (source, target) in enumerate(zip(ins, buffers)):
        copy = pltpu.make_async_copy(source, target, loads.at[number])
        copy.start()
        incoming.append(copy)
    outgoing = []

    def store(source, target):
        copy = pltpu.make_async_copy(source, target, stores.at[len(outgoing)])
        copy.start()
        outgoing.append(copy)

    places = (0, 1, 4, 5, None, 9, 10)
    for number in (0, 1, 5, 6, 2, 3):
        incoming[number].wait()
        if number < 2:
            store(buffers[number], outs[places[number]])
        else:
            wide[number][...] = buffers[number][...].astype(F32)
            target = outs[places[number]]
            store(wide[number], target.at[0] if number > 4 else target)
    incoming[4].wait()
    rows = small_buffer.shape[0]
    padded = jnp.concatenate([small_buffer[...], jnp.zeros((256 - rows, LANES), F32)], 0).T
    outs[8][...] = padded[:experts, :rows]
    for place, output in enumerate((2, 3, 6, 7)):
        outs[output][...] = padded[experts + place : experts + place + 1, :rows].reshape(rows)
    for copy in outgoing:
        copy.wait()


def widen(mixed, grad_tokens, gwq, gwp, small, gw1, gw2, experts):
    ins = (mixed, grad_tokens, gwq, gwp, small, gw1, gw2)
    rows = small.shape[0]
    anywhere, vmem = pl.BlockSpec(memory_space=pl.ANY), pl.BlockSpec(memory_space=pltpu.VMEM)
    shapes = [
        (mixed.shape, BF16), (grad_tokens.shape, F32), ((rows,), F32), ((rows,), F32), (gwq.shape, F32), (gwp.shape, F32),
        ((rows,), F32), ((rows,), F32), ((experts, rows), F32), ((1, *gw1.shape), F32), ((1, *gw2.shape), F32),
    ]
    return pl.pallas_call(
        functools.partial(widen_kernel, experts),
        out_shape=[jax.ShapeDtypeStruct(*shape) for shape in shapes],
        in_specs=[anywhere] * 7,
        out_specs=[anywhere if place in (0, 1, 4, 5, 9, 10) else vmem for place in range(11)],
        scratch_shapes=[pltpu.VMEM(array.shape, array.dtype) for array in ins]
        + [pltpu.VMEM(array.shape, F32) for array in ins]
        + [pltpu.SemaphoreType.DMA((7,)), pltpu.SemaphoreType.DMA((6,))],
        compiler_params=pltpu.CompilerParams(vmem_limit_bytes=58 * MIB),
        cost_estimate=pl.CostEstimate(flops=0, bytes_accessed=13 * MIB, transcendentals=0),
        name="widen_outputs",
    )(*ins)


def on_device(
    tokens, ln1_gain, ln1_bias, w_qkv, w_proj, ln2_gain, ln2_bias, w_router,
    expert_in, expert_out, routes, cotangent,
):
    rows = tokens.shape[0]
    experts = w_router.shape[1]
    capacity = (5 * rows // 2 + 8 * experts - 1) // (8 * experts) * 8
    *kept, g_first, g_second, side_first, side_second = forward(
        tokens, cotangent, routes.T, w_qkv, w_proj, w_router.T, (ln1_gain, ln1_bias, ln2_gain, ln2_bias),
        expert_in[0], expert_out[0], experts, capacity,
    )
    sums = tail((tokens, cotangent, *kept), (g_first, g_second, side_first, side_second), 3)
    outputs = list(widen(*sums, experts))
    outputs[8] = outputs[8].T
    return tuple(outputs)


def solution(mesh):
    in_specs = (
        P(("expert", "wshard"), None),
        P("wshard"),
        P("wshard"),
        P("wshard", None),
        P("wshard", None),
        P("wshard"),
        P("wshard"),
        P("wshard", None),
        P("expert", None, None),
        P("expert", None, None),
        P(("expert", "wshard"), None),
        P(("expert", "wshard"), None),
    )
    out_specs = (
        P(("expert", "wshard"), None),
        P(("expert", "wshard"), None),
        P("wshard"),
        P("wshard"),
        P("wshard", None),
        P("wshard", None),
        P("wshard"),
        P("wshard"),
        P("wshard", None),
        P("expert", "wshard", None),
        P("expert", "wshard", None),
    )
    return jax.shard_map(
        on_device, mesh=mesh, in_specs=in_specs, out_specs=out_specs, check_vma=False
    )
```

```python
import functools

import jax
import jax.numpy as jnp
from jax import lax
from jax.experimental import pallas as pl
from jax.experimental.pallas import tpu as pltpu
from jax.sharding import PartitionSpec as P

HEAD_DIM = 64
EPSILON = 1e-06
F32 = jnp.float32
BF16 = jnp.bfloat16
LANES = 128
MIB = 1 << 20


def mm(left, right, left_dim=1, right_dim=0):
    return lax.dot_general(
        left, right, (((left_dim,), (right_dim,)), ((), ())), preferred_element_type=F32
    )


def normalize(values):
    centered = values - jnp.mean(values, -1, keepdims=True)
    inverse = lax.rsqrt(jnp.mean(centered * centered, -1, keepdims=True) + EPSILON)
    return centered * inverse, inverse


def norm_back(upstream, normed, inverse, gain):
    scaled = upstream * gain
    return inverse * (
        scaled
        - jnp.mean(scaled, -1, keepdims=True)
        - normed * jnp.mean(scaled * normed, -1, keepdims=True)
    )


def lane_iota(rows, columns=LANES):
    return lax.broadcasted_iota(jnp.int32, (rows, columns), 1)


MESH = pl.DeviceIdType.MESH
SIDE = 4


def remote(source, target, send, receive, expert, shard):
    return pltpu.make_async_remote_copy(
        src_ref=source, dst_ref=target, send_sem=send, recv_sem=receive,
        device_id=(expert, shard), device_id_type=MESH,
    )


def greet(devices):
    barrier = pltpu.get_barrier_semaphore()
    for expert, shard in devices:
        pl.semaphore_signal(barrier, inc=1, device_id=(expert, shard), device_id_type=MESH)
    pl.semaphore_wait(barrier, len(devices))


class RowGather:
    def __init__(self, shard_ref, full_ref, columns, send, receive, expert, shard):
        self.rows = shard_ref.shape[0]
        self.columns = columns
        self.shard_ref, self.full_ref = shard_ref, full_ref
        self.send, self.receive = send, receive
        self.expert, self.shard = expert, shard
        core = lax.rem(expert, 2)
        self.sibling = expert + 1 - 2 * core
        self.after, self.before = lax.rem(shard + 1, SIDE), lax.rem(shard + 3, SIDE)
        self.across = lax.rem(shard + 2, SIDE)

    def at(self, shard, start, count, columns):
        place = pl.multiple_of(shard * self.rows + start, 16)
        return self.full_ref.at[pl.ds(place, count), columns]

    def ring(self, number, source, target, shard):
        return remote(
            source, target, self.send.at[number], self.receive.at[number], self.expert, shard
        )

    def first(self):
        target = self.at(self.shard, 0, self.rows, self.columns)
        source = self.shard_ref.at[:, self.columns]
        self.to_after = self.ring(0, source, target, self.after)
        self.to_before = self.ring(1, source, target, self.before)
        self.own = pltpu.make_async_copy(
            self.shard_ref, self.at(self.shard, 0, self.rows, pl.ds(0, self.shard_ref.shape[1])),
            self.send.at[8],
        )
        self.to_after.start()
        self.to_before.start()
        self.own.start()

    def hand(self, number, shard, start, count):
        block = self.at(shard, start, count, self.columns)
        copy = remote(
            block, block, self.send.at[number], self.receive.at[number], self.sibling, self.shard
        )
        copy.start()
        return copy

    def second(self):
        half = self.rows // 2
        self.to_after.wait_recv()
        top = self.at(self.before, 0, half, self.columns)
        self.pass_after = self.ring(2, top, top, self.after)
        self.pass_after.start()
        self.to_before.wait_recv()
        bottom = self.at(self.after, half, half, self.columns)
        self.pass_before = self.ring(3, bottom, bottom, self.before)
        self.pass_before.start()
        self.handed = [
            self.hand(4, self.before, 0, self.rows),
            self.hand(5, self.after, 0, self.rows),
        ]

    def third(self):
        half = self.rows // 2
        self.pass_after.wait_recv()
        self.handed.append(self.hand(6, self.across, 0, half))
        self.pass_before.wait_recv()
        self.handed.append(self.hand(7, self.across, half, half))

    def finish(self):
        self.own.wait()
        for copy in self.handed:
            copy.wait_recv()

    def drain(self):
        for copy in (self.to_after, self.to_before, self.pass_after, self.pass_before, *self.handed):
            copy.wait_send()


class PlaneGather:
    def __init__(self, shard_ref, full_ref, columns, stride, send, receive, expert, shard):
        self.rows = shard_ref.shape[0]
        self.shard_ref, self.full_ref, self.columns = shard_ref, full_ref, columns
        self.send, self.receive = send, receive
        self.expert, self.shard, self.stride = expert, shard, stride
        self.place = lax.rem(expert // stride, SIDE)
        self.sibling = expert + 1 - 2 * lax.rem(expert, 2)
        self.sent = []

    def at(self, shard, start, count):
        return self.full_ref.at[pl.ds(pl.multiple_of(shard * self.rows + start, 16), count), self.columns]

    def go(self, number, source, target, expert, shard):
        copy = remote(source, target, self.send.at[number], self.receive.at[number], expert, shard)
        copy.start()
        self.sent.append(copy)
        return copy

    def first(self):
        quarter = self.rows // SIDE
        start = pl.multiple_of(self.place * quarter, 16)
        source = self.shard_ref.at[pl.ds(start, quarter), self.columns]
        self.pieces = [
            self.go(
                by - 1, source, self.at(self.shard, start, quarter), self.expert, lax.rem(self.shard + by, SIDE)
            )
            for by in (2, 1, 3)
        ]

    def second(self):
        quarter = self.rows // SIDE
        self.shares = []
        for copy, by in zip(self.pieces, (2, 1, 3)):
            copy.wait_recv()
            piece = self.at(lax.rem(self.shard + SIDE - by, SIDE), self.place * quarter, quarter)
            for step in (2, 1, 3):
                peer = self.expert + (lax.rem(self.place + step, SIDE) - self.place) * self.stride
                self.shares.append(self.go(3 * by + step - 1, piece, piece, peer, self.shard))

    def third(self):
        for copy in self.shares:
            copy.wait_recv()
        self.handed = []
        for by in (1, 2, 3):
            block = self.at(lax.rem(self.shard + by, SIDE), 0, self.rows)
            self.handed.append(self.go(11 + by, block, block, self.sibling, self.shard))

    def finish(self):
        for copy in self.handed:
            copy.wait_recv()

    def drain(self):
        for copy in self.sent:
            copy.wait_send()


class Gather:
    def __init__(self, shard_ref, full_ref, send, receive, expert, shard):
        third = shard_ref.shape[1] // 6
        start = lax.rem(expert, 2) * 3 * third
        parts = [pl.ds(pl.multiple_of(start + number * third, LANES), third) for number in range(3)]
        self.parts = [
            PlaneGather(shard_ref, full_ref, parts[1], 2, send.at[1], receive.at[1], expert, shard),
            PlaneGather(shard_ref, full_ref, parts[2], 8, send.at[2], receive.at[2], expert, shard),
            RowGather(shard_ref, full_ref, parts[0], send.at[0], receive.at[0], expert, shard),
        ]

    def first(self):
        for part in self.parts:
            part.first()

    def second(self):
        for part in self.parts:
            part.second()

    def third(self):
        for part in self.parts:
            part.third()

    def finish(self):
        for part in self.parts:
            part.finish()

    def drain(self):
        for part in self.parts:
            part.drain()


def exchange_peers(expert):
    return [
        lax.rem(expert // 8 + dz, SIDE) * 8 + lax.rem(lax.rem(expert // 2, SIDE) + dx, SIDE) * 2
        + lax.rem(expert + dc, 2)
        for dz, dx, dc in exchange_order()
    ]


def exchange_order():
    reach = [0, 1, 2, 1]
    steps = [(dz, dx, dc) for dz in range(SIDE) for dx in range(SIDE) for dc in range(2)]
    return sorted(steps[1:], key=lambda step: -reach[step[0]] - reach[step[1]])


def exchange_start(source_ref, target_ref, send, receive, local, expert, shard, capacity):
    own = pl.ds(pl.multiple_of(expert * capacity, 16), capacity)
    copies = []
    for number, peer in enumerate(exchange_peers(expert)):
        block = pl.ds(pl.multiple_of(peer * capacity, 16), capacity)
        copy = remote(
            source_ref.at[block, :], target_ref.at[own, :], send.at[number], receive.at[number], peer, shard
        )
        copy.start()
        copies.append(copy)
    keep = pltpu.make_async_copy(source_ref.at[own, :], target_ref.at[own, :], local)
    keep.start()
    return copies, keep


def exchange_wait(copies, keep):
    keep.wait()
    for copy in copies:
        copy.wait()


def main_kernel(
    experts, capacity, x_in, g_in, routes_ref, wq_shard, wp_shard, router_ref, gain1_ref, bias1_ref, gain2_ref, bias2_ref,
    w1_in, w2_in,
    routes_out, wq_out, wp_out, ws_ref, ln_ref, qkv_ref, lse_ref, o_ref, x2_ref, gates_ref, pick0_ref, pick1_ref,
    y_out, dz_out, gw1_out, gw2_out, side1_out, side2_out,
    x_ref, g_ref, own_ref, small_ref, wq_ref, wp_ref, send_z, send_dy, z_ref, g_rows_ref, dy_ref,
    w1_ref, w2_ref, a_ref, slope_ref, gw1_ref, gw2_ref, rows_ref, y_ref, dz_ref,
    sends, receives, s_send, s_receive, ex_send, ex_receive, half_send, half_receive, local,
):
    rows, width = x_ref.shape
    load_x = pltpu.make_async_copy(x_in, x_ref, local.at[3])
    load_x.start()
    load_g = pltpu.make_async_copy(g_in, g_ref, local.at[4])
    load_g.start()
    expert, shard = lax.axis_index("expert"), lax.axis_index("wshard")
    core = lax.rem(expert, 2)
    pad = jnp.zeros((own_ref.shape[0] - experts - 4, width // SIDE), F32)
    mini = [router_ref[...].astype(F32)] + [
        ref[...].astype(F32).reshape(1, width // SIDE) for ref in (gain1_ref, bias1_ref, gain2_ref, bias2_ref)
    ]
    own_ref[:, : width // SIDE] = jnp.concatenate(mini + [pad], 0).astype(BF16)
    own_ref[:, width // SIDE :] = jnp.zeros((own_ref.shape[0], own_ref.shape[1] - width // SIDE), BF16)
    greet(
        [(expert, lax.rem(shard + by, SIDE)) for by in (1, 2, 3)]
        + [(peer, shard) for peer in exchange_peers(expert)]
    )
    small = []
    for by in (1, 2, 3):
        copy = remote(
            own_ref, small_ref.at[by - 1], s_send.at[by - 1], s_receive.at[by - 1], expert, lax.rem(shard + by, SIDE)
        )
        copy.start()
        small.append(copy)
    first_w, second_w = [
        Gather(shard_ref, full_ref, sends.at[number], receives.at[number], expert, shard)
        for number, (shard_ref, full_ref) in enumerate(((wq_shard, wq_ref), (wp_shard, wp_ref)))
    ]
    first_w.first()
    load_w1 = pltpu.make_async_copy(w1_in, w1_ref, local.at[5])
    load_w1.start()
    load_w2 = pltpu.make_async_copy(w2_in, w2_ref, local.at[6])
    load_w2.start()
    load_x.wait()
    x = x_ref[...].astype(F32)
    normed, _ = normalize(x)
    lane = lane_iota(rows)
    diagonal = lax.broadcasted_iota(jnp.int32, (rows, rows), 0) == lane_iota(rows, rows)
    routes = mm(diagonal.astype(F32).astype(BF16), routes_ref[...].astype(F32).astype(BF16), 1, 1)
    lane_number = lane.astype(F32)
    match = [lane_number == routes[:, k : k + 1] for k in range(2)]
    routes_out[...] = jnp.where(lane == 0, routes[:, 0:1], routes[:, 1:2])
    hits = (match[0] | match[1]).astype(F32).astype(BF16)
    earlier = lax.broadcasted_iota(jnp.int32, (rows, rows), 0) > lane_iota(rows, rows)
    before = mm(earlier.astype(F32).astype(BF16), hits)
    slots = lane_iota(rows, experts * capacity).astype(F32)
    for k, pick_ref in enumerate((pick0_ref, pick1_ref)):
        slot = jnp.sum(jnp.where(match[k], before, 0.0), -1, keepdims=True)
        place = routes[:, k : k + 1] * capacity + slot
        pick_ref[...] = (slots == place).astype(F32).astype(BF16)
    load_g.wait()
    send_dy[...] = mm(pick0_ref[...] + pick1_ref[...], g_ref[...], 0, 0).astype(BF16)
    moves = []

    def move(source, target):
        number = len(moves)
        moves.append(
            exchange_start(
                source, target, ex_send.at[number], ex_receive.at[number], local.at[7 + number], expert, shard, capacity
            )
        )
        return moves[-1]

    first_w.second()
    second_w.first()
    for copy in small:
        copy.wait_recv()
    pieces = []
    for place in range(SIDE):
        piece = own_ref[...].astype(F32)
        for by in (1, 2, 3):
            piece = jnp.where(lax.rem(shard + SIDE - by, SIDE) == place, small_ref[by - 1].astype(F32), piece)
        pieces.append(piece[:, : width // SIDE])
    both = jnp.concatenate(pieces, 1)
    vectors = both[experts : experts + 8, :]
    ln_ref[...] = vectors
    ws_ref[...] = jnp.concatenate([both[:experts], jnp.zeros((LANES - experts, width), F32)], 0).astype(BF16)
    h1 = (normed * vectors[0:1, :] + vectors[1:2, :]).astype(BF16)
    first_w.third()
    second_w.second()
    first_w.finish()
    dy_move = move(send_dy, g_rows_ref)
    keep_first = pltpu.make_async_copy(wq_ref, wq_out, local.at[1])
    keep_first.start()
    qkv_ref[...] = mm(h1, wq_ref[...]).astype(BF16)
    scale = HEAD_DIM ** (-0.5)
    lse_all = jnp.zeros((rows, LANES), F32)
    for pair in range(width // LANES):
        if pair == 2:
            second_w.third()
        at = pair * LANES
        q = qkv_ref[:, at : at + LANES]
        k = qkv_ref[:, width + at : width + at + LANES]
        v = qkv_ref[:, 2 * width + at : 2 * width + at + LANES]
        halves = []
        for half in range(2):
            own = (lane // HEAD_DIM) == half
            s = mm(jnp.where(own, q, jnp.zeros_like(q)), k, 1, 1) * scale
            top = jnp.max(s, -1, keepdims=True)
            e = jnp.exp(s - top)
            total = jnp.sum(e, -1, keepdims=True)
            lse_all = jnp.where(lane == 2 * pair + half, top + jnp.log(total), lse_all)
            halves.append(mm((e / total).astype(BF16), v))
        o_ref[:, at : at + LANES] = jnp.where(lane < HEAD_DIM, halves[0], halves[1]).astype(BF16)
    lse_ref[...] = lse_all
    second_w.finish()
    keep_second = pltpu.make_async_copy(wp_ref, wp_out, local.at[2])
    keep_second.start()
    x2 = x + mm(o_ref[...], wp_ref[...])
    x2_ref[...] = x2
    normed2, _ = normalize(x2)
    h2 = (normed2 * vectors[2:3, :] + vectors[3:4, :]).astype(BF16)
    logits = jnp.where(lane < experts, mm(h2, ws_ref[...], 1, 1), -jnp.inf)
    e = jnp.exp(logits - jnp.max(logits, -1, keepdims=True))
    gates = e / jnp.sum(e, -1, keepdims=True)
    gates_ref[...] = gates
    shares = []
    for k in range(2):
        chosen = jnp.sum(jnp.where(match[k], gates, 0.0), -1, keepdims=True)
        high = chosen.astype(BF16)
        rest = chosen - high.astype(F32)
        middle = rest.astype(BF16)
        rest = rest - middle.astype(F32)
        share = jnp.where(lane == 0, high.astype(F32), jnp.where(lane == 1, middle.astype(F32), rest))
        shares.append(jnp.where(lane < 3, share, 0.0).astype(BF16))
    both_picks = pick0_ref[...] + pick1_ref[...]
    send_z[:, :width] = mm(both_picks, h2, 0, 0).astype(BF16)
    send_z[:, width:] = (mm(pick0_ref[...], shares[0], 0, 0) + mm(pick1_ref[...], shares[1], 0, 0)).astype(BF16)
    z_move = move(send_z, z_ref)
    for copy in small:
        copy.wait_send()
    for gather in (first_w, second_w):
        gather.drain()
    keep_first.wait()
    keep_second.wait()
    load_w1.wait()
    load_w2.wait()
    block = width
    blocks = w1_ref.shape[1] // block
    exchange_wait(*z_move)

    def columns(number):
        return pl.ds(pl.multiple_of(number * block, block), block)

    rows_ref[...] = jnp.zeros_like(rows_ref)

    z = z_ref.at[:, pl.ds(0, width)]
    exchange_wait(*dy_move)
    share = z_ref[:, width:].astype(F32)
    dy_ref[...] = (g_rows_ref[...].astype(F32) * (share[:, 0:1] + share[:, 1:2] + share[:, 2:3])).astype(BF16)
    after, before, across = [lax.rem(shard + by, SIDE) for by in (1, 3, 2)]
    halves = []

    def pass_halves(place, source, target, at=slice(None)):
        rows_each = source.shape[0] // SIDE
        for number, peer in enumerate((after, before)):
            start = pl.multiple_of(across * rows_each + number * (rows_each // 2), 16)
            copy = remote(
                source.at[pl.ds(start, rows_each // 2), at], target.at[number, :, at],
                half_send.at[place, number], half_receive.at[place, number], expert, peer,
            )
            copy.start()
            halves.append(copy)

    def activate(number):
        at = columns(number)
        u = mm(z[...], w1_ref[:, at])
        phi = 0.5 * (1.0 + lax.erf(u * (2.0**-0.5)))
        density = jnp.exp(-0.5 * u * u) * 0.3989422804014327
        slope_ref[:, at] = phi + u * density
        a = (u * phi).astype(BF16)
        a_ref[:, at] = a
        rows_ref[...] += mm(a, w2_ref[at, :])
        gw2_ref[at, :] = mm(a, dy_ref[...], 0, 0).astype(BF16)

    activate(across)
    pass_halves(0, gw2_ref, side2_out)

    def activate_others(step, _):
        activate(lax.rem(across + step, SIDE))
        return 0

    lax.fori_loop(1, blocks, activate_others, 0)
    y_ref[...] = rows_ref[...].astype(BF16)
    move(y_ref, y_out)

    keep_gw2 = pltpu.make_async_copy(gw2_ref, gw2_out, local.at[11])
    keep_gw2.start()
    rows_ref[...] = jnp.zeros_like(rows_ref)

    for number in range(blocks):
        at = slice(number * block, (number + 1) * block)
        da = mm(dy_ref[...], w2_ref[at, :], 1, 1)
        du = (da * slope_ref[:, at]).astype(BF16)
        rows_ref[...] += mm(du, w1_ref[:, at], 1, 1)
        gw1_ref[:, at] = mm(z[...], du, 0, 0).astype(BF16)
        pass_halves(1 + number, gw1_ref, side1_out, at)

    dz_ref[...] = rows_ref[...].astype(BF16)
    move(dz_ref, dz_out)
    keep_gw1 = pltpu.make_async_copy(gw1_ref, gw1_out, local.at[12])
    keep_gw1.start()
    keep_gw2.wait()
    keep_gw1.wait()
    for copies, keep in moves[2:]:
        exchange_wait(copies, keep)
    for copy in halves:
        copy.wait()


def forward(tokens, cotangent, routes, wq, wp, router, vectors, w1, w2, experts, capacity):
    rows, width = tokens.shape
    hidden = w1.shape[1]
    slots = experts * capacity
    vmem, anywhere = pl.BlockSpec(memory_space=pltpu.VMEM), pl.BlockSpec(memory_space=pl.ANY)
    return pl.pallas_call(
        functools.partial(main_kernel, experts, capacity),
        out_shape=(
            jax.ShapeDtypeStruct((rows, LANES), F32),
            jax.ShapeDtypeStruct((width, 3 * width), BF16),
            jax.ShapeDtypeStruct((width, width), BF16),
            jax.ShapeDtypeStruct((LANES, width), BF16),
            jax.ShapeDtypeStruct((8, width), F32),
            jax.ShapeDtypeStruct((rows, 3 * width), BF16),
            jax.ShapeDtypeStruct((rows, LANES), F32),
            jax.ShapeDtypeStruct((rows, width), BF16),
            jax.ShapeDtypeStruct((rows, width), F32),
            jax.ShapeDtypeStruct((rows, LANES), F32),
            jax.ShapeDtypeStruct((rows, slots), BF16),
            jax.ShapeDtypeStruct((rows, slots), BF16),
            jax.ShapeDtypeStruct((slots, width), BF16),
            jax.ShapeDtypeStruct((slots, width), BF16),
            jax.ShapeDtypeStruct((width, hidden), BF16),
            jax.ShapeDtypeStruct((hidden, width), BF16),
            jax.ShapeDtypeStruct((2, width // 8, hidden), BF16),
            jax.ShapeDtypeStruct((2, hidden // 8, width), BF16),
        ),
        in_specs=[anywhere] * 2 + [vmem] + [anywhere] * 2 + [vmem] * 5 + [anywhere] * 2,
        out_specs=[vmem] + [anywhere] * 2 + [vmem] * 9 + [anywhere] * 6,
        scratch_shapes=[
            pltpu.VMEM((rows, width), BF16),
            pltpu.VMEM((rows, width), BF16),
            pltpu.VMEM((48, 256), BF16),
            pltpu.VMEM((3, 48, 256), BF16),
            pltpu.VMEM((width, 3 * width), BF16),
            pltpu.VMEM((width, width), BF16),
            pltpu.VMEM((slots, width + LANES), BF16),
            pltpu.VMEM((slots, width), BF16),
            pltpu.VMEM((slots, width + LANES), BF16),
            pltpu.VMEM((slots, width), BF16),
            pltpu.VMEM((slots, width), BF16),
            pltpu.VMEM((width, hidden), BF16),
            pltpu.VMEM((hidden, width), BF16),
            pltpu.VMEM((slots, hidden), BF16),
            pltpu.VMEM((slots, hidden), F32),
            pltpu.VMEM((width, hidden), BF16),
            pltpu.VMEM((hidden, width), BF16),
            pltpu.VMEM((slots, width), F32),
            pltpu.VMEM((slots, width), BF16),
            pltpu.VMEM((slots, width), BF16),
            pltpu.SemaphoreType.DMA((2, 3, 15)),
            pltpu.SemaphoreType.DMA((2, 3, 15)),
            pltpu.SemaphoreType.DMA((3,)),
            pltpu.SemaphoreType.DMA((3,)),
            pltpu.SemaphoreType.DMA((4, 31)),
            pltpu.SemaphoreType.DMA((4, 31)),
            pltpu.SemaphoreType.DMA((5, 2)),
            pltpu.SemaphoreType.DMA((5, 2)),
            pltpu.SemaphoreType.DMA((13,)),
        ],
        compiler_params=pltpu.CompilerParams(
            vmem_limit_bytes=58 * MIB, collective_id=1, has_side_effects=True
        ),
        cost_estimate=pl.CostEstimate(
            flops=12 * slots * width * hidden, bytes_accessed=48 * MIB, transcendentals=2 * slots * hidden
        ),
        name="forward_and_experts",
    )(tokens, cotangent, routes, wq, wp, router, *vectors, w1, w2)


def tail_kernel(
    x_in, g_in, routes_in, wq_in, wp_in, ws_in, ln_in, qkv_in, lse_in, o_in, x2_in, gates_in, pick0_in, pick1_in,
    y_in, dz_in, gw1_in, gw2_in, side1_in, side2_in,
    mixed_ref, dx_ref, gwq_ref, gwp_ref, small_ref, gw1_ref, gw2_ref,
    x_ref, g_ref, routes_ref, wq_ref, wp_ref, ws_ref, ln_ref, qkv_ref, lse_ref, o_ref, x2_ref, gates_ref,
    pick0_ref, pick1_ref, y_ref, dz_ref, side1, side2, part1, part2, came1, came2, do_ref, dqkv_ref, h1_ref,
    theirs, ours, paired, summed, side, first_in, second, second_in, third_in, piece, line, plane, gathered,
    s_ref, s_pair, s_sum, s_in, s_out, s_other,
    loads, send, receive, s_send, s_receive, g_send, g_receive,
):
    expert, shard = lax.axis_index("expert"), lax.axis_index("wshard")
    core = lax.rem(expert, 2)
    x_at, z_at = lax.rem(expert // 2, SIDE), expert // 8
    sibling = expert + 1 - 2 * core
    first, second_at = x_at * (1 - core) + z_at * core, z_at * (1 - core) + x_at * core
    first_step, second_step = 2 + 6 * core, 8 - 6 * core

    def turn(place, by):
        return lax.rem(place + by, SIDE)

    def on_first(by):
        return expert + (turn(first, by) - first) * first_step

    def on_second(by):
        return expert + (turn(second_at, by) - second_at) * second_step

    load_count = [0]

    def load(source, target):
        copy = pltpu.make_async_copy(source, target, loads.at[load_count[0]])
        load_count[0] += 1
        copy.start()
        return copy

    rows1, rows2 = part1.shape[1], part2.shape[1]

    def shard_rows(ref, by, rows):
        return ref.at[pl.ds(pl.multiple_of(turn(shard, by) * rows, 16), rows), :]

    load_first = [load(side1_in, side1)] + [
        load(shard_rows(gw1_in, by, rows1), part1.at[number]) for number, by in enumerate((1, 3))
    ]
    load_out = [
        load(*pair) for pair in (
            (y_in, y_ref), (pick0_in, pick0_ref), (pick1_in, pick1_ref), (x2_in, x2_ref), (g_in, g_ref),
            (gates_in, gates_ref), (routes_in, routes_ref),
        )
    ]
    load_gates = [
        load(*pair) for pair in (
            (dz_in, dz_ref), (ws_in, ws_ref), (ln_in, ln_ref), (wp_in, wp_ref), (o_in, o_ref), (x_in, x_ref),
        )
    ]
    load_heads = [load(qkv_in, qkv_ref), load(lse_in, lse_ref)]
    load_second = [load(side2_in, side2)] + [
        load(shard_rows(gw2_in, by, rows2), part2.at[number]) for number, by in enumerate((1, 3))
    ]
    load_last = [load(wq_in, wq_ref)]
    load_own = [
        load(shard_rows(gw1_in, 0, rows1), part1.at[2]), load(shard_rows(gw2_in, 0, rows2), part2.at[2])
    ]

    greet(
        [(sibling, shard)]
        + [(on_first(by), shard) for by in (1, 2, 3)]
        + [(on_second(by), shard) for by in (1, 2, 3)]
        + [(expert, turn(shard, by)) for by in (1, 2, 3)]
    )
    started = []
    counts = {}

    def go(source, target, to_expert, to_shard, sends=send, receives=receive, kind="wide"):
        number = counts.get(kind, 0)
        counts[kind] = number + 1
        copy = remote(source, target, sends.at[number], receives.at[number], to_expert, to_shard)
        copy.start()
        started.append(copy)
        return copy

    def go_small(*args):
        return go(*args, sends=s_send, receives=s_receive, kind="small")

    def add(left, right):
        return (left.astype(F32) + right.astype(F32)).astype(BF16)

    def join(part, came_half):
        half = part.shape[1] // 2
        part[0, :half] = add(part[0, :half], came_half[0])
        part[1, half:] = add(part[1, half:], came_half[1])

    def pass_on(part, came, start, count):
        at = pl.ds(start, count)
        return [
            go(
                part.at[number, at], came.at[number, at], expert, turn(shard, by), g_send, g_receive, "expert"
            )
            for number, by in enumerate((1, 3))
        ]

    for copy in load_first:
        copy.wait()
    join(part1, side1)
    grads_first = pass_on(part1, came1, 0, rows1)

    for copy in load_out:
        copy.wait()
    rows, width = x_ref.shape
    lane = lane_iota(rows)
    g = g_ref[...].astype(F32)
    x2 = x2_ref[...]
    gates = gates_ref[...]
    routes = routes_ref[...]
    out = x2
    dgates = jnp.zeros((rows, LANES), F32)
    for k, pick_ref in enumerate((pick0_ref, pick1_ref)):
        match = lane.astype(F32) == routes[:, k : k + 1]
        picked = mm(pick_ref[...], y_ref[...])
        chosen = jnp.sum(jnp.where(match, gates, 0.0), -1, keepdims=True)
        out = out + chosen * picked
        dgates = jnp.where(match, jnp.sum(g * picked, -1, keepdims=True), dgates)
    mixed_ref[...] = out.astype(BF16)
    dl = (gates * (dgates - jnp.sum(gates * dgates, -1, keepdims=True))).astype(BF16)
    for copy in load_gates:
        copy.wait()
    dh2 = mm(pick0_ref[...] + pick1_ref[...], dz_ref[...]) + mm(dl, ws_ref[...])
    gain1, bias1 = ln_ref[0:1, :], ln_ref[1:2, :]
    gain2, bias2 = ln_ref[2:3, :], ln_ref[3:4, :]
    n2, r2 = normalize(x2)
    h2 = (n2 * gain2 + bias2).astype(BF16)
    g_router = mm(dl, h2, 0, 0)
    g_gain2 = jnp.sum(dh2 * n2, 0, keepdims=True)
    g_bias2 = jnp.sum(dh2, 0, keepdims=True)
    dx2 = g + norm_back(dh2, n2, r2, gain2)
    dx_ref[...] = dx2
    dx2b = dx2.astype(BF16)
    do_ref[...] = dx2b
    block = width // 2
    mine = pl.ds(pl.multiple_of(core * block, LANES), block)
    others = pl.ds(pl.multiple_of((1 - core) * block, LANES), block)
    theirs[3] = mm(o_ref[...], do_ref[:, others], 0, 0).astype(BF16)
    pair = [None] * SIDE
    pair[3] = go(theirs.at[3], paired.at[3], sibling, shard)
    ours[3] = mm(o_ref[...], do_ref[:, mine], 0, 0).astype(BF16)
    do_ref[...] = mm(dx2b, wp_ref[...], 1, 1).astype(BF16)
    n1, r1 = normalize(x_ref[...].astype(F32))
    h1_ref[...] = (n1 * gain1 + bias1).astype(BF16)
    for copy in load_second:
        copy.wait()
    join(part2, side2)
    early = rows2 // 4
    grads_second = pass_on(part2, came2, 0, early)
    for copy in load_heads:
        copy.wait()
    scale = HEAD_DIM ** (-0.5)
    low = lane < HEAD_DIM

    def heads(start):
        for step in range(block // LANES):
            at = [
                pl.ds(pl.multiple_of(third * width + start + step * LANES, LANES), LANES) for third in range(3)
            ]
            q, k, v = qkv_ref[:, at[0]], qkv_ref[:, at[1]], qkv_ref[:, at[2]]
            do = do_ref[:, at[0]]
            parts = []
            for half in range(2):
                own = (lane // HEAD_DIM) == half
                head = start // HEAD_DIM + 2 * step + half
                lse = jnp.sum(jnp.where(lane == head, lse_ref[...], 0.0), -1, keepdims=True)
                s = mm(jnp.where(own, q, jnp.zeros_like(q)), k, 1, 1) * scale
                p = jnp.exp(s - lse)
                dp = mm(jnp.where(own, do, jnp.zeros_like(do)), v, 1, 1)
                ds = (p * (dp - jnp.sum(dp * p, -1, keepdims=True))).astype(BF16)
                parts.append((mm(ds, k) * scale, mm(ds, q, 0, 0) * scale, mm(p.astype(BF16), do, 0, 0)))
            for third, (left, right) in enumerate(zip(*parts)):
                dqkv_ref[:, at[third]] = jnp.where(low, left, right).astype(BF16)

    def weight_grads(target, start):
        for third in range(3):
            columns = pl.ds(pl.multiple_of(third * width + start, LANES), block)
            target[third] = mm(h1_ref[...], dqkv_ref[:, columns], 0, 0).astype(BF16)

    heads((1 - core) * block)
    weight_grads(theirs, (1 - core) * block)
    for third in range(3):
        pair[third] = go(theirs.at[third], paired.at[third], sibling, shard)
    heads(core * block)
    weight_grads(ours, core * block)
    for copy in pair:
        copy.wait_recv()

    order = (2, 1, 3, 0)

    def add_pair(number):
        chunk = turn(first, order[number])
        summed[number] = add(ours[chunk], paired[chunk])

    wide = s_ref.shape[1]
    part, quarter, half = wide // 2, wide // 4, 2 * wide
    add_pair(0)
    relay_up = go(summed.at[0, pl.ds(0, half)], side.at[0], on_first(1), shard)
    relay_down = go(summed.at[0, pl.ds(half, half)], side.at[1], on_first(3), shard)
    add_pair(1)
    add_pair(2)

    for copy in load_last:
        copy.wait()
    dh1 = mm(dqkv_ref[...], wq_ref[...], 1, 1)
    g_gain1 = jnp.sum(dh1 * n1, 0, keepdims=True)
    g_bias1 = jnp.sum(dh1, 0, keepdims=True)
    row = lax.broadcasted_iota(jnp.int32, (LANES, width), 0)
    vectors = g_router
    for place, vector in enumerate((g_gain1, g_bias1, g_gain2, g_bias2)):
        vectors = jnp.where(row == 32 + place, vector, vectors)
    s_ref[...] = vectors.T.astype(BF16).reshape(s_ref.shape)
    small_pair = go_small(s_ref, s_pair, sibling, shard)

    relay_up.wait_recv()
    summed[1, :half] = add(summed[1, :half], side[0])
    up = go(summed.at[1], first_in.at[0], on_first(1), shard)
    relay_down.wait_recv()
    summed[2, half:] = add(summed[2, half:], side[1])
    down = go(summed.at[2], first_in.at[1], on_first(3), shard)
    add_pair(3)
    dx_ref[...] += norm_back(dh1, n1, r1, gain1)

    small_pair.wait_recv()
    s_sum[...] = add(s_ref[...], s_pair[...])
    s_mine = pl.ds(pl.multiple_of(core * part, 16), part)
    s_others = pl.ds(pl.multiple_of((1 - core) * part, 16), part)
    small_along = [
        go_small(s_sum.at[turn(shard, by), s_mine, :], s_in.at[by - 1], expert, turn(shard, by)) for by in (1, 2, 3)
    ]
    for copy in small_along:
        copy.wait_recv()

    def four(own, a, b, c):
        return own.astype(F32) + a.astype(F32) + b.astype(F32) + c.astype(F32)

    s_out[0] = four(s_sum[shard, s_mine, :], s_in[0], s_in[1], s_in[2]).astype(BF16)
    small_first = [go_small(s_out.at[0], s_in.at[2 + by], on_first(by), shard) for by in (1, 2, 3)]

    up.wait_recv()
    down.wait_recv()
    for own_shard in range(SIDE):
        for place in range(SIDE):
            at = pl.ds(own_shard * wide + place * quarter, quarter)
            second[place, own_shard] = (
                summed[3, at, :].astype(F32) + first_in[0, at, :].astype(F32) + first_in[1, at, :].astype(F32)
            ).astype(BF16)
    along_second = [
        go(second.at[turn(second_at, by)], second_in.at[by - 1], on_second(by), shard) for by in (2, 1, 3)
    ]
    for copy in small_first:
        copy.wait_recv()
    s_out[1] = four(s_out[0], s_in[3], s_in[4], s_in[5]).astype(BF16)
    small_second = [go_small(s_out.at[1], s_in.at[5 + by], on_second(by), shard) for by in (1, 2, 3)]
    for copy in along_second:
        copy.wait_recv()
    piece[...] = four(second[second_at], second_in[0], second_in[1], second_in[2]).astype(BF16)
    along_shard = [
        go(piece.at[turn(shard, by)], third_in.at[by - 1], expert, turn(shard, by)) for by in (2, 1, 3)
    ]
    grads_second += pass_on(part2, came2, early, rows2 - early)
    for copy in small_second:
        copy.wait_recv()
    s_out[2] = four(s_out[1], s_in[6], s_in[7], s_in[8]).astype(BF16)
    small_back = go_small(s_out.at[2], s_other, sibling, shard)
    for copy in load_own:
        copy.wait()
    for copy in along_shard:
        copy.wait_recv()
    line[second_at] = four(piece[shard], third_in[0], third_in[1], third_in[2]).astype(BF16)
    back_second = [
        go(line.at[second_at], line.at[second_at], on_second(by), shard) for by in (2, 1, 3)
    ]
    small_back.wait_recv()
    small_ref[s_mine, :] = s_out[2].astype(F32)
    small_ref[s_others, :] = s_other[...].astype(F32)
    for copy in back_second:
        copy.wait_recv()
    plane[first] = line[...].reshape(wide, line.shape[-1])
    back_first = [
        go(plane.at[first], plane.at[first], on_first(by), shard) for by in (2, 1, 3)
    ]
    own_back = go(plane.at[first], gathered.at[first], sibling, shard)
    for copy in grads_first:
        copy.wait_recv()
    gw1_ref[...] = (part1[2].astype(F32) + came1[0].astype(F32) + came1[1].astype(F32)).astype(BF16)
    hands = []
    for copy, by in zip(back_first, (2, 1, 3)):
        copy.wait_recv()
        came = turn(first, SIDE - by)
        hands.append(go(plane.at[came], gathered.at[came], sibling, shard))

    def put(source, start):
        for third in range(3):
            columns = pl.ds(pl.multiple_of(third * width + start, LANES), block)
            gwq_ref[:, columns] = source[third]
        gwp_ref[:, pl.ds(pl.multiple_of(start, LANES), block)] = source[3]

    put(plane, core * block)
    own_back.wait_recv()
    for copy in hands:
        copy.wait_recv()
    put(gathered, (1 - core) * block)
    for copy in grads_second:
        copy.wait_recv()
    gw2_ref[...] = (part2[2].astype(F32) + came2[0].astype(F32) + came2[1].astype(F32)).astype(BF16)
    for copy in started:
        copy.wait_send()


def tail(operands, expert_operands, collective_id):
    tokens, width = operands[0].shape
    columns = width // 2
    rows = width // SIDE
    hidden = expert_operands[0].shape[1]
    quarter, part = rows // 4, rows // 2
    vmem, semaphores = pltpu.VMEM, pltpu.SemaphoreType.DMA
    anywhere = pl.BlockSpec(memory_space=pl.ANY)
    everything = (*operands, *expert_operands)
    return pl.pallas_call(
        tail_kernel,
        out_shape=(
            jax.ShapeDtypeStruct((tokens, width), BF16),
            jax.ShapeDtypeStruct((tokens, width), F32),
            jax.ShapeDtypeStruct((rows, 3 * width), BF16),
            jax.ShapeDtypeStruct((rows, width), BF16),
            jax.ShapeDtypeStruct((rows, LANES), F32),
            jax.ShapeDtypeStruct((rows, hidden), BF16),
            jax.ShapeDtypeStruct((hidden // SIDE, width), BF16),
        ),
        in_specs=[anywhere] * len(everything),
        out_specs=[pl.BlockSpec(memory_space=vmem)] * 7,
        scratch_shapes=[vmem(array.shape, array.dtype) for array in operands] + [
            vmem((2, rows // 2, hidden), BF16),
            vmem((2, hidden // 8, width), BF16),
            vmem((3, rows, hidden), BF16),
            vmem((3, hidden // SIDE, width), BF16),
            vmem((2, rows, hidden), BF16),
            vmem((2, hidden // SIDE, width), BF16),
            vmem((tokens, width), BF16),
            vmem((tokens, 3 * width), BF16),
            vmem((tokens, width), BF16),
            vmem((SIDE, width, columns), BF16),
            vmem((SIDE, width, columns), BF16),
            vmem((SIDE, width, columns), BF16),
            vmem((SIDE, width, columns), BF16),
            vmem((2, 2 * rows, columns), BF16),
            vmem((2, width, columns), BF16),
            vmem((SIDE, SIDE, quarter, columns), BF16),
            vmem((3, SIDE, quarter, columns), BF16),
            vmem((3, quarter, columns), BF16),
            vmem((SIDE, quarter, columns), BF16),
            vmem((SIDE, quarter, columns), BF16),
            vmem((SIDE, rows, columns), BF16),
            vmem((SIDE, rows, columns), BF16),
            vmem((SIDE, rows, LANES), BF16),
            vmem((SIDE, rows, LANES), BF16),
            vmem((SIDE, rows, LANES), BF16),
            vmem((9, part, LANES), BF16),
            vmem((3, part, LANES), BF16),
            vmem((part, LANES), BF16),
            semaphores((24,)),
            semaphores((24,)),
            semaphores((24,)),
            semaphores((11,)),
            semaphores((11,)),
            semaphores((6,)),
            semaphores((6,)),
        ],
        compiler_params=pltpu.CompilerParams(
            vmem_limit_bytes=58 * MIB, collective_id=collective_id, has_side_effects=True
        ),
        cost_estimate=pl.CostEstimate(
            flops=2 * tokens * width * 14 * width, bytes_accessed=48 * MIB, transcendentals=tokens * tokens * 12
        ),
        name="backward_and_sums",
    )(*everything)


def widen_kernel(experts, *refs):
    ins, outs, buffers, wide, loads, stores = refs[:7], refs[7:18], refs[18:25], refs[25:32], refs[32], refs[33]
    small_in, small_buffer = ins[4], buffers[4]
    incoming = []
    for number, (source, target) in enumerate(zip(ins, buffers)):
        copy = pltpu.make_async_copy(source, target, loads.at[number])
        copy.start()
        incoming.append(copy)
    outgoing = []

    def store(source, target):
        copy = pltpu.make_async_copy(source, target, stores.at[len(outgoing)])
        copy.start()
        outgoing.append(copy)

    places = (0, 1, 4, 5, None, 9, 10)
    for number in (0, 1, 5, 6, 2, 3):
        incoming[number].wait()
        if number < 2:
            store(buffers[number], outs[places[number]])
        else:
            wide[number][...] = buffers[number][...].astype(F32)
            target = outs[places[number]]
            store(wide[number], target.at[0] if number > 4 else target)
    incoming[4].wait()
    rows = small_buffer.shape[0]
    padded = jnp.concatenate([small_buffer[...], jnp.zeros((256 - rows, LANES), F32)], 0).T
    outs[8][...] = padded[:experts, :rows]
    for place, output in enumerate((2, 3, 6, 7)):
        outs[output][...] = padded[experts + place : experts + place + 1, :rows].reshape(rows)
    for copy in outgoing:
        copy.wait()


def widen(mixed, grad_tokens, gwq, gwp, small, gw1, gw2, experts):
    ins = (mixed, grad_tokens, gwq, gwp, small, gw1, gw2)
    rows = small.shape[0]
    anywhere, vmem = pl.BlockSpec(memory_space=pl.ANY), pl.BlockSpec(memory_space=pltpu.VMEM)
    shapes = [
        (mixed.shape, BF16), (grad_tokens.shape, F32), ((rows,), F32), ((rows,), F32), (gwq.shape, F32), (gwp.shape, F32),
        ((rows,), F32), ((rows,), F32), ((experts, rows), F32), ((1, *gw1.shape), F32), ((1, *gw2.shape), F32),
    ]
    return pl.pallas_call(
        functools.partial(widen_kernel, experts),
        out_shape=[jax.ShapeDtypeStruct(*shape) for shape in shapes],
        in_specs=[anywhere] * 7,
        out_specs=[anywhere if place in (0, 1, 4, 5, 9, 10) else vmem for place in range(11)],
        scratch_shapes=[pltpu.VMEM(array.shape, array.dtype) for array in ins]
        + [pltpu.VMEM(array.shape, F32) for array in ins]
        + [pltpu.SemaphoreType.DMA((7,)), pltpu.SemaphoreType.DMA((6,))],
        compiler_params=pltpu.CompilerParams(vmem_limit_bytes=58 * MIB),
        cost_estimate=pl.CostEstimate(flops=0, bytes_accessed=13 * MIB, transcendentals=0),
        name="widen_outputs",
    )(*ins)


def on_device(
    tokens, ln1_gain, ln1_bias, w_qkv, w_proj, ln2_gain, ln2_bias, w_router,
    expert_in, expert_out, routes, cotangent,
):
    rows = tokens.shape[0]
    experts = w_router.shape[1]
    capacity = (5 * rows // 2 + 8 * experts - 1) // (8 * experts) * 8
    *kept, g_first, g_second, side_first, side_second = forward(
        tokens, cotangent, routes.T, w_qkv, w_proj, w_router.T, (ln1_gain, ln1_bias, ln2_gain, ln2_bias),
        expert_in[0], expert_out[0], experts, capacity,
    )
    sums = tail((tokens, cotangent, *kept), (g_first, g_second, side_first, side_second), 3)
    outputs = list(widen(*sums, experts))
    outputs[8] = outputs[8].T
    return tuple(outputs)


def solution(mesh):
    in_specs = (
        P(("expert", "wshard"), None),
        P("wshard"),
        P("wshard"),
        P("wshard", None),
        P("wshard", None),
        P("wshard"),
        P("wshard"),
        P("wshard", None),
        P("expert", None, None),
        P("expert", None, None),
        P(("expert", "wshard"), None),
        P(("expert", "wshard"), None),
    )
    out_specs = (
        P(("expert", "wshard"), None),
        P(("expert", "wshard"), None),
        P("wshard"),
        P("wshard"),
        P("wshard", None),
        P("wshard", None),
        P("wshard"),
        P("wshard"),
        P("wshard", None),
        P("expert", "wshard", None),
        P("expert", "wshard", None),
    )
    return jax.shard_map(
        on_device, mesh=mesh, in_specs=in_specs, out_specs=out_specs, check_vma=False
    )
```

```python
import functools

import jax
import jax.numpy as jnp
from jax import lax
from jax.experimental import pallas as pl
from jax.experimental.pallas import tpu as pltpu
from jax.sharding import PartitionSpec as P

HEAD_DIM = 64
EPSILON = 1e-06
F32 = jnp.float32
BF16 = jnp.bfloat16
LANES = 128
MIB = 1 << 20


def mm(left, right, left_dim=1, right_dim=0):
    return lax.dot_general(
        left, right, (((left_dim,), (right_dim,)), ((), ())), preferred_element_type=F32
    )


def normalize(values):
    centered = values - jnp.mean(values, -1, keepdims=True)
    inverse = lax.rsqrt(jnp.mean(centered * centered, -1, keepdims=True) + EPSILON)
    return centered * inverse, inverse


def norm_back(upstream, normed, inverse, gain):
    scaled = upstream * gain
    return inverse * (
        scaled
        - jnp.mean(scaled, -1, keepdims=True)
        - normed * jnp.mean(scaled * normed, -1, keepdims=True)
    )


def lane_iota(rows, columns=LANES):
    return lax.broadcasted_iota(jnp.int32, (rows, columns), 1)


MESH = pl.DeviceIdType.MESH
SIDE = 4


def remote(source, target, send, receive, expert, shard):
    return pltpu.make_async_remote_copy(
        src_ref=source, dst_ref=target, send_sem=send, recv_sem=receive,
        device_id=(expert, shard), device_id_type=MESH,
    )


def greet(devices):
    barrier = pltpu.get_barrier_semaphore()
    for expert, shard in devices:
        pl.semaphore_signal(barrier, inc=1, device_id=(expert, shard), device_id_type=MESH)
    pl.semaphore_wait(barrier, len(devices))


class RowGather:
    def __init__(self, shard_ref, full_ref, columns, send, receive, expert, shard):
        self.rows = shard_ref.shape[0]
        self.columns = columns
        self.shard_ref, self.full_ref = shard_ref, full_ref
        self.send, self.receive = send, receive
        self.expert, self.shard = expert, shard
        core = lax.rem(expert, 2)
        self.sibling = expert + 1 - 2 * core
        self.after, self.before = lax.rem(shard + 1, SIDE), lax.rem(shard + 3, SIDE)
        self.across = lax.rem(shard + 2, SIDE)

    def at(self, shard, start, count, columns):
        place = pl.multiple_of(shard * self.rows + start, 16)
        return self.full_ref.at[pl.ds(place, count), columns]

    def ring(self, number, source, target, shard):
        return remote(
            source, target, self.send.at[number], self.receive.at[number], self.expert, shard
        )

    def first(self):
        target = self.at(self.shard, 0, self.rows, self.columns)
        source = self.shard_ref.at[:, self.columns]
        self.to_after = self.ring(0, source, target, self.after)
        self.to_before = self.ring(1, source, target, self.before)
        self.own = pltpu.make_async_copy(
            self.shard_ref, self.at(self.shard, 0, self.rows, pl.ds(0, self.shard_ref.shape[1])),
            self.send.at[8],
        )
        self.to_after.start()
        self.to_before.start()
        self.own.start()

    def hand(self, number, shard, start, count):
        block = self.at(shard, start, count, self.columns)
        copy = remote(
            block, block, self.send.at[number], self.receive.at[number], self.sibling, self.shard
        )
        copy.start()
        return copy

    def second(self):
        half = self.rows // 2
        self.to_after.wait_recv()
        top = self.at(self.before, 0, half, self.columns)
        self.pass_after = self.ring(2, top, top, self.after)
        self.pass_after.start()
        self.to_before.wait_recv()
        bottom = self.at(self.after, half, half, self.columns)
        self.pass_before = self.ring(3, bottom, bottom, self.before)
        self.pass_before.start()
        self.handed = [
            self.hand(4, self.before, 0, self.rows),
            self.hand(5, self.after, 0, self.rows),
        ]

    def third(self):
        half = self.rows // 2
        self.pass_after.wait_recv()
        self.handed.append(self.hand(6, self.across, 0, half))
        self.pass_before.wait_recv()
        self.handed.append(self.hand(7, self.across, half, half))

    def finish(self):
        self.own.wait()
        for copy in self.handed:
            copy.wait_recv()

    def drain(self):
        for copy in (self.to_after, self.to_before, self.pass_after, self.pass_before, *self.handed):
            copy.wait_send()


class PlaneGather:
    def __init__(self, shard_ref, full_ref, columns, stride, send, receive, expert, shard):
        self.rows = shard_ref.shape[0]
        self.shard_ref, self.full_ref, self.columns = shard_ref, full_ref, columns
        self.send, self.receive = send, receive
        self.expert, self.shard, self.stride = expert, shard, stride
        self.place = lax.rem(expert // stride, SIDE)
        self.sibling = expert + 1 - 2 * lax.rem(expert, 2)
        self.sent = []

    def at(self, shard, start, count):
        return self.full_ref.at[pl.ds(pl.multiple_of(shard * self.rows + start, 16), count), self.columns]

    def go(self, number, source, target, expert, shard):
        copy = remote(source, target, self.send.at[number], self.receive.at[number], expert, shard)
        copy.start()
        self.sent.append(copy)
        return copy

    def first(self):
        quarter = self.rows // SIDE
        start = pl.multiple_of(self.place * quarter, 16)
        source = self.shard_ref.at[pl.ds(start, quarter), self.columns]
        self.pieces = [
            self.go(
                by - 1, source, self.at(self.shard, start, quarter), self.expert, lax.rem(self.shard + by, SIDE)
            )
            for by in (2, 1, 3)
        ]

    def second(self):
        quarter = self.rows // SIDE
        self.shares = []
        for copy, by in zip(self.pieces, (2, 1, 3)):
            copy.wait_recv()
            piece = self.at(lax.rem(self.shard + SIDE - by, SIDE), self.place * quarter, quarter)
            for step in (2, 1, 3):
                peer = self.expert + (lax.rem(self.place + step, SIDE) - self.place) * self.stride
                self.shares.append(self.go(3 * by + step - 1, piece, piece, peer, self.shard))

    def third(self):
        for copy in self.shares:
            copy.wait_recv()
        self.handed = []
        for by in (1, 2, 3):
            block = self.at(lax.rem(self.shard + by, SIDE), 0, self.rows)
            self.handed.append(self.go(11 + by, block, block, self.sibling, self.shard))

    def finish(self):
        for copy in self.handed:
            copy.wait_recv()

    def drain(self):
        for copy in self.sent:
            copy.wait_send()


class Gather:
    def __init__(self, shard_ref, full_ref, send, receive, expert, shard):
        third = shard_ref.shape[1] // 6
        start = lax.rem(expert, 2) * 3 * third
        parts = [pl.ds(pl.multiple_of(start + number * third, LANES), third) for number in range(3)]
        self.parts = [
            PlaneGather(shard_ref, full_ref, parts[1], 2, send.at[1], receive.at[1], expert, shard),
            PlaneGather(shard_ref, full_ref, parts[2], 8, send.at[2], receive.at[2], expert, shard),
            RowGather(shard_ref, full_ref, parts[0], send.at[0], receive.at[0], expert, shard),
        ]

    def first(self):
        for part in self.parts:
            part.first()

    def second(self):
        for part in self.parts:
            part.second()

    def third(self):
        for part in self.parts:
            part.third()

    def finish(self):
        for part in self.parts:
            part.finish()

    def drain(self):
        for part in self.parts:
            part.drain()


def exchange_peers(expert):
    return [
        lax.rem(expert // 8 + dz, SIDE) * 8 + lax.rem(lax.rem(expert // 2, SIDE) + dx, SIDE) * 2
        + lax.rem(expert + dc, 2)
        for dz, dx, dc in exchange_order()
    ]


def exchange_order():
    reach = [0, 1, 2, 1]
    steps = [(dz, dx, dc) for dz in range(SIDE) for dx in range(SIDE) for dc in range(2)]
    return sorted(steps[1:], key=lambda step: -reach[step[0]] - reach[step[1]])


def exchange_start(source_ref, target_ref, send, receive, local, expert, shard, capacity):
    own = pl.ds(pl.multiple_of(expert * capacity, 16), capacity)
    copies = []
    for number, peer in enumerate(exchange_peers(expert)):
        block = pl.ds(pl.multiple_of(peer * capacity, 16), capacity)
        copy = remote(
            source_ref.at[block, :], target_ref.at[own, :], send.at[number], receive.at[number], peer, shard
        )
        copy.start()
        copies.append(copy)
    keep = pltpu.make_async_copy(source_ref.at[own, :], target_ref.at[own, :], local)
    keep.start()
    return copies, keep


def exchange_wait(copies, keep):
    keep.wait()
    for copy in copies:
        copy.wait()


def main_kernel(
    experts, capacity, x_in, g_in, routes_ref, wq_shard, wp_shard, router_ref, gain1_ref, bias1_ref, gain2_ref, bias2_ref,
    w1_in, w2_in,
    mixed_ref, dx_ref, gwq_ref, gwp_ref, small_out, gw1_out, gw2_out, y_out, dz_out,
    routes_out, ws_ref, ln_ref, qkv_ref, lse_ref, o_ref, x2_ref, gates_ref, pick0_ref, pick1_ref,
    x_ref, g_ref, own_ref, small_ref, wq_ref, wp_ref, send_z, send_dy, z_ref, g_rows_ref, dy_ref,
    w1_ref, w2_ref, a_ref, slope_ref, gw1_ref, gw2_ref, side1_ref, side2_ref, rows_ref,
    do_ref, dqkv_ref, h1_ref, summed, side, first_in, second, second_in, third_in, piece, line, plane, gathered,
    s_ref, s_pair, s_sum, s_in, s_out, s_other,
    sends, receives, mini_send, mini_receive, ex_send, ex_receive, half_send, half_receive, local,
    send, receive, s_send, s_receive, g_send, g_receive,
):
    rows, width = x_ref.shape
    load_x = pltpu.make_async_copy(x_in, x_ref, local.at[3])
    load_x.start()
    load_g = pltpu.make_async_copy(g_in, g_ref, local.at[4])
    load_g.start()
    expert, shard = lax.axis_index("expert"), lax.axis_index("wshard")
    core = lax.rem(expert, 2)
    pad = jnp.zeros((own_ref.shape[0] - experts - 4, width // SIDE), F32)
    mini = [router_ref[...].astype(F32)] + [
        ref[...].astype(F32).reshape(1, width // SIDE) for ref in (gain1_ref, bias1_ref, gain2_ref, bias2_ref)
    ]
    own_ref[:, : width // SIDE] = jnp.concatenate(mini + [pad], 0).astype(BF16)
    own_ref[:, width // SIDE :] = jnp.zeros((own_ref.shape[0], own_ref.shape[1] - width // SIDE), BF16)
    greet(
        [(expert, lax.rem(shard + by, SIDE)) for by in (1, 2, 3)]
        + [(peer, shard) for peer in exchange_peers(expert)]
    )
    small = []
    for by in (1, 2, 3):
        copy = remote(
            own_ref, small_ref.at[by - 1], mini_send.at[by - 1], mini_receive.at[by - 1], expert, lax.rem(shard + by, SIDE)
        )
        copy.start()
        small.append(copy)
    first_w, second_w = [
        Gather(shard_ref, full_ref, sends.at[number], receives.at[number], expert, shard)
        for number, (shard_ref, full_ref) in enumerate(((wq_shard, wq_ref), (wp_shard, wp_ref)))
    ]
    first_w.first()
    load_w1 = pltpu.make_async_copy(w1_in, w1_ref, local.at[5])
    load_w1.start()
    load_w2 = pltpu.make_async_copy(w2_in, w2_ref, local.at[6])
    load_w2.start()
    load_x.wait()
    x = x_ref[...].astype(F32)
    normed, _ = normalize(x)
    lane = lane_iota(rows)
    diagonal = lax.broadcasted_iota(jnp.int32, (rows, rows), 0) == lane_iota(rows, rows)
    routes = mm(diagonal.astype(F32).astype(BF16), routes_ref[...].astype(F32).astype(BF16), 1, 1)
    lane_number = lane.astype(F32)
    match = [lane_number == routes[:, k : k + 1] for k in range(2)]
    routes_out[...] = jnp.where(lane == 0, routes[:, 0:1], routes[:, 1:2])
    hits = (match[0] | match[1]).astype(F32).astype(BF16)
    earlier = lax.broadcasted_iota(jnp.int32, (rows, rows), 0) > lane_iota(rows, rows)
    before = mm(earlier.astype(F32).astype(BF16), hits)
    slots = lane_iota(rows, experts * capacity).astype(F32)
    for k, pick_ref in enumerate((pick0_ref, pick1_ref)):
        slot = jnp.sum(jnp.where(match[k], before, 0.0), -1, keepdims=True)
        place = routes[:, k : k + 1] * capacity + slot
        pick_ref[...] = (slots == place).astype(F32).astype(BF16)
    load_g.wait()
    send_dy[...] = mm(pick0_ref[...] + pick1_ref[...], g_ref[...], 0, 0).astype(BF16)
    moves = []

    def move(source, target):
        number = len(moves)
        moves.append(
            exchange_start(
                source, target, ex_send.at[number], ex_receive.at[number], local.at[7 + number], expert, shard, capacity
            )
        )
        return moves[-1]

    first_w.second()
    second_w.first()
    for copy in small:
        copy.wait_recv()
    pieces = []
    for place in range(SIDE):
        strip = own_ref[...].astype(F32)
        for by in (1, 2, 3):
            strip = jnp.where(lax.rem(shard + SIDE - by, SIDE) == place, small_ref[by - 1].astype(F32), strip)
        pieces.append(strip[:, : width // SIDE])
    both = jnp.concatenate(pieces, 1)
    vectors = both[experts : experts + 8, :]
    ln_ref[...] = vectors
    ws_ref[...] = jnp.concatenate([both[:experts], jnp.zeros((LANES - experts, width), F32)], 0).astype(BF16)
    h1 = (normed * vectors[0:1, :] + vectors[1:2, :]).astype(BF16)
    first_w.third()
    second_w.second()
    first_w.finish()
    dy_move = move(send_dy, g_rows_ref)
    qkv_ref[...] = mm(h1, wq_ref[...]).astype(BF16)
    scale = HEAD_DIM ** (-0.5)
    lse_ref[...] = jnp.zeros((rows, LANES), F32)

    def attend(pair, _):
        at = [pl.ds(pl.multiple_of(third * width + pair * LANES, LANES), LANES) for third in range(3)]
        q, k, v = qkv_ref[:, at[0]], qkv_ref[:, at[1]], qkv_ref[:, at[2]]
        parts = []
        for half in range(2):
            own = (lane // HEAD_DIM) == half
            s = mm(jnp.where(own, q, jnp.zeros_like(q)), k, 1, 1) * scale
            top = jnp.max(s, -1, keepdims=True)
            e = jnp.exp(s - top)
            total = jnp.sum(e, -1, keepdims=True)
            lse_ref[...] = jnp.where(lane == 2 * pair + half, top + jnp.log(total), lse_ref[...])
            parts.append(mm((e / total).astype(BF16), v))
        o_ref[:, at[0]] = jnp.where(lane < HEAD_DIM, parts[0], parts[1]).astype(BF16)
        return 0

    lax.fori_loop(0, 2, attend, 0)
    second_w.third()
    lax.fori_loop(2, width // LANES, attend, 0)
    second_w.finish()
    x2 = x + mm(o_ref[...], wp_ref[...])
    x2_ref[...] = x2
    normed2, _ = normalize(x2)
    h2 = (normed2 * vectors[2:3, :] + vectors[3:4, :]).astype(BF16)
    logits = jnp.where(lane < experts, mm(h2, ws_ref[...], 1, 1), -jnp.inf)
    e = jnp.exp(logits - jnp.max(logits, -1, keepdims=True))
    gates = e / jnp.sum(e, -1, keepdims=True)
    gates_ref[...] = gates
    shares = []
    for k in range(2):
        chosen = jnp.sum(jnp.where(match[k], gates, 0.0), -1, keepdims=True)
        high = chosen.astype(BF16)
        rest = chosen - high.astype(F32)
        middle = rest.astype(BF16)
        rest = rest - middle.astype(F32)
        share = jnp.where(lane == 0, high.astype(F32), jnp.where(lane == 1, middle.astype(F32), rest))
        shares.append(jnp.where(lane < 3, share, 0.0).astype(BF16))
    both_picks = pick0_ref[...] + pick1_ref[...]
    send_z[:, :width] = mm(both_picks, h2, 0, 0).astype(BF16)
    send_z[:, width:] = (mm(pick0_ref[...], shares[0], 0, 0) + mm(pick1_ref[...], shares[1], 0, 0)).astype(BF16)
    z_move = move(send_z, z_ref)
    for copy in small:
        copy.wait_send()
    for gather in (first_w, second_w):
        gather.drain()
    load_w1.wait()
    load_w2.wait()
    block = width
    blocks = w1_ref.shape[1] // block
    exchange_wait(*z_move)

    def columns(number):
        return pl.ds(pl.multiple_of(number * block, block), block)

    rows_ref[...] = jnp.zeros_like(rows_ref)

    z = z_ref.at[:, pl.ds(0, width)]
    exchange_wait(*dy_move)
    share = z_ref[:, width:].astype(F32)
    dy_ref[...] = (g_rows_ref[...].astype(F32) * (share[:, 0:1] + share[:, 1:2] + share[:, 2:3])).astype(BF16)
    after, before, across = [lax.rem(shard + by, SIDE) for by in (1, 3, 2)]
    halves = []

    def pass_halves(place, source, target, at=slice(None)):
        rows_each = source.shape[0] // SIDE
        for number, peer in enumerate((after, before)):
            start = pl.multiple_of(across * rows_each + number * (rows_each // 2), 16)
            copy = remote(
                source.at[pl.ds(start, rows_each // 2), at], target.at[number, :, at],
                half_send.at[place, number], half_receive.at[place, number], expert, peer,
            )
            copy.start()
            halves.append(copy)

    def activate(number):
        at = columns(number)
        u = mm(z[...], w1_ref[:, at])
        phi = 0.5 * (1.0 + lax.erf(u * (2.0**-0.5)))
        density = jnp.exp(-0.5 * u * u) * 0.3989422804014327
        slope_ref[:, at] = (phi + u * density).astype(BF16)
        a = (u * phi).astype(BF16)
        a_ref[:, at] = a
        rows_ref[...] += mm(a, w2_ref[at, :])
        gw2_ref[at, :] = mm(a, dy_ref[...], 0, 0).astype(BF16)

    def activate_one(step, _):
        activate(lax.rem(across + step, SIDE))
        return 0

    lax.fori_loop(0, 1, activate_one, 0)
    pass_halves(0, gw2_ref, side2_ref)
    lax.fori_loop(1, blocks, activate_one, 0)
    send_dy[...] = rows_ref[...].astype(BF16)
    move(send_dy, y_out)

    rows_ref[...] = jnp.zeros_like(rows_ref)

    def in_grads(number, _):
        at = columns(number)
        da = mm(dy_ref[...], w2_ref[at, :], 1, 1)
        du = (da * slope_ref[:, at].astype(F32)).astype(BF16)
        rows_ref[...] += mm(du, w1_ref[:, at], 1, 1)
        gw1_ref[:, at] = mm(z[...], du, 0, 0).astype(BF16)
        return 0

    lax.fori_loop(0, blocks, in_grads, 0)
    pass_halves(1, gw1_ref, side1_ref)

    dz_ref = send_z.at[:, pl.ds(0, width)]
    dz_ref[...] = rows_ref[...].astype(BF16)
    move(dz_ref, dz_out)

    x_at, z_at = lax.rem(expert // 2, SIDE), expert // 8
    sibling = expert + 1 - 2 * core
    first, second_at = x_at * (1 - core) + z_at * core, z_at * (1 - core) + x_at * core
    first_step, second_step = 2 + 6 * core, 8 - 6 * core

    def turn(place, by):
        return lax.rem(place + by, SIDE)

    def on_first(by):
        return expert + (turn(first, by) - first) * first_step

    def on_second(by):
        return expert + (turn(second_at, by) - second_at) * second_step

    rows1, rows2 = width // SIDE, w1_ref.shape[1] // SIDE
    started = []
    counts = {}

    def go(source, target, to_expert, to_shard, sends=send, receives=receive, kind="wide"):
        number = counts.get(kind, 0)
        counts[kind] = number + 1
        copy = remote(source, target, sends.at[number], receives.at[number], to_expert, to_shard)
        copy.start()
        started.append(copy)
        return copy

    def go_small(*args):
        return go(*args, sends=s_send, receives=s_receive, kind="small")

    def add(left, right):
        return (left.astype(F32) + right.astype(F32)).astype(BF16)

    def shard_rows(by, each, start, count):
        return pl.ds(pl.multiple_of(turn(shard, by) * each + start, 16), count)

    def join(ref, came_half, each):
        for number, by in enumerate((1, 3)):
            at = shard_rows(by, each, number * (each // 2), each // 2)
            ref[at, :] = add(ref[at, :], came_half[number])

    def pass_on(ref, came, each, start, count):
        copies = []
        for number, by in enumerate((1, 3)):
            landing = pl.ds(number * each + start, count)
            copies.append(
                go(
                    ref.at[shard_rows(by, each, start, count), :], came.at[landing, :], expert, turn(shard, by),
                    g_send, g_receive, "expert",
                )
            )
        return copies

    def final_sum(ref, came, each, target, number):
        own = shard_rows(0, each, 0, each)
        ref[own, :] = (
            ref[own, :].astype(F32) + came[:each, :].astype(F32) + came[each : 2 * each, :].astype(F32)
        ).astype(BF16)
        copy = pltpu.make_async_copy(ref.at[own, :], target, local.at[number])
        copy.start()
        return copy

    def their(chunk):
        return w1_ref.at[:, pl.ds(chunk * block, block)]

    def our(chunk):
        return w1_ref.at[:, pl.ds(pl.multiple_of((SIDE + chunk) * block, LANES), block)]

    def paired(chunk):
        start = 2 * width + chunk // 2 * width
        return w2_ref.at[pl.ds(pl.multiple_of(start, 16), width), pl.ds(pl.multiple_of(chunk % 2 * block, LANES), block)]

    block = width // 2
    for copy in halves[2:]:
        copy.wait_recv()
    join(gw1_ref, side1_ref, rows1)
    grads_first = pass_on(gw1_ref, a_ref, rows1, 0, rows1)
    exchange_wait(*moves[2])
    load_y = pltpu.make_async_copy(y_out, g_rows_ref, local.at[1])
    load_y.start()
    for copy in halves[:2]:
        copy.wait_recv()
    join(gw2_ref, side2_ref, rows2)
    early = rows2 // 4
    grads_second = pass_on(gw2_ref, w2_ref, rows2, 0, early)
    load_y.wait()
    rows, width = x_ref.shape
    lane = lane_iota(rows)
    g = g_ref[...].astype(F32)
    x2 = x2_ref[...]
    gates = gates_ref[...]
    routes = routes_out[...]
    out = x2
    dgates = jnp.zeros((rows, LANES), F32)
    for k, pick_ref in enumerate((pick0_ref, pick1_ref)):
        match = lane.astype(F32) == routes[:, k : k + 1]
        picked = mm(pick_ref[...], g_rows_ref[...])
        chosen = jnp.sum(jnp.where(match, gates, 0.0), -1, keepdims=True)
        out = out + chosen * picked
        dgates = jnp.where(match, jnp.sum(g * picked, -1, keepdims=True), dgates)
    mixed_ref[...] = out.astype(BF16)
    dl = (gates * (dgates - jnp.sum(gates * dgates, -1, keepdims=True))).astype(BF16)
    exchange_wait(*moves[3])
    load_dz = pltpu.make_async_copy(dz_out, dy_ref, local.at[2])
    load_dz.start()
    load_dz.wait()
    dh2 = mm(pick0_ref[...] + pick1_ref[...], dy_ref[...]) + mm(dl, ws_ref[...])
    gain1, bias1 = ln_ref[0:1, :], ln_ref[1:2, :]
    gain2, bias2 = ln_ref[2:3, :], ln_ref[3:4, :]
    n2, r2 = normalize(x2)
    h2 = (n2 * gain2 + bias2).astype(BF16)
    g_router = mm(dl, h2, 0, 0)
    g_gain2 = jnp.sum(dh2 * n2, 0, keepdims=True)
    g_bias2 = jnp.sum(dh2, 0, keepdims=True)
    dx2 = g + norm_back(dh2, n2, r2, gain2)
    dx_ref[...] = dx2
    dx2b = dx2.astype(BF16)
    do_ref[...] = dx2b
    block = width // 2
    mine = pl.ds(pl.multiple_of(core * block, LANES), block)
    others = pl.ds(pl.multiple_of((1 - core) * block, LANES), block)
    their(3)[...] = mm(o_ref[...], do_ref[:, others], 0, 0).astype(BF16)
    pair = [None] * SIDE
    pair[3] = go(their(3), paired(3), sibling, shard)
    our(3)[...] = mm(o_ref[...], do_ref[:, mine], 0, 0).astype(BF16)
    do_ref[...] = mm(dx2b, wp_ref[...], 1, 1).astype(BF16)
    n1, r1 = normalize(x_ref[...].astype(F32))
    h1_ref[...] = (n1 * gain1 + bias1).astype(BF16)
    scale = HEAD_DIM ** (-0.5)
    low = lane < HEAD_DIM

    def heads(start):
        def one(step, _):
            at = [
                pl.ds(pl.multiple_of(third * width + start + step * LANES, LANES), LANES) for third in range(3)
            ]
            q, k, v = qkv_ref[:, at[0]], qkv_ref[:, at[1]], qkv_ref[:, at[2]]
            do = do_ref[:, at[0]]
            parts = []
            for half in range(2):
                own = (lane // HEAD_DIM) == half
                head = start // HEAD_DIM + 2 * step + half
                lse = jnp.sum(jnp.where(lane == head, lse_ref[...], 0.0), -1, keepdims=True)
                s = mm(jnp.where(own, q, jnp.zeros_like(q)), k, 1, 1) * scale
                p = jnp.exp(s - lse)
                dp = mm(jnp.where(own, do, jnp.zeros_like(do)), v, 1, 1)
                ds = (p * (dp - jnp.sum(dp * p, -1, keepdims=True))).astype(BF16)
                parts.append((mm(ds, k) * scale, mm(ds, q, 0, 0) * scale, mm(p.astype(BF16), do, 0, 0)))
            for third, (left, right) in enumerate(zip(*parts)):
                dqkv_ref[:, at[third]] = jnp.where(low, left, right).astype(BF16)
            return 0

        lax.fori_loop(0, block // LANES, one, 0)

    def weight_grads(target, start):
        for third in range(3):
            columns = pl.ds(pl.multiple_of(third * width + start, LANES), block)
            target(third)[...] = mm(h1_ref[...], dqkv_ref[:, columns], 0, 0).astype(BF16)

    heads((1 - core) * block)
    weight_grads(their, (1 - core) * block)
    for third in range(3):
        pair[third] = go(their(third), paired(third), sibling, shard)
    heads(core * block)
    weight_grads(our, core * block)
    for copy in pair:
        copy.wait_recv()

    order = (2, 1, 3, 0)

    def add_pair(number):
        chunk = turn(first, order[number])
        summed[number] = add(our(chunk)[...], paired(chunk)[...])

    wide = s_ref.shape[1]
    part, quarter, half = wide // 2, wide // 4, 2 * wide
    add_pair(0)
    relay_up = go(summed.at[0, pl.ds(0, half)], side.at[0], on_first(1), shard)
    relay_down = go(summed.at[0, pl.ds(half, half)], side.at[1], on_first(3), shard)
    add_pair(1)
    add_pair(2)

    dh1 = mm(dqkv_ref[...], wq_ref[...], 1, 1)
    g_gain1 = jnp.sum(dh1 * n1, 0, keepdims=True)
    g_bias1 = jnp.sum(dh1, 0, keepdims=True)
    row = lax.broadcasted_iota(jnp.int32, (LANES, width), 0)
    vectors = g_router
    for place, vector in enumerate((g_gain1, g_bias1, g_gain2, g_bias2)):
        vectors = jnp.where(row == 32 + place, vector, vectors)
    s_ref[...] = vectors.T.astype(BF16).reshape(s_ref.shape)
    small_pair = go_small(s_ref, s_pair, sibling, shard)

    relay_up.wait_recv()
    summed[1, :half] = add(summed[1, :half], side[0])
    up = go(summed.at[1], first_in.at[0], on_first(1), shard)
    relay_down.wait_recv()
    summed[2, half:] = add(summed[2, half:], side[1])
    down = go(summed.at[2], first_in.at[1], on_first(3), shard)
    add_pair(3)
    dx_ref[...] += norm_back(dh1, n1, r1, gain1)

    small_pair.wait_recv()
    s_sum[...] = add(s_ref[...], s_pair[...])
    s_mine = pl.ds(pl.multiple_of(core * part, 16), part)
    s_others = pl.ds(pl.multiple_of((1 - core) * part, 16), part)
    small_along = [
        go_small(s_sum.at[turn(shard, by), s_mine, :], s_in.at[by - 1], expert, turn(shard, by)) for by in (1, 2, 3)
    ]
    for copy in small_along:
        copy.wait_recv()

    def four(own, a, b, c):
        return own.astype(F32) + a.astype(F32) + b.astype(F32) + c.astype(F32)

    s_out[0] = four(s_sum[shard, s_mine, :], s_in[0], s_in[1], s_in[2]).astype(BF16)
    small_first = [go_small(s_out.at[0], s_in.at[2 + by], on_first(by), shard) for by in (1, 2, 3)]

    up.wait_recv()
    down.wait_recv()
    for own_shard in range(SIDE):
        for place in range(SIDE):
            at = pl.ds(own_shard * wide + place * quarter, quarter)
            second[place, own_shard] = (
                summed[3, at, :].astype(F32) + first_in[0, at, :].astype(F32) + first_in[1, at, :].astype(F32)
            ).astype(BF16)
    along_second = [
        go(second.at[turn(second_at, by)], second_in.at[by - 1], on_second(by), shard) for by in (2, 1, 3)
    ]
    for copy in small_first:
        copy.wait_recv()
    s_out[1] = four(s_out[0], s_in[3], s_in[4], s_in[5]).astype(BF16)
    small_second = [go_small(s_out.at[1], s_in.at[5 + by], on_second(by), shard) for by in (1, 2, 3)]
    for copy in along_second:
        copy.wait_recv()
    piece[...] = four(second[second_at], second_in[0], second_in[1], second_in[2]).astype(BF16)
    along_shard = [
        go(piece.at[turn(shard, by)], third_in.at[by - 1], expert, turn(shard, by)) for by in (2, 1, 3)
    ]
    grads_second += pass_on(gw2_ref, w2_ref, rows2, early, rows2 - early)
    for copy in small_second:
        copy.wait_recv()
    s_out[2] = four(s_out[1], s_in[6], s_in[7], s_in[8]).astype(BF16)
    small_back = go_small(s_out.at[2], s_other, sibling, shard)
    for copy in along_shard:
        copy.wait_recv()
    line[second_at] = four(piece[shard], third_in[0], third_in[1], third_in[2]).astype(BF16)
    back_second = [
        go(line.at[second_at], line.at[second_at], on_second(by), shard) for by in (2, 1, 3)
    ]
    small_back.wait_recv()
    small_out[s_mine, :] = s_out[2].astype(F32)
    small_out[s_others, :] = s_other[...].astype(F32)
    for copy in back_second:
        copy.wait_recv()
    plane[first] = line[...].reshape(wide, line.shape[-1])
    back_first = [
        go(plane.at[first], plane.at[first], on_first(by), shard) for by in (2, 1, 3)
    ]
    own_back = go(plane.at[first], gathered.at[first], sibling, shard)
    for copy in grads_first:
        copy.wait_recv()
    write_first = final_sum(gw1_ref, a_ref, rows1, gw1_out, 11)
    hands = []
    for copy, by in zip(back_first, (2, 1, 3)):
        copy.wait_recv()
        came = turn(first, SIDE - by)
        hands.append(go(plane.at[came], gathered.at[came], sibling, shard))

    def put(source, start):
        for third in range(3):
            columns = pl.ds(pl.multiple_of(third * width + start, LANES), block)
            gwq_ref[:, columns] = source[third]
        gwp_ref[:, pl.ds(pl.multiple_of(start, LANES), block)] = source[3]

    put(plane, core * block)
    own_back.wait_recv()
    for copy in hands:
        copy.wait_recv()
    put(gathered, (1 - core) * block)
    for copy in grads_second:
        copy.wait_recv()
    write_second = final_sum(gw2_ref, w2_ref, rows2, gw2_out, 12)
    write_first.wait()
    write_second.wait()
    for copy in halves:
        copy.wait_send()
    for copy in started:
        copy.wait_send()


def block_step(tokens, cotangent, routes, wq, wp, router, vectors, w1, w2, experts, capacity):
    rows, width = tokens.shape
    hidden = w1.shape[1]
    each, block = width // SIDE, width // 2
    quarter, part = each // 4, each // 2
    slots = experts * capacity
    vmem, anywhere = pl.BlockSpec(memory_space=pltpu.VMEM), pl.BlockSpec(memory_space=pl.ANY)
    return pl.pallas_call(
        functools.partial(main_kernel, experts, capacity),
        out_shape=(
            jax.ShapeDtypeStruct((rows, width), BF16),
            jax.ShapeDtypeStruct((rows, width), F32),
            jax.ShapeDtypeStruct((each, 3 * width), BF16),
            jax.ShapeDtypeStruct((each, width), BF16),
            jax.ShapeDtypeStruct((each, LANES), F32),
            jax.ShapeDtypeStruct((each, hidden), BF16),
            jax.ShapeDtypeStruct((hidden // SIDE, width), BF16),
            jax.ShapeDtypeStruct((slots, width), BF16),
            jax.ShapeDtypeStruct((slots, width), BF16),
        ),
        in_specs=[anywhere] * 2 + [vmem] + [anywhere] * 2 + [vmem] * 5 + [anywhere] * 2,
        out_specs=[vmem] * 5 + [anywhere] * 4,
        scratch_shapes=[
            pltpu.VMEM((rows, LANES), F32),
            pltpu.VMEM((LANES, width), BF16),
            pltpu.VMEM((8, width), F32),
            pltpu.VMEM((rows, 3 * width), BF16),
            pltpu.VMEM((rows, LANES), F32),
            pltpu.VMEM((rows, width), BF16),
            pltpu.VMEM((rows, width), F32),
            pltpu.VMEM((rows, LANES), F32),
            pltpu.VMEM((rows, slots), BF16),
            pltpu.VMEM((rows, slots), BF16),
            pltpu.VMEM((rows, width), BF16),
            pltpu.VMEM((rows, width), BF16),
            pltpu.VMEM((48, 256), BF16),
            pltpu.VMEM((3, 48, 256), BF16),
            pltpu.VMEM((width, 3 * width), BF16),
            pltpu.VMEM((width, width), BF16),
            pltpu.VMEM((slots, width + LANES), BF16),
            pltpu.VMEM((slots, width), BF16),
            pltpu.VMEM((slots, width + LANES), BF16),
            pltpu.VMEM((slots, width), BF16),
            pltpu.VMEM((slots, width), BF16),
            pltpu.VMEM((width, hidden), BF16),
            pltpu.VMEM((hidden, width), BF16),
            pltpu.VMEM((slots, hidden), BF16),
            pltpu.VMEM((slots, hidden), BF16),
            pltpu.VMEM((width, hidden), BF16),
            pltpu.VMEM((hidden, width), BF16),
            pltpu.VMEM((2, width // 8, hidden), BF16),
            pltpu.VMEM((2, hidden // 8, width), BF16),
            pltpu.VMEM((slots, width), F32),
            pltpu.VMEM((rows, width), BF16),
            pltpu.VMEM((rows, 3 * width), BF16),
            pltpu.VMEM((rows, width), BF16),
            pltpu.VMEM((SIDE, width, block), BF16),
            pltpu.VMEM((2, 2 * each, block), BF16),
            pltpu.VMEM((2, width, block), BF16),
            pltpu.VMEM((SIDE, SIDE, quarter, block), BF16),
            pltpu.VMEM((3, SIDE, quarter, block), BF16),
            pltpu.VMEM((3, quarter, block), BF16),
            pltpu.VMEM((SIDE, quarter, block), BF16),
            pltpu.VMEM((SIDE, quarter, block), BF16),
            pltpu.VMEM((SIDE, each, block), BF16),
            pltpu.VMEM((SIDE, each, block), BF16),
            pltpu.VMEM((SIDE, each, LANES), BF16),
            pltpu.VMEM((SIDE, each, LANES), BF16),
            pltpu.VMEM((SIDE, each, LANES), BF16),
            pltpu.VMEM((9, part, LANES), BF16),
            pltpu.VMEM((3, part, LANES), BF16),
            pltpu.VMEM((part, LANES), BF16),
            pltpu.SemaphoreType.DMA((2, 3, 15)),
            pltpu.SemaphoreType.DMA((2, 3, 15)),
            pltpu.SemaphoreType.DMA((3,)),
            pltpu.SemaphoreType.DMA((3,)),
            pltpu.SemaphoreType.DMA((4, 31)),
            pltpu.SemaphoreType.DMA((4, 31)),
            pltpu.SemaphoreType.DMA((2, 2)),
            pltpu.SemaphoreType.DMA((2, 2)),
            pltpu.SemaphoreType.DMA((13,)),
            pltpu.SemaphoreType.DMA((24,)),
            pltpu.SemaphoreType.DMA((24,)),
            pltpu.SemaphoreType.DMA((11,)),
            pltpu.SemaphoreType.DMA((11,)),
            pltpu.SemaphoreType.DMA((6,)),
            pltpu.SemaphoreType.DMA((6,)),
        ],
        compiler_params=pltpu.CompilerParams(
            vmem_limit_bytes=62 * MIB, collective_id=1, has_side_effects=True
        ),
        cost_estimate=pl.CostEstimate(
            flops=12 * slots * width * hidden, bytes_accessed=48 * MIB, transcendentals=2 * slots * hidden
        ),
        name="whole_block",
    )(tokens, cotangent, routes, wq, wp, router, *vectors, w1, w2)


def widen_kernel(experts, *refs):
    ins, outs, buffers, wide, loads, stores = refs[:7], refs[7:18], refs[18:25], refs[25:32], refs[32], refs[33]
    small_in, small_buffer = ins[4], buffers[4]
    incoming = []
    for number, (source, target) in enumerate(zip(ins, buffers)):
        copy = pltpu.make_async_copy(source, target, loads.at[number])
        copy.start()
        incoming.append(copy)
    outgoing = []

    def store(source, target):
        copy = pltpu.make_async_copy(source, target, stores.at[len(outgoing)])
        copy.start()
        outgoing.append(copy)

    places = (0, 1, 4, 5, None, 9, 10)
    for number in (0, 1, 5, 6, 2, 3):
        incoming[number].wait()
        if number < 2:
            store(buffers[number], outs[places[number]])
        else:
            wide[number][...] = buffers[number][...].astype(F32)
            target = outs[places[number]]
            store(wide[number], target.at[0] if number > 4 else target)
    incoming[4].wait()
    rows = small_buffer.shape[0]
    padded = jnp.concatenate([small_buffer[...], jnp.zeros((256 - rows, LANES), F32)], 0).T
    outs[8][...] = padded[:experts, :rows]
    for place, output in enumerate((2, 3, 6, 7)):
        outs[output][...] = padded[experts + place : experts + place + 1, :rows].reshape(rows)
    for copy in outgoing:
        copy.wait()


def widen(mixed, grad_tokens, gwq, gwp, small, gw1, gw2, experts):
    ins = (mixed, grad_tokens, gwq, gwp, small, gw1, gw2)
    rows = small.shape[0]
    anywhere, vmem = pl.BlockSpec(memory_space=pl.ANY), pl.BlockSpec(memory_space=pltpu.VMEM)
    shapes = [
        (mixed.shape, BF16), (grad_tokens.shape, F32), ((rows,), F32), ((rows,), F32), (gwq.shape, F32), (gwp.shape, F32),
        ((rows,), F32), ((rows,), F32), ((experts, rows), F32), ((1, *gw1.shape), F32), ((1, *gw2.shape), F32),
    ]
    return pl.pallas_call(
        functools.partial(widen_kernel, experts),
        out_shape=[jax.ShapeDtypeStruct(*shape) for shape in shapes],
        in_specs=[anywhere] * 7,
        out_specs=[anywhere if place in (0, 1, 4, 5, 9, 10) else vmem for place in range(11)],
        scratch_shapes=[pltpu.VMEM(array.shape, array.dtype) for array in ins]
        + [pltpu.VMEM(array.shape, F32) for array in ins]
        + [pltpu.SemaphoreType.DMA((7,)), pltpu.SemaphoreType.DMA((6,))],
        compiler_params=pltpu.CompilerParams(vmem_limit_bytes=58 * MIB),
        cost_estimate=pl.CostEstimate(flops=0, bytes_accessed=13 * MIB, transcendentals=0),
        name="widen_outputs",
    )(*ins)


def on_device(
    tokens, ln1_gain, ln1_bias, w_qkv, w_proj, ln2_gain, ln2_bias, w_router,
    expert_in, expert_out, routes, cotangent,
):
    rows = tokens.shape[0]
    experts = w_router.shape[1]
    capacity = (5 * rows // 2 + 8 * experts - 1) // (8 * experts) * 8
    *sums, _, _ = block_step(
        tokens, cotangent, routes.T, w_qkv, w_proj, w_router.T, (ln1_gain, ln1_bias, ln2_gain, ln2_bias),
        expert_in[0], expert_out[0], experts, capacity,
    )
    outputs = list(widen(*sums, experts))
    outputs[8] = outputs[8].T
    return tuple(outputs)


def solution(mesh):
    in_specs = (
        P(("expert", "wshard"), None),
        P("wshard"),
        P("wshard"),
        P("wshard", None),
        P("wshard", None),
        P("wshard"),
        P("wshard"),
        P("wshard", None),
        P("expert", None, None),
        P("expert", None, None),
        P(("expert", "wshard"), None),
        P(("expert", "wshard"), None),
    )
    out_specs = (
        P(("expert", "wshard"), None),
        P(("expert", "wshard"), None),
        P("wshard"),
        P("wshard"),
        P("wshard", None),
        P("wshard", None),
        P("wshard"),
        P("wshard"),
        P("wshard", None),
        P("expert", "wshard", None),
        P("expert", "wshard", None),
    )
    return jax.shard_map(
        on_device, mesh=mesh, in_specs=in_specs, out_specs=out_specs, check_vma=False
    )
```
